32 devices in a mesh: dp: 16 (over z, x, core), seq: 2 (over y).
Axes of the slice: x: 2, y: 2, z: 4, core: 2. Of those that a mesh axis runs over, the one named last changes fastest.
Arguments:
- block_in: bfloat16 [16, 256, 1024], P('dp', 'seq'), may hold values from -6 to 6
- conditioning: bfloat16 [16, 768], P('dp'), may hold values from -6 to 6
- crop_ids: int32 [16, 256], P('dp', 'seq'), may hold values from 0 to 15, as said below
- positions: int32 [16, 2, 256], P('dp', None, 'seq'), may hold values from 0 to 15
- qkv_weight: bfloat16 [1024, 3072], P(('dp', 'seq')), may hold values from -0.1875 to 0.1875
- out_weight: bfloat16 [1024, 1024], P(('dp', 'seq')), may hold values from -0.75 to 0.75
- up_weight: bfloat16 [1024, 6144], P(('dp', 'seq')), may hold values from -0.1875 to 0.1875
- down_weight: bfloat16 [3072, 1024], P(('dp', 'seq')), may hold values from -0.109375 to 0.109375
- attn_modulate: bfloat16 [768, 1024], P(('dp', 'seq')), may hold values from -0.0546875 to 0.0546875
- ffn_modulate: bfloat16 [768, 1024], P(('dp', 'seq')), may hold values from -0.0546875 to 0.0546875
- head_scale: float32 [16], replicated, may hold values from 6 to 20
- cotangent: bfloat16 [16, 256, 1024], P('dp', 'seq'), may hold values from -6 to 6
Outputs:
- block_out: bfloat16 [16, 256, 1024], P('dp', 'seq')
- input_grad: float32 [16, 256, 1024], P('dp', 'seq')
- cond_grad: float32 [16, 768], P('dp')
- qkv_grad: float32 [1024, 3072], P(('dp', 'seq'))
- out_grad: float32 [1024, 1024], P(('dp', 'seq'))
- up_grad: float32 [1024, 6144], P(('dp', 'seq'))
- down_grad: float32 [3072, 1024], P(('dp', 'seq'))
- attnmod_grad: float32 [768, 1024], P(('dp', 'seq'))
- ffnmod_grad: float32 [768, 1024], P(('dp', 'seq'))
- scale_grad: float32 [16], replicated
The draws below stay inside these ranges and needn't reach their ends.
Inputs may be any that keep to these rules, and one draw needn't show every extreme that they name: `crop_ids`: in every canvas each crop id from 0 to 15 labels exactly 16 tokens, and the first and the last token of a canvas carry the same crop id.
All inputs are finite; a program needn't handle non-finite values.
Results may differ from the reference program's by a relative error of at most 0.03.
Values may be sent and summed in bfloat16 or wider, within the bound.
A program may use at most 256 MiB of HBM per device.

```python
import math
import jax
import jax.numpy as jnp
from jax import lax

D = 1024
HEADS = 16
FF = 3072
COND = 768
CROP = 16
CANVAS = 256
CANVASES = 16


def draw_crop_ids(key, part):
    key = jax.random.fold_in(key, 11)
    key_span, key_jitter = jax.random.split(key)
    length = CANVAS
    places = jnp.arange(length, dtype=jnp.int32)[None, :]
    power = jax.random.randint(key_span, (CANVASES, 1), 0, 5)
    span = jnp.minimum(CROP * jnp.left_shift(jnp.int32(1), 2 * power), length)
    jitter = jax.random.randint(key_jitter, (CANVASES, length), 0, 1 << 20) % span
    score = (places + jitter) * length + places
    order = jnp.argsort(score, axis=1, stable=True)
    ranks = jnp.argsort(order, axis=1, stable=True).astype(jnp.int32)
    crops = ranks // CROP
    first_crop = crops[:, :1]
    partner = jnp.max(jnp.where((crops == first_crop) & (places > 0), places, -1), axis=1, keepdims=True)
    last_crop = crops[:, -1:]
    crops = jnp.where(places == partner, last_crop, crops)
    crops = jnp.where(places == length - 1, first_crop, crops)
    return crops.astype(jnp.int32)


def with_ends(array, stream_key, least, top_value):
    index_at = [jax.random.randint(jax.random.fold_in(stream_key, axis), (), 0, length) for axis, length in enumerate(array.shape)]
    main_axis = array.shape.index(max(array.shape))
    next_to = index_at[:main_axis] + [(index_at[main_axis] + 1) % array.shape[main_axis]] + index_at[main_axis + 1:]
    return array.at[tuple(index_at)].set(least).at[tuple(next_to)].set(top_value)


def block_levels(key, extent, pieces, low, largest):
    gain, own = 1.0, jax.random.fold_in(key, 6)
    for axis_at, shards_of in pieces:
        draws = jnp.exp(jax.random.uniform(jax.random.fold_in(own, axis_at), (shards_of,), jnp.float32, low / len(pieces), largest / len(pieces)))
        gain = gain * jnp.repeat(draws, extent[axis_at] // shards_of).reshape([-1 if axis == axis_at else 1 for axis in range(len(extent))])
    return gain


def noise(own_key, dims, scale, reach, cuts=(), kind=jnp.bfloat16):
    entries = jax.random.normal(own_key, dims, jnp.float32) * scale
    if len(cuts) > 0:
        entries = block_levels(own_key, dims, cuts, -0.22, 0.18) * entries
    return jnp.clip(entries, min=-reach, max=reach).astype(kind)


def setup_inputs(seed: int = 0) -> dict:
    seeds = jax.random.split(jax.random.key(seed), 13)
    block_in = noise(seeds[0], (CANVASES, CANVAS, D), 1.0, 6.0, ((0, 16), (1, 2)))
    conditioning = noise(seeds[1], (CANVASES, COND), 1.0, 6.0, ((0, 16),))
    crop_ids = draw_crop_ids(jax.random.fold_in(seeds[12], 71), 0)
    positions = with_ends(jax.random.randint(seeds[3], (CANVASES, 2, CANVAS), 0, 16), jax.random.fold_in(seeds[3], 1), 0, 15).astype(jnp.int32)
    qkv_weight = noise(seeds[4], (D, 3 * D), D ** -0.5, 0.1875, ((0, 32),))
    out_weight = noise(seeds[5], (D, D), (D // CROP) ** -0.5, 0.75, ((0, 32),))
    up_weight = noise(seeds[6], (D, 2 * FF), D ** -0.5, 0.1875, ((0, 32),))
    down_weight = noise(seeds[7], (FF, D), FF ** -0.5, 0.109375, ((0, 32),))
    attn_modulate = noise(seeds[8], (COND, D), (16 * COND) ** -0.5, 0.0546875, ((0, 32),))
    ffn_modulate = noise(seeds[9], (COND, D), (16 * COND) ** -0.5, 0.0546875, ((0, 32),))
    head_scale = jnp.clip(jnp.exp(jax.random.uniform(seeds[10], (HEADS,), jnp.float32, math.log(6.0), math.log(20.0))), 6.0, 20.0)
    cotangent = noise(seeds[11], (CANVASES, CANVAS, D), 1.0, 6.0, ((0, 16), (1, 2)))
    return dict(block_in=block_in, conditioning=conditioning, crop_ids=crop_ids, positions=positions, qkv_weight=qkv_weight, out_weight=out_weight, up_weight=up_weight, down_weight=down_weight, attn_modulate=attn_modulate, ffn_modulate=ffn_modulate, head_scale=head_scale, cotangent=cotangent)


eps_norm = 1e-06
eps_cosine = 1e-06
negative = -1e+30
highest = lax.Precision.HIGHEST

@jax.custom_vjp
def low(v):
    return lax.optimization_barrier(v.astype(jnp.bfloat16)).astype(jnp.float32)

@jax.custom_vjp
def low_back(v):
    return v

def low_keep(v):
    return (low(v), None)

def low_pass(kept, grad):
    return (grad,)

def back_keep(v):
    return (v, None)

def back_low(kept, grad):
    return (low(grad),)
low.defvjp(low_keep, low_pass)
low_back.defvjp(back_keep, back_low)

def rope_tables(positions, heads):
    unit_pos = (2.0 * positions.astype(jnp.float32) + 1.0) / 16.0 - 1.0
    exponent = (jnp.arange(8, dtype=jnp.float32)[None, :] * heads + jnp.arange(heads, dtype=jnp.float32)[:, None]) / (8.0 * heads)
    frequency = math.pi * 10.0 ** exponent
    angles = jnp.moveaxis(unit_pos[..., None, None] * frequency, -4, -2)
    return (jnp.cos(angles), jnp.sin(angles))

def rotate(vector, cosine, sine):
    leading = vector.shape[:-1]
    turned_part = vector[..., :32].reshape(leading + (2, 2, 8))
    first_half = turned_part[..., 0, :]
    second_half = turned_part[..., 1, :]
    turned = jnp.stack([first_half * cosine - second_half * sine, first_half * sine + second_half * cosine], axis=-2)
    return jnp.concatenate([turned.reshape(leading + (32,)), vector[..., 32:]], axis=-1)

def ada_norm(value, scale):
    inverse = lax.rsqrt(lax.optimization_barrier(jnp.mean(value * value, axis=-1, keepdims=True)) + eps_norm)
    return value * inverse * scale

def cosine_scale(value, root_scale):
    return value * root_scale[:, None] * lax.rsqrt(lax.optimization_barrier(jnp.sum(value * value, axis=-1, keepdims=True)) + eps_cosine)

def canvas_forward(tokens, condition, crops, places, weight_qkv, weight_out, weight_up, weight_down, modulate_attn, modulate_ffn, scales):
    length, width = tokens.shape
    heads = scales.shape[0]
    head_size = width // heads
    hidden_width = weight_down.shape[0]
    scale_attn = 1.0 + low_back(jnp.dot(condition, modulate_attn, precision=highest))
    scale_ffn = 1.0 + low_back(jnp.dot(condition, modulate_ffn, precision=highest))
    normed_attn = low(ada_norm(tokens, scale_attn))
    qkv_all = low_back(jnp.dot(normed_attn, weight_qkv, precision=highest)).reshape(length, 3, heads, head_size)
    root_scale = jnp.sqrt(scales)
    cosine, sine = rope_tables(places, heads)
    queries = low(rotate(cosine_scale(qkv_all[:, 0], root_scale), cosine, sine))
    keys_rot = low(rotate(cosine_scale(qkv_all[:, 1], root_scale), cosine, sine))
    values = low(qkv_all[:, 2])
    block_rows = math.gcd(length, 512)

    def attend_block(inputs):
        query_block, crop_block = inputs
        scores = low_back(jnp.einsum('qhd,khd->hqk', query_block, keys_rot, precision=highest))
        allowed = (crop_block[:, None] == crops[None, :])[None]
        shifted = jnp.where(allowed, scores, negative)
        row_max = lax.optimization_barrier(jnp.max(shifted, axis=-1, keepdims=True))
        weights = jnp.where(allowed, jnp.exp(shifted - row_max), 0.0)
        probs = weights / lax.optimization_barrier(jnp.sum(weights, axis=-1, keepdims=True))
        return low(low_back(jnp.einsum('hqk,khd->qhd', low(probs), values, precision=highest)))
    attended = lax.map(jax.checkpoint(attend_block), (queries.reshape(length // block_rows, block_rows, heads, head_size), crops.reshape(length // block_rows, block_rows))).reshape(length, width)
    attn_out = low_back(jnp.dot(attended, weight_out, precision=highest))
    middle = tokens + attn_out
    normed_ffn = low(ada_norm(middle, scale_ffn))
    up_all = low_back(jnp.dot(normed_ffn, weight_up, precision=highest))
    hidden = low(up_all[:, :hidden_width] * jax.nn.gelu(up_all[:, hidden_width:], approximate=False))
    ffn_out = low_back(jnp.dot(hidden, weight_down, precision=highest))
    return middle + ffn_out

def reference(block_in, conditioning, crop_ids, positions, qkv_weight, out_weight, up_weight, down_weight, attn_modulate, ffn_modulate, head_scale, cotangent):

    def forward(tokens, condition, weight_qkv, weight_out, weight_up, weight_down, modulate_attn, modulate_ffn, scales):

        def one_canvas(inputs):
            canvas_tokens, canvas_cond, canvas_crops, canvas_places = inputs
            return canvas_forward(canvas_tokens, canvas_cond, canvas_crops, canvas_places, weight_qkv, weight_out, weight_up, weight_down, modulate_attn, modulate_ffn, scales)
        return lax.map(jax.checkpoint(one_canvas), (tokens, condition, crop_ids, positions))
    floats = tuple((array_in.astype(jnp.float32) for array_in in (block_in, conditioning, qkv_weight, out_weight, up_weight, down_weight, attn_modulate, ffn_modulate, head_scale)))
    outputs, pull_back = jax.vjp(forward, *floats)
    grads = pull_back(cotangent.astype(jnp.float32))
    return (outputs.astype(jnp.bfloat16), grads[0], grads[1], grads[2], grads[3], grads[4], grads[5], grads[6], grads[7], grads[8])
```

```python
import functools
import math
import types

import jax
import jax.numpy as jnp
import ml_dtypes
import numpy as np
from jax import lax
from jax.experimental import pallas as pl
from jax.experimental.pallas import tpu as pltpu
from jax.sharding import PartitionSpec as P

eps_norm = 1e-06
eps_cosine = 1e-06
negative = -1e30
key_rows = 256


def block_split(count, limit):
    size_rows = math.gcd(count, limit)
    return (size_rows, count // size_rows)


def rope_tables(positions, heads):
    unit_pos = (2.0 * positions.astype(jnp.float32) + 1.0) / 16.0 - 1.0
    exponent = (
        jnp.arange(8, dtype=jnp.float32)[None, :] * heads
        + jnp.arange(heads, dtype=jnp.float32)[:, None]
    ) / (8.0 * heads)
    frequency = math.pi * 10.0**exponent
    angles = jnp.moveaxis(unit_pos[..., None, None] * frequency, -4, -2)
    return (jnp.cos(angles), jnp.sin(angles))


def rotate(vector, cosine, sine):
    leading = vector.shape[:-1]
    turned_part = vector[..., :32].reshape(leading + (2, 2, 8))
    first_half = turned_part[..., 0, :]
    second_half = turned_part[..., 1, :]
    turned = jnp.stack(
        [first_half * cosine - second_half * sine, first_half * sine + second_half * cosine],
        axis=-2,
    )
    return jnp.concatenate([turned.reshape(leading + (32,)), vector[..., 32:]], axis=-1)


def norm_forward(value, scale):
    inverse = lax.rsqrt(jnp.mean(value * value, axis=-1, keepdims=True) + eps_norm)
    return (value * inverse * scale[:, None], inverse)


def norm_backward(value, inverse, scale, grad_norm):
    scaled = grad_norm * scale[:, None]
    grad_value = inverse * scaled - value * inverse**3 * jnp.mean(
        scaled * value, axis=-1, keepdims=True
    )
    grad_scale = jnp.sum(grad_norm * value * inverse, axis=1)
    return (grad_value, grad_scale)


def cosine_forward(value, root_scale):
    factor = root_scale[:, None] * lax.rsqrt(
        jnp.sum(value * value, axis=-1, keepdims=True) + eps_cosine
    )
    return (value * factor, factor)


def cosine_backward(value, factor, grad):
    squares = jnp.sum(value * value, axis=-1, keepdims=True) + eps_cosine
    along = jnp.sum(grad * value, axis=-1, keepdims=True)
    grad_value = factor * grad - value * factor * along / squares
    return (grad_value, jnp.sum(along * factor, axis=(0, 1, 3)))


def geglu(value_part, gate_part):
    return value_part * jax.nn.gelu(gate_part, approximate=False)


def pair_grads(queries, grad_att, log_total, deltas, query_crop, key_block, value_block, key_crop):
    scores = jnp.einsum("cqhd,ckhd->cqhk", queries, key_block, preferred_element_type=jnp.float32)
    allowed = (query_crop[:, :, None] == key_crop[:, None, :])[:, :, None, :]
    probs = jnp.exp(jnp.where(allowed, scores - log_total[..., None], negative))
    probs = jnp.where(allowed, probs, 0.0)
    dotted = jnp.einsum(
        "cqhd,ckhd->cqhk", grad_att, value_block, preferred_element_type=jnp.float32
    )
    slope = (probs * (dotted - deltas[..., None])).astype(jnp.bfloat16)
    grad_q = jnp.einsum("cqhk,ckhd->cqhd", slope, key_block, preferred_element_type=jnp.float32)
    grad_k = jnp.einsum("cqhk,cqhd->ckhd", slope, queries, preferred_element_type=jnp.float32)
    grad_v = jnp.einsum(
        "cqhk,cqhd->ckhd", probs.astype(jnp.bfloat16), grad_att, preferred_element_type=jnp.float32
    )
    return (grad_q, grad_k, grad_v)


def pack_terms(terms, lead_shape):
    return jnp.concatenate([term.reshape(lead_shape + (-1,)) for term in terms], axis=-1)


def unpack_terms(packed_row, terms, owners):
    results = []
    offset = 0
    for term in terms:
        own_rows = term.shape[0] // owners
        count = own_rows * term.shape[1]
        results.append(packed_row[offset : offset + count].reshape(own_rows, term.shape[1]))
        offset = offset + count
    return results


def shards(
    block_in,
    conditioning,
    crop_ids,
    positions,
    qkv_weight,
    out_weight,
    up_weight,
    down_weight,
    attn_modulate,
    ffn_modulate,
    head_scale,
    cotangent,
):
    qkv_full, out_full, up_full, down_full, attn_mod, ffn_mod = (
        lax.all_gather(qkv_weight, ("dp", "seq"), axis=0, tiled=True),
        lax.all_gather(out_weight, ("dp", "seq"), axis=0, tiled=True),
        lax.all_gather(up_weight, ("dp", "seq"), axis=0, tiled=True),
        lax.all_gather(down_weight, ("dp", "seq"), axis=0, tiled=True),
        lax.all_gather(attn_modulate, ("dp", "seq"), axis=0, tiled=True),
        lax.all_gather(ffn_modulate, ("dp", "seq"), axis=0, tiled=True),
    )
    canvases, rows, width = block_in.shape
    heads = head_scale.shape[0]
    head_size = width // heads
    hidden_width = down_full.shape[0]
    seq_count = lax.axis_size("seq")
    inputs = block_in.astype(jnp.float32)
    scale_attn = 1.0 + jnp.dot(conditioning, attn_mod, preferred_element_type=jnp.float32)
    scale_ffn = 1.0 + jnp.dot(conditioning, ffn_mod, preferred_element_type=jnp.float32)
    normed_attn, inverse_attn = norm_forward(inputs, scale_attn)
    normed_attn = normed_attn.astype(jnp.bfloat16)
    qkv_all = jnp.einsum(
        "csd,de->cse", normed_attn, qkv_full, preferred_element_type=jnp.float32
    ).reshape(canvases, rows, 3, heads, head_size)
    root_scale = jnp.sqrt(head_scale)
    query_cos, query_factor = cosine_forward(qkv_all[:, :, 0], root_scale)
    key_cos, key_factor = cosine_forward(qkv_all[:, :, 1], root_scale)
    cosine, sine = rope_tables(positions, heads)
    queries = rotate(query_cos, cosine, sine).astype(jnp.bfloat16)
    keys_flat = rotate(key_cos, cosine, sine).astype(jnp.bfloat16).reshape(canvases, rows, width)
    values_flat = qkv_all[:, :, 2].astype(jnp.bfloat16).reshape(canvases, rows, width)
    start_state = (
        jnp.full((canvases, rows, heads), negative, jnp.float32),
        jnp.zeros((canvases, rows, heads), jnp.float32),
        jnp.zeros((canvases, rows, heads, head_size), jnp.float32),
    )
    state_now = start_state
    piece_keys = lax.all_gather(keys_flat, "seq", axis=1, tiled=True)
    piece_values = lax.all_gather(values_flat, "seq", axis=1, tiled=True)
    piece_crop = lax.all_gather(crop_ids, "seq", axis=1, tiled=True)
    size_rows, number = block_split(piece_keys.shape[1], key_rows)

    def step_block(state, block_index):
        running_max, row_total, weighted = state
        offset = block_index * size_rows
        key_block = lax.dynamic_slice_in_dim(piece_keys, offset, size_rows, 1).reshape(
            canvases, size_rows, heads, head_size
        )
        value_block = lax.dynamic_slice_in_dim(piece_values, offset, size_rows, 1).reshape(
            canvases, size_rows, heads, head_size
        )
        crop_block = lax.dynamic_slice_in_dim(piece_crop, offset, size_rows, 1)
        scores = jnp.einsum(
            "cqhd,ckhd->cqhk", queries, key_block, preferred_element_type=jnp.float32
        )
        allowed = (crop_ids[:, :, None] == crop_block[:, None, :])[:, :, None, :]
        scores = jnp.where(allowed, scores, negative)
        new_max = jnp.maximum(running_max, jnp.max(scores, axis=-1))
        weights = jnp.where(allowed, jnp.exp(scores - new_max[..., None]), 0.0)
        shrink = jnp.exp(running_max - new_max)
        row_total = row_total * shrink + jnp.sum(weights, axis=-1)
        weighted = weighted * shrink[..., None] + jnp.einsum(
            "cqhk,ckhd->cqhd",
            weights.astype(jnp.bfloat16),
            value_block,
            preferred_element_type=jnp.float32,
        )
        return ((new_max, row_total, weighted), None)

    state_now, unused = lax.scan(step_block, state_now, jnp.arange(number))
    running_max, row_total, weighted = state_now
    log_total = running_max + jnp.log(row_total)
    attended_raw = weighted / row_total[..., None]
    attended = attended_raw.astype(jnp.bfloat16).reshape(canvases, rows, width)
    middle = inputs + jnp.einsum(
        "csd,de->cse", attended, out_full, preferred_element_type=jnp.float32
    )
    normed_ffn, inverse_ffn = norm_forward(middle, scale_ffn)
    normed_ffn = normed_ffn.astype(jnp.bfloat16)
    up_all = jnp.einsum("csd,de->cse", normed_ffn, up_full, preferred_element_type=jnp.float32)
    value_part = up_all[..., :hidden_width]
    gate_part = up_all[..., hidden_width:]
    hidden = geglu(value_part, gate_part).astype(jnp.bfloat16)
    block_out = (
        middle + jnp.einsum("csf,fd->csd", hidden, down_full, preferred_element_type=jnp.float32)
    ).astype(jnp.bfloat16)
    down_term = jnp.einsum("csf,csd->fd", hidden, cotangent, preferred_element_type=jnp.float32)
    grad_hidden = jnp.einsum(
        "csd,fd->csf", cotangent, down_full, preferred_element_type=jnp.float32
    )
    unused_value, geglu_pull = jax.vjp(geglu, value_part, gate_part)
    grad_value, grad_gate = geglu_pull(grad_hidden)
    grad_up = jnp.concatenate([grad_value, grad_gate], axis=-1).astype(jnp.bfloat16)
    up_term = jnp.einsum("csd,cse->de", normed_ffn, grad_up, preferred_element_type=jnp.float32)
    grad_normed_ffn = jnp.einsum(
        "cse,de->csd", grad_up, up_full, preferred_element_type=jnp.float32
    )
    grad_mid_norm, ffn_scale_sum = norm_backward(middle, inverse_ffn, scale_ffn, grad_normed_ffn)
    grad_middle = cotangent.astype(jnp.float32) + grad_mid_norm
    grad_branch = grad_middle.astype(jnp.bfloat16)
    out_term = jnp.einsum("csd,cse->de", attended, grad_branch, preferred_element_type=jnp.float32)
    grad_attended = (
        jnp.einsum("cse,de->csd", grad_branch, out_full, preferred_element_type=jnp.float32)
        .astype(jnp.bfloat16)
        .reshape(canvases, rows, heads, head_size)
    )
    deltas = jnp.sum(grad_attended.astype(jnp.float32) * attended_raw, axis=-1)
    start_back = (
        jnp.zeros((canvases, rows, heads, head_size), jnp.float32),
        jnp.zeros((canvases, rows * seq_count, 2 * width), jnp.float32),
    )
    state_now = start_back
    fold_piece_keys = lax.all_gather(keys_flat, "seq", axis=1, tiled=True)
    fold_piece_values = lax.all_gather(values_flat, "seq", axis=1, tiled=True)
    fold_piece_crop = lax.all_gather(crop_ids, "seq", axis=1, tiled=True)
    fold_size_rows, number = block_split(fold_piece_keys.shape[1], key_rows)

    def step_block(state, block_index):
        grad_q_sum, grad_kv_all = state
        offset = block_index * fold_size_rows
        key_block = lax.dynamic_slice_in_dim(fold_piece_keys, offset, fold_size_rows, 1).reshape(
            canvases, fold_size_rows, heads, head_size
        )
        value_block = lax.dynamic_slice_in_dim(
            fold_piece_values, offset, fold_size_rows, 1
        ).reshape(canvases, fold_size_rows, heads, head_size)
        crop_block = lax.dynamic_slice_in_dim(fold_piece_crop, offset, fold_size_rows, 1)
        grad_q, grad_k, grad_v = pair_grads(
            queries, grad_attended, log_total, deltas, crop_ids, key_block, value_block, crop_block
        )
        update = jnp.concatenate(
            [
                grad_k.reshape(canvases, fold_size_rows, width),
                grad_v.reshape(canvases, fold_size_rows, width),
            ],
            axis=-1,
        )
        previous = lax.dynamic_slice_in_dim(grad_kv_all, offset, fold_size_rows, 1)
        grad_kv_all = lax.dynamic_update_slice_in_dim(grad_kv_all, previous + update, offset, 1)
        return ((grad_q_sum + grad_q, grad_kv_all), None)

    state_now, unused = lax.scan(step_block, state_now, jnp.arange(number))
    grad_queries, grad_kv_all = state_now
    grad_kv = lax.psum_scatter(
        grad_kv_all.astype(jnp.bfloat16), "seq", scatter_dimension=1, tiled=True
    ).astype(jnp.float32)
    grad_keys = grad_kv[..., :width].reshape(canvases, rows, heads, head_size)
    grad_values = grad_kv[..., width:].reshape(canvases, rows, heads, head_size)
    grad_query_cos = rotate(grad_queries, cosine, -sine)
    grad_key_cos = rotate(grad_keys, cosine, -sine)
    grad_query_raw, query_part = cosine_backward(qkv_all[:, :, 0], query_factor, grad_query_cos)
    grad_key_raw, key_part = cosine_backward(qkv_all[:, :, 1], key_factor, grad_key_cos)
    scale_local = (query_part + key_part) / (2.0 * head_scale)
    grad_qkv = (
        jnp.stack([grad_query_raw, grad_key_raw, grad_values], axis=2)
        .astype(jnp.bfloat16)
        .reshape(canvases, rows, 3 * width)
    )
    qkv_term = jnp.einsum("csd,cse->de", normed_attn, grad_qkv, preferred_element_type=jnp.float32)
    grad_normed_attn = jnp.einsum(
        "cse,de->csd", grad_qkv, qkv_full, preferred_element_type=jnp.float32
    )
    grad_in_norm, attn_scale_sum = norm_backward(inputs, inverse_attn, scale_attn, grad_normed_attn)
    input_grad = grad_middle + grad_in_norm
    attn_sums, ffn_sums = lax.psum((attn_scale_sum, ffn_scale_sum), "seq")
    attn_sums = attn_sums.astype(jnp.bfloat16)
    ffn_sums = ffn_sums.astype(jnp.bfloat16)
    cond_grad = jnp.einsum(
        "cd,nd->cn", attn_sums, attn_mod, preferred_element_type=jnp.float32
    ) + jnp.einsum("cd,nd->cn", ffn_sums, ffn_mod, preferred_element_type=jnp.float32)
    leader = lax.axis_index("seq") == 0
    attn_mod_term = jnp.where(
        leader,
        jnp.einsum("cn,cd->nd", conditioning, attn_sums, preferred_element_type=jnp.float32),
        0.0,
    )
    ffn_mod_term = jnp.where(
        leader,
        jnp.einsum("cn,cd->nd", conditioning, ffn_sums, preferred_element_type=jnp.float32),
        0.0,
    )
    terms = (qkv_term, out_term, up_term, down_term, attn_mod_term, ffn_mod_term)
    groups = lax.axis_size("dp")
    owners = groups * seq_count
    packed = pack_terms(terms, (owners,))
    summed = lax.psum_scatter(packed, ("dp", "seq"), scatter_dimension=0, tiled=True)
    packed_row = summed[0]
    qkv_grad, out_grad, up_grad, down_grad, attnmod_grad, ffnmod_grad = unpack_terms(
        packed_row, terms, owners
    )
    scale_grad = lax.psum(scale_local, ("dp", "seq"))
    return (
        block_out,
        input_grad,
        cond_grad,
        qkv_grad,
        out_grad,
        up_grad,
        down_grad,
        attnmod_grad,
        ffnmod_grad,
        scale_grad,
    )


MESH = pl.DeviceIdType.MESH
BF = jnp.bfloat16
F32 = jnp.float32
PLANE = ((1, 0, 0), (0, 0, 1), (1, 0, 1), (0, 1, 0), (1, 1, 0), (0, 1, 1), (1, 1, 1))
CHIPS = ((1, 0), (0, 1), (1, 1))
ERF_P = (
    0.00022905065861350646,
    0.0034082910107109506,
    0.050955695062380861,
    0.18520832239976145,
    1.128379143519084,
)
ERF_Q = (
    -1.1791602954361697e-7,
    0.000023547966471313185,
    0.0010179625278914885,
    0.014070470171167667,
    0.11098505178285362,
    0.49746925110067538,
    1.0,
)


def erf(value):
    value = jnp.clip(value, -3.832506856900711, 3.832506856900711)
    square = value * value
    top = jnp.full_like(value, ERF_P[0])
    for term in ERF_P[1:]:
        top = top * square + term
    bottom = jnp.full_like(value, ERF_Q[0])
    for term in ERF_Q[1:]:
        bottom = bottom * square + term
    return value * top / bottom


def dot(lhs, rhs, on_lhs=1, on_rhs=0):
    return lax.dot_general(
        lhs, rhs, (((on_lhs,), (on_rhs,)), ((), ())), preferred_element_type=F32
    )


def block_kernel(
    lines,
    x_ref,
    cot_ref,
    qkv_ref,
    up_ref,
    out_ref,
    down_ref,
    amod_ref,
    fmod_ref,
    cond_ref,
    crop_ref,
    pos_ref,
    scale_ref,
    table_ref,
    block_out,
    input_grad,
    cond_grad,
    qkv_grad,
    out_grad,
    up_grad,
    down_grad,
    amod_grad,
    fmod_grad,
    scale_grad,
    *scratch,
):
    names = list(scratch_plan(lines, x_ref, qkv_ref, up_ref, out_ref, down_ref))
    s = types.SimpleNamespace(**dict(zip(names, scratch)))
    dp = lax.axis_index("dp")
    y = lax.axis_index("seq")
    z = dp // 4
    x = (dp // 2) % 2
    c = dp % 2
    rows, width = x_ref.shape
    own_cols = qkv_ref.shape[2]
    lanes = own_cols // 3
    half_head = out_ref.shape[0]
    hidden = up_ref.shape[2] // 2
    down_rows = down_ref.shape[0]
    up_rows = up_ref.shape[1]
    mod_rows = amod_ref.shape[0]
    canvas_rows = 2 * rows
    crops = canvas_rows // 16
    me = 4 * x + 2 * c + y
    device_index = 8 * z + me

    def member(step):
        return 4 * ((x + step[0]) % 2) + 2 * ((c + step[1]) % 2) + (y + step[2]) % 2

    def device(step, along=0):
        return (
            ((z + along) % lines) * 4 + ((x + step[0]) % 2) * 2 + (c + step[1]) % 2,
            (y + step[2]) % 2,
        )

    here = (0, 0, 0)
    core = (0, 1, 0)
    sends = []

    class Copy:
        def __init__(self, src, dst_there, dst_here, sems, at, target):
            self.out = pltpu.make_async_remote_copy(
                src_ref=src,
                dst_ref=dst_there,
                send_sem=sems.at[0, at],
                recv_sem=sems.at[1, at],
                device_id=target,
                device_id_type=MESH,
            )
            self.into = pltpu.make_async_remote_copy(
                src_ref=src,
                dst_ref=dst_here,
                send_sem=sems.at[0, at],
                recv_sem=sems.at[1, at],
                device_id=target,
                device_id_type=MESH,
            )

        def start(self):
            self.out.start()
            sends.append(self.out)

        def arrive(self):
            self.into.wait_recv()

    class Gather:
        def __init__(self, buffer, sems):
            self.buffer = buffer
            at = lambda step: buffer.at[member(step)]
            self.across = [
                Copy(at(here), at(here), at((dx, 0, dy)), sems, k, device((dx, 0, dy)))
                for k, (dx, dy) in enumerate(CHIPS)
            ]
            self.pair = Copy(at(here), at(here), at(core), sems, 3, device(core))
            self.forward = [
                Copy(at((dx, 0, dy)), at((dx, 0, dy)), at((dx, 1, dy)), sems, 4 + k, device(core))
                for k, (dx, dy) in enumerate(CHIPS)
            ]

        def start(self):
            for copy in self.across:
                copy.start()
            self.pair.start()

        def middle(self):
            for copy, onward in zip(self.across, self.forward):
                copy.arrive()
                onward.start()

        def finish(self):
            self.pair.arrive()
            for copy in self.forward:
                copy.arrive()

    class Reduce:
        def __init__(self, part, pair_in, onward, chip_in, sems):
            self.part, self.pair_in, self.onward, self.chip_in = part, pair_in, onward, chip_in
            steps = ((0, 0),) + CHIPS
            self.pair = [
                Copy(
                    part.at[member((dx, 1, dy))],
                    pair_in.at[k],
                    pair_in.at[k],
                    sems,
                    k,
                    device(core),
                )
                for k, (dx, dy) in enumerate(steps)
            ]
            self.across = [
                Copy(
                    onward.at[k], chip_in.at[k], chip_in.at[k], sems, 4 + k, device((dx, 0, dy))
                )
                for k, (dx, dy) in enumerate(CHIPS)
            ]

        def start(self):
            for k in (1, 2, 3, 0):
                self.pair[k].start()

        def middle(self):
            for k, (dx, dy) in enumerate(CHIPS):
                self.pair[k + 1].arrive()
                total = self.part[member((dx, 0, dy))].astype(F32) + self.pair_in[k + 1].astype(F32)
                self.onward[k] = total.astype(BF)
                self.across[k].start()

        def finish(self):
            self.pair[0].arrive()
            total = self.part[me].astype(F32) + self.pair_in[0].astype(F32)
            for k in range(len(CHIPS)):
                self.across[k].arrive()
                total = total + self.chip_in[k].astype(F32)
            return total

    class Spread:
        def __init__(self, source, target, sems):
            self.source, self.target = source, target
            self.copies = [
                Copy(
                    source.at[member(step)],
                    target.at[me],
                    target.at[member(step)],
                    sems,
                    k,
                    device(step),
                )
                for k, step in enumerate(PLANE)
            ]

        def start(self):
            for copy in self.copies:
                copy.start()
            self.target[me] = self.source[me]

        def finish(self):
            for copy in self.copies:
                copy.arrive()

    class Share:
        def __init__(self, buffer, sems, block=None):
            self.copies = [
                Copy(
                    buffer.at[me] if block is None else block,
                    buffer.at[me],
                    buffer.at[member(step)],
                    sems,
                    k,
                    device(step),
                )
                for k, step in enumerate(PLANE)
            ]

        def start(self):
            for copy in self.copies:
                copy.start()

        def finish(self):
            for copy in self.copies:
                copy.arrive()

    class Line:
        def __init__(self, buffer, sems, first=None):
            self.copies = []
            for along in range(1, lines):
                back = (z + lines - along) % lines
                if first is None:
                    mine, theirs = buffer.at[z], buffer.at[back]
                else:
                    mine, theirs = buffer.at[pl.ds(first * z, first)], buffer.at[pl.ds(first * back, first)]
                self.copies.append(Copy(mine, mine, theirs, sems, along - 1, device(here, along)))

        def start(self):
            for copy in self.copies:
                copy.start()

        def finish(self):
            for copy in self.copies:
                copy.arrive()

    class Fold:
        def __init__(self, terms, landed, sems):
            self.terms, self.landed = terms, landed
            self.copies = [
                Copy(
                    terms.at[(z + along) % lines],
                    landed.at[along - 1],
                    landed.at[along - 1],
                    sems,
                    along - 1,
                    device(here, along),
                )
                for along in range(1, lines)
            ]

        def start(self):
            for copy in self.copies:
                copy.start()

        def finish(self):
            total = self.terms[z].astype(F32)
            for k, copy in enumerate(self.copies):
                copy.arrive()
                total = total + self.landed[k].astype(F32)
            return total

    class Canvases:
        def __init__(self, buffer, sems):
            self.near = [
                Copy(
                    buffer.at[dp],
                    buffer.at[dp],
                    buffer.at[device(step)[0]],
                    sems,
                    k,
                    device(step),
                )
                for k, step in enumerate(((1, 0, 0), (0, 1, 0), (1, 1, 0)))
            ]
            self.far = []
            for along in range(1, lines):
                back = (z + lines - along) % lines
                mine = buffer.at[pl.ds(4 * z, 4)]
                self.far.append(
                    Copy(
                        mine,
                        mine,
                        buffer.at[pl.ds(4 * back, 4)],
                        sems,
                        2 + along,
                        device(here, along),
                    )
                )

        def start(self):
            for copy in self.near:
                copy.start()

        def middle(self):
            for copy in self.near:
                copy.arrive()
            for copy in self.far:
                copy.start()

        def finish(self):
            for copy in self.far:
                copy.arrive()

    def each_canvas(body, which=None):
        if which is None:
            lax.fori_loop(0, 4, lambda t, carry: (body(t), carry)[1], 0)
        else:
            base = c if which == 0 else 1 - c
            lax.fori_loop(0, 2, lambda t, carry: (body(2 * t + base), carry)[1], 0)

    def slots(t):
        return pl.ds(2 * t, 2)

    lane = lax.broadcasted_iota(jnp.int32, (1, lanes), 1)
    first_head = lane < lanes // 2
    first_part = (lane % 16) < 8

    def per_head(pair):
        return jnp.where(first_head, pair[0], pair[1])

    def head_sums(value):
        left = jnp.where(first_head, value, 0.0)
        right = jnp.where(first_head, 0.0, value)
        return (
            jnp.sum(left, axis=-1, keepdims=True),
            jnp.sum(right, axis=-1, keepdims=True),
        )

    def partner(value):
        return jnp.where(
            first_part, pltpu.roll(value, lanes - 8, 1), pltpu.roll(value, 8, 1)
        )

    ids = s.ids
    ids[me] = jnp.zeros(ids.shape[1:], jnp.int32)
    ids[me, 0:1, :] = crop_ref[...]
    ids[me, 1:3, :] = pos_ref[0]
    conds = s.conds
    conds[dp] = jnp.zeros(conds.shape[1:], F32)
    for r in range(cond_ref.shape[1] // 128):
        conds[dp, r : r + 1, :] = cond_ref[:, 128 * r : 128 * (r + 1)].astype(F32)
    s.tokens[me] = x_ref[...]
    s.cots[me] = cot_ref[...]
    s.out_line[z] = out_ref[...]
    s.down_line[z] = down_ref[...]
    mod_full = s.mod_full
    mod_full[...] = jnp.zeros(mod_full.shape, BF)
    mod_full[0:mod_rows, 0:width] = amod_ref[...]
    mod_full[0:mod_rows, width : 2 * width] = fmod_ref[...]

    barrier = pltpu.get_barrier_semaphore()
    partners = [device(step) for step in PLANE] + [device(here, k) for k in range(1, lines)]
    for target in partners:
        pl.semaphore_signal(barrier, inc=1, device_id=target, device_id_type=MESH)
    pl.semaphore_wait(barrier, len(partners))

    cond_copy = Canvases(conds, s.sem_cond)
    ids_copy = Share(ids, s.sem_ids)
    qkv_spread = Spread(qkv_ref, s.qkv_line.at[z], s.sem_qkv_spread)
    up_spread = Spread(up_ref, s.up_line.at[z], s.sem_up_spread)
    qkv_line = Line(s.qkv_line, s.sem_qkv_line)
    out_line = Line(s.out_line, s.sem_out_line)
    up_line = Line(s.up_line, s.sem_up_line)
    down_line = Line(s.down_line, s.sem_down_line)
    token_copy = Gather(s.tokens, s.sem_tokens)
    cot_copy = Gather(s.cots, s.sem_cots)
    cond_copy.start()
    qkv_spread.start()
    ids_copy.start()
    out_line.start()
    token_copy.start()
    cond_copy.middle()
    qkv_spread.finish()
    qkv_line.start()
    up_spread.start()

    cond_copy.finish()
    picked = jnp.zeros((conds.shape[0], 128), F32)
    for r in range(cond_ref.shape[1] // 128):
        at_row = lax.broadcasted_iota(jnp.int32, (128, 128), 0) + 128 * r
        at_col = lax.broadcasted_iota(jnp.int32, (128, 128), 1)
        choose = (at_row == at_col + mod_rows * device_index) & (at_col < mod_rows)
        picked = picked + dot(
            conds[:, r, :].astype(BF), jnp.where(choose, 1.0, 0.0).astype(BF)
        )
    cond_mine = picked.astype(BF)
    block_cols = 2 * width // 8
    mod_terms, mod_in = s.mod_terms, s.mod_in
    for m in range(8):
        mod_terms[m] = dot(cond_mine, mod_full[:, block_cols * m : block_cols * (m + 1)])
    mod_spread = Spread(mod_terms, mod_in, s.sem_mod_spread)
    mod_spread.start()
    token_copy.middle()
    mod_spread.finish()
    mod_sum = mod_in[0]
    for m in range(1, 8):
        mod_sum = mod_sum + mod_in[m]
    mod_line = s.mod_line
    mod_line[z] = mod_sum
    mod_copy = Line(mod_line, s.sem_mod_line)
    mod_copy.start()
    up_spread.finish()
    up_line.start()
    down_line.start()
    mod_copy.finish()
    mod_sum = mod_line[0]
    for k in range(1, lines):
        mod_sum = mod_sum + mod_line[k]
    s.mod_total[...] = 1.0 + mod_sum
    mod_share = Share(s.mods, s.sem_mods)
    own_rows = s.mod_total[pl.ds(8 * (z // 2), 8), :]
    s.mods[me] = own_rows
    mod_share.start()
    token_copy.finish()
    mod_share.finish()
    scales = s.scales
    for m in range(8):
        scales[:, block_cols * m : block_cols * (m + 1)] = s.mods[m]
    cot_copy.start()
    ids_copy.finish()

    def scale_row(canvas, ffn):
        row = scales[pl.ds(4 * (z % 2) + canvas, 1), :]
        return row[:, width:] if ffn else row[:, :width]

    own_canvas = 2 * x + c

    def inverse_rms(value):
        return lax.rsqrt(jnp.mean(value * value, axis=-1, keepdims=True) + eps_norm)

    normed = s.normed

    def norm_tokens(canvas):
        value = s.tokens[slots(canvas)].reshape(canvas_rows, width).astype(F32)
        scaled = value * inverse_rms(value) * scale_row(canvas, False)
        normed[slots(canvas)] = scaled.astype(BF).reshape(2, rows, width)

    each_canvas(norm_tokens)
    out_line.finish()
    out_half = s.out_half
    half_copy = Copy(
        s.out_line.at[pl.ds(2 * (1 - y), 2)],
        out_half,
        out_half,
        s.sem_half,
        0,
        device((0, 0, 1)),
    )
    half_copy.start()
    qkv_line.finish()
    head_of = lambda k: 8 * y + 4 * k + 2 * x + c
    head_scales = [scale_ref[head_of(k)] for k in range(2)]
    scale_lanes = per_head(head_scales)
    root_lanes = jnp.sqrt(scale_lanes)

    def canvas_ids(canvas, row):
        return jnp.concatenate(
            [ids[2 * canvas, row : row + 1, :], ids[2 * canvas + 1, row : row + 1, :]], axis=1
        )

    def one_hot(row, count):
        return jnp.where(
            lax.broadcasted_iota(jnp.int32, (count, canvas_rows), 0) == row, 1.0, 0.0
        ).astype(BF)

    def attend(canvas):
        qkv = dot(
            normed[slots(canvas)].reshape(canvas_rows, width),
            s.qkv_line[...].reshape(width, own_cols),
        )
        places = [one_hot(canvas_ids(canvas, 1), 16), one_hot(canvas_ids(canvas, 2), 16)]
        turn = dot(jnp.concatenate(places + places, axis=0), table_ref[me], 0, 0)
        s.turns[canvas] = turn
        cosine, sine = turn[:, :lanes], turn[:, lanes:]
        rotated = []
        for part in range(2):
            raw = qkv[:, part * lanes : (part + 1) * lanes]
            s.raw[canvas, part] = raw
            sums = head_sums(raw * raw)
            factor = per_head([lax.rsqrt(value + eps_cosine) for value in sums]) * root_lanes
            turned = raw * factor
            turned = (turned * cosine + partner(turned) * sine).astype(BF)
            s.rotated[canvas, part] = turned
            rotated.append(turned)
        values = qkv[:, 2 * lanes :].astype(BF)
        s.rotated[canvas, 2] = values
        crop_hot = one_hot(canvas_ids(canvas, 0), crops)
        allowed = dot(crop_hot, crop_hot, 0, 0)
        heads = []
        for k in range(2):
            mine = first_head if k == 0 else jnp.logical_not(first_head)
            query = jnp.where(mine, rotated[0], jnp.zeros_like(rotated[0]))
            weights = jnp.exp(dot(query, rotated[1], 1, 1)) * allowed
            probs = weights / jnp.sum(weights, axis=-1, keepdims=True)
            s.probs[canvas, k] = probs
            heads.append(dot(probs.astype(BF), values))
        attended = per_head(heads)
        s.raw_attended[canvas] = attended
        s.attended[canvas] = attended.astype(BF)

    each_canvas(attend)
    half_copy.arrive()
    out_full = s.out_full
    for k in range(2):
        out_full[k, y] = s.out_line[2 * y + k]
        out_full[k, 1 - y] = out_half[k]

    def to_middle(canvas):
        value = dot(s.attended[canvas], out_full[...].reshape(lanes, width))
        s.mid_part[slots(canvas)] = value.astype(BF).reshape(2, rows, width)

    mid_reduce = Reduce(
        s.mid_part, s.mid_pair, s.mid_onward, s.mid_chip, s.sem_mid
    )
    each_canvas(to_middle, 1)
    mid_reduce.start()
    each_canvas(to_middle, 0)
    mid_reduce.middle()
    cot_copy.middle()
    middle = x_ref[...].astype(F32) + mid_reduce.finish()
    s.middle[...] = middle
    ffn_row = scale_row(own_canvas, True)
    s.ffn[me] = (middle * inverse_rms(middle) * ffn_row).astype(BF)
    ffn_copy = Gather(s.ffn, s.sem_ffn)
    ffn_copy.start()
    cot_copy.finish()
    up_line.finish()

    def feed(canvas):
        up = dot(
            s.ffn[slots(canvas)].reshape(canvas_rows, width),
            s.up_line[...].reshape(width, 2 * hidden),
        )
        value, gate = up[:, :hidden], up[:, hidden:]
        cdf = 0.5 + 0.5 * erf(gate * math.sqrt(0.5))
        act = gate * cdf
        s.hidden[canvas] = (value * act).astype(BF)
        s.act[canvas] = act
        density = jnp.exp(-0.5 * gate * gate) * (1.0 / math.sqrt(2.0 * math.pi))
        s.slope[canvas] = value * (cdf + gate * density)

    ffn_copy.middle()
    each_canvas(feed, 0)
    ffn_copy.finish()
    each_canvas(feed, 1)

    def cots_of(canvas):
        return s.cots[slots(canvas)].reshape(canvas_rows, width)

    all_rows = 8 * rows
    chunk = 256

    def down_term(n, carry):
        cols = pl.ds(pl.multiple_of(n * chunk, chunk), chunk)
        term = dot(
            s.hidden[...].reshape(all_rows, hidden),
            s.cots[:, :, cols].reshape(all_rows, chunk),
            0,
            0,
        )
        s.down_term[:, :, cols] = term.astype(BF).reshape(lines, down_rows, chunk)
        return carry

    lax.fori_loop(0, width // chunk, down_term, 0)
    down_fold = Fold(s.down_term, s.down_in, s.sem_down_fold)
    down_fold.start()
    down_line.finish()

    def feed_back(canvas):
        grad_hidden = dot(cots_of(canvas), s.down_line[...].reshape(hidden, width), 1, 1)
        grad_up = jnp.concatenate(
            [grad_hidden * s.act[canvas], grad_hidden * s.slope[canvas]], axis=1
        ).astype(BF)
        s.grad_up[canvas] = grad_up
        part = dot(grad_up, s.up_line[...].reshape(width, 2 * hidden), 1, 1)
        s.gnf_part[slots(canvas)] = part.astype(BF).reshape(2, rows, width)

    gnf_reduce = Reduce(
        s.gnf_part, s.gnf_pair, s.gnf_onward, s.gnf_chip, s.sem_gnf
    )
    each_canvas(feed_back, 1)
    gnf_reduce.start()
    each_canvas(feed_back, 0)
    gnf_reduce.middle()

    def up_term(k, carry):
        cols = pl.ds(pl.multiple_of(k * 8 * up_rows, 8 * up_rows), 8 * up_rows)
        term = dot(
            s.ffn[:, :, cols].reshape(all_rows, 8 * up_rows),
            s.grad_up[...].reshape(all_rows, 2 * hidden),
            0,
            0,
        )
        s.up_term[k] = term.astype(BF).reshape(8, up_rows, 2 * hidden)
        return carry

    lax.fori_loop(0, lines, up_term, 0)
    up_fold = Fold(s.up_term, s.up_in, s.sem_up_fold)
    up_fold.start()

    def norm_back(value, row, grad):
        inverse = inverse_rms(value)
        scaled = grad * row
        along = jnp.mean(scaled * value, axis=-1, keepdims=True)
        grad_value = inverse * scaled - value * (inverse * inverse * inverse) * along
        return grad_value, jnp.sum(grad * value * inverse, axis=0, keepdims=True)

    def put_row(target, offset, row):
        for r in range(width // 128):
            target[offset + r : offset + r + 1, :] = row[:, 128 * r : 128 * (r + 1)]

    grad_mid, ffn_sum = norm_back(s.middle[...], ffn_row, gnf_reduce.finish())
    grad_middle = cot_ref[...].astype(F32) + grad_mid
    s.grad_middle[...] = grad_middle
    s.branch[me] = grad_middle.astype(BF)
    branch_copy = Gather(s.branch, s.sem_branch)
    branch_copy.start()
    sums_own = s.sums_own
    put_row(sums_own, 8, ffn_sum)

    def to_out(canvas):
        part = dot(s.hidden[canvas], s.down_line[...].reshape(hidden, width))
        s.out_part[slots(canvas)] = part.astype(BF).reshape(2, rows, width)

    out_reduce = Reduce(
        s.out_part, s.out_pair, s.out_onward, s.out_chip, s.sem_out
    )
    each_canvas(to_out)
    branch_copy.middle()
    out_reduce.start()

    def attend_back(canvas):
        branch = s.branch[slots(canvas)].reshape(canvas_rows, width)
        grad_att = dot(branch, out_full[...].reshape(lanes, width), 1, 1).astype(BF)
        turn = s.turns[canvas]
        cosine, sine = turn[:, :lanes], turn[:, lanes:]
        query, key, values = (s.rotated[canvas, part] for part in range(3))
        deltas = head_sums(grad_att.astype(F32) * s.raw_attended[canvas])
        grads = [[], [], []]
        for k in range(2):
            mine = first_head if k == 0 else jnp.logical_not(first_head)
            probs = s.probs[canvas, k]
            one_head = jnp.where(mine, grad_att, jnp.zeros_like(grad_att))
            dotted = dot(one_head, values, 1, 1)
            slope = (probs * (dotted - deltas[k])).astype(BF)
            grads[0].append(dot(slope, key))
            grads[1].append(dot(slope, query, 0, 0))
            grads[2].append(dot(probs.astype(BF), grad_att, 0, 0))
        pieces = []
        for part in range(2):
            grad = per_head(grads[part])
            grad = grad * cosine - partner(grad) * sine
            raw = s.raw[canvas, part]
            squares = [value + eps_cosine for value in head_sums(raw * raw)]
            along = head_sums(grad * raw)
            inverse = [lax.rsqrt(value) for value in squares]
            factor = per_head(inverse) * root_lanes
            shrink = per_head([along[k] * inverse[k] * inverse[k] for k in range(2)])
            pieces.append(factor * grad - raw * factor * shrink)
            term = per_head([jnp.sum(along[k] * inverse[k], axis=0, keepdims=True) for k in range(2)])
            s.head_terms[...] += term * root_lanes / (2.0 * scale_lanes)
        pieces.append(per_head(grads[2]))
        grad_qkv = jnp.concatenate(pieces, axis=1).astype(BF)
        s.grad_qkv[canvas] = grad_qkv
        part = dot(grad_qkv, s.qkv_line[...].reshape(width, own_cols), 1, 1)
        s.gna_part[slots(canvas)] = part.astype(BF).reshape(2, rows, width)

    s.head_terms[...] = jnp.zeros((1, lanes), F32)
    branch_copy.finish()
    gna_reduce = Reduce(
        s.gna_part, s.gna_pair, s.gna_onward, s.gna_chip, s.sem_gna
    )
    each_canvas(attend_back, 1)
    gna_reduce.start()
    each_canvas(attend_back, 0)
    gna_reduce.middle()

    def qkv_term(k, carry):
        cols = pl.ds(pl.multiple_of(k * 8 * up_rows, 8 * up_rows), 8 * up_rows)
        term = dot(
            normed[:, :, cols].reshape(all_rows, 8 * up_rows),
            s.grad_qkv[...].reshape(all_rows, own_cols),
            0,
            0,
        )
        s.qkv_term[k] = term.astype(BF).reshape(8, up_rows, own_cols)
        return carry

    lax.fori_loop(0, lines, qkv_term, 0)
    qkv_fold = Fold(s.qkv_term, s.qkv_in, s.sem_qkv_fold)
    qkv_fold.start()

    term = dot(
        s.attended[...].reshape(all_rows, lanes),
        s.branch[...].reshape(all_rows, width),
        0,
        0,
    ).astype(BF).reshape(2, 2, half_head, width)
    halves = s.out_halves
    for k in range(2):
        for half in range(2):
            halves[half, k] = term[k, half]
    swap = Copy(
        halves.at[1 - y], s.out_swap, s.out_swap, s.sem_half, 1, device((0, 0, 1))
    )
    swap.start()

    grad_in, attn_sum = norm_back(x_ref[...].astype(F32), scale_row(own_canvas, False), gna_reduce.finish())
    input_grad[...] = s.grad_middle[...] + grad_in
    put_row(sums_own, 0, attn_sum)
    head_rows = lax.broadcasted_iota(jnp.int32, (8, lanes), 0)
    head_lane = lax.broadcasted_iota(jnp.int32, (8, lanes), 1)
    head_tile = jnp.zeros((8, lanes), F32)
    for k in range(2):
        value = jnp.sum(
            jnp.where(lane == k * (lanes // 2), s.head_terms[...], 0.0), axis=1, keepdims=True
        )
        head_tile = head_tile + jnp.where(
            (head_rows == 0) & (head_lane == head_of(k)), value, 0.0
        )
    sums_own[16:24, :] = head_tile
    sums_copy = Copy(
        sums_own, s.sums_pair, s.sums_pair, s.sem_half, 2, device((0, 0, 1))
    )
    sums_copy.start()
    out_reduce.middle()
    swap.arrive()
    out_terms = s.out_terms
    for k in range(2):
        out_terms[2 * y + k] = halves[y, k]
        out_terms[2 * (1 - y) + k] = s.out_swap[k]
    out_fold = Fold(out_terms, s.out_in, s.sem_out_fold)
    out_fold.start()
    sums_copy.arrive()
    sums = s.sums
    sums[dp] = sums_own[...] + s.sums_pair[...]
    all_sums = Canvases(sums, s.sem_sums)
    all_sums.start()
    down_grad[...] = down_fold.finish().reshape(down_rows, width)
    all_sums.middle()
    block_out[...] = (s.middle[...] + out_reduce.finish()).astype(BF)
    s.up_sum[...] = up_fold.finish().astype(BF)
    up_return = Spread(s.up_sum, s.up_back, s.sem_up_back)
    up_return.start()
    s.qkv_sum[...] = qkv_fold.finish().astype(BF)
    qkv_return = Spread(s.qkv_sum, s.qkv_back, s.sem_qkv_back)
    qkv_return.start()

    all_sums.finish()
    rounded = [
        jnp.concatenate([sums[:, offset + r, :] for r in range(width // 128)], axis=1).astype(BF)
        for offset in (0, 8)
    ]
    mine_for = dot(rounded[0], mod_full[:, :width], 1, 1) + dot(
        rounded[1], mod_full[:, width:], 1, 1
    )
    cond_line, cond_in = s.cond_line, s.cond_in
    s.cond_all[...] = mine_for
    for k in range(lines):
        cond_line[k] = s.cond_all[8 * (k // 2) : 8 * (k // 2) + 8, :]
    cond_send = [
        Copy(
            cond_line.at[(z + along) % lines],
            cond_in.at[me, z],
            cond_in.at[me, (z + lines - along) % lines],
            s.sem_cond_line,
            along - 1,
            device(here, along),
        )
        for along in range(1, lines)
    ]
    for copy in cond_send:
        copy.start()
    cond_in[me, z] = cond_line[z]
    amod_grad[...] = dot(cond_mine, rounded[0], 0, 0)[:mod_rows]
    fmod_grad[...] = dot(cond_mine, rounded[1], 0, 0)[:mod_rows]
    head_sum = sums[0, 16:17, :]
    for k in range(1, sums.shape[0]):
        head_sum = head_sum + sums[k, 16:17, :]
    scale_grad[...] = head_sum
    for copy in cond_send:
        copy.arrive()
    cond_share = Share(cond_in, s.sem_cond_share)
    cond_share.start()
    out_grad[...] = out_fold.finish()
    cond_share.finish()
    for k in range(lines):
        for m in range(8):
            at_row = 8 * k + m
            cond_grad[at_row : at_row + 1, :] = cond_in[m, k, pl.ds(4 * (z % 2) + own_canvas, 1), :]
    up_return.finish()
    up_grad[...] = s.up_back[...]
    qkv_return.finish()
    qkv_grad[...] = s.qkv_back[...]
    for copy in sends:
        copy.wait_send()


def scratch_plan(lines, x_ref, qkv_ref, up_ref, out_ref, down_ref):
    rows, width = x_ref.shape
    own_cols = qkv_ref.shape[2]
    up_rows, up_cols = up_ref.shape[1:]
    hidden = up_cols // 2
    half_head = out_ref.shape[0]
    down_rows = down_ref.shape[0]
    lanes = own_cols // 3
    groups = 4 * lines
    plane = (8, rows, width)
    vm = lambda shape, kind=BF: pltpu.VMEM(shape, kind)
    sem = lambda count: pltpu.SemaphoreType.DMA((2, count))
    plan = dict(
        ids=vm((8, 8, rows), jnp.int32),
        conds=vm((groups, 8, 128), F32),
        tokens=vm(plane),
        cots=vm(plane),
        normed=vm(plane),
        ffn=vm(plane),
        branch=vm(plane),
        qkv_line=vm((lines, 8, up_rows, own_cols)),
        up_line=vm((lines, 8, up_rows, up_cols)),
        out_line=vm((lines, half_head, width)),
        down_line=vm((lines, down_rows, width)),
        out_half=vm((2, half_head, width)),
        out_full=vm((2, 2, half_head, width)),
        mod_full=vm((128, 2 * width)),
        mod_terms=vm((8, groups, width // 4), F32),
        mod_in=vm((8, groups, width // 4), F32),
        mod_line=vm((lines, groups, width // 4), F32),
        mod_total=vm((groups, width // 4), F32),
        mods=vm((8, 8, width // 4), F32),
        scales=vm((8, 2 * width), F32),
        turns=vm((4, 2 * rows, 2 * lanes), F32),
        raw=vm((4, 2, 2 * rows, lanes), F32),
        rotated=vm((4, 3, 2 * rows, lanes)),
        probs=vm((4, 2, 2 * rows, 2 * rows), F32),
        raw_attended=vm((4, 2 * rows, lanes), F32),
        attended=vm((4, 2 * rows, lanes)),
        middle=vm((rows, width), F32),
        grad_middle=vm((rows, width), F32),
        hidden=vm((4, 2 * rows, hidden)),
        act=vm((4, 2 * rows, hidden), F32),
        slope=vm((4, 2 * rows, hidden), F32),
        grad_up=vm((4, 2 * rows, up_cols)),
        grad_qkv=vm((4, 2 * rows, own_cols)),
        head_terms=vm((1, lanes), F32),
        sums_own=vm((24, 128), F32),
        sums_pair=vm((24, 128), F32),
        sums=vm((groups, 24, 128), F32),
        cond_all=vm((groups, 128), F32),
        cond_line=vm((lines, 8, 128), F32),
        cond_in=vm((8, lines, 8, 128), F32),
        down_term=vm((lines, down_rows, width)),
        down_in=vm((lines - 1, down_rows, width)),
        up_term=vm((lines, 8, up_rows, up_cols)),
        up_in=vm((lines - 1, 8, up_rows, up_cols)),
        up_sum=vm((8, up_rows, up_cols)),
        up_back=vm((8, up_rows, up_cols)),
        qkv_term=vm((lines, 8, up_rows, own_cols)),
        qkv_in=vm((lines - 1, 8, up_rows, own_cols)),
        qkv_sum=vm((8, up_rows, own_cols)),
        qkv_back=vm((8, up_rows, own_cols)),
        out_halves=vm((2, 2, half_head, width)),
        out_swap=vm((2, half_head, width)),
        out_terms=vm((lines, half_head, width)),
        out_in=vm((lines - 1, half_head, width)),
    )
    for name in ("mid", "gnf", "out", "gna"):
        plan[name + "_part"] = vm(plane)
        plan[name + "_pair"] = vm((4, rows, width))
        plan[name + "_onward"] = vm((3, rows, width))
        plan[name + "_chip"] = vm((3, rows, width))
        plan["sem_" + name] = sem(7)
    plan.update(
        sem_tokens=sem(7),
        sem_cots=sem(7),
        sem_ffn=sem(7),
        sem_branch=sem(7),
        sem_ids=sem(7),
        sem_qkv_spread=sem(7),
        sem_up_spread=sem(7),
        sem_mod_spread=sem(7),
        sem_mods=sem(7),
        sem_up_back=sem(7),
        sem_qkv_back=sem(7),
        sem_cond_share=sem(7),
        sem_qkv_line=sem(lines - 1),
        sem_up_line=sem(lines - 1),
        sem_out_line=sem(lines - 1),
        sem_down_line=sem(lines - 1),
        sem_mod_line=sem(lines - 1),
        sem_cond_line=sem(lines - 1),
        sem_down_fold=sem(lines - 1),
        sem_up_fold=sem(lines - 1),
        sem_qkv_fold=sem(lines - 1),
        sem_out_fold=sem(lines - 1),
        sem_cond=sem(lines + 2),
        sem_sums=sem(lines + 2),
        sem_half=sem(3),
    )
    return plan


def turn_tables(heads, lines):
    head_size = 64
    table = np.zeros((heads, 2, 16, 2, head_size), np.float64)
    for axis in range(2):
        for j in range(8):
            freq = math.pi * 10.0 ** ((j * heads + np.arange(heads)) / (8.0 * heads))
            unit = (2.0 * np.arange(16) + 1.0) / 16.0 - 1.0
            angle = freq[:, None].astype(np.float32) * unit[None, :].astype(np.float32)
            angle = angle.astype(np.float64)
            for half in range(2):
                at = axis * 16 + half * 8 + j
                table[:, axis, :, 0, at] = np.cos(angle)
                table[:, axis, :, 1, at] = np.sin(angle) * (1.0 if half else -1.0)
    table[:, 0, :, 0, 32:] = 1.0
    high = table.astype(ml_dtypes.bfloat16)
    low = (table - high.astype(np.float64)).astype(ml_dtypes.bfloat16)
    parts = []
    for term in (high, low):
        term = term.reshape(2, 2, 2, 2, 2, 16, 2, head_size)
        term = term.transpose(2, 3, 0, 4, 5, 6, 1, 7)
        parts.append(term.reshape(8, 32, 4 * head_size))
    return np.concatenate(parts, axis=1)


def plane_shards(
    block_in,
    conditioning,
    crop_ids,
    positions,
    qkv_weight,
    out_weight,
    up_weight,
    down_weight,
    attn_modulate,
    ffn_modulate,
    head_scale,
    cotangent,
):
    lines = lax.axis_size("dp") // 4
    rows, width = block_in.shape[1:]
    heads = head_scale.shape[0]
    up_rows = qkv_weight.shape[0]
    own_hidden = down_weight.shape[0]
    qkv = qkv_weight.reshape(up_rows, 3, 2, 2, 2, 2, 64).transpose(4, 5, 2, 0, 1, 3, 6)
    qkv = qkv.reshape(8, up_rows, -1)
    up = up_weight.reshape(up_rows, 2, lines, 8, own_hidden).transpose(3, 0, 1, 2, 4)
    up = up.reshape(8, up_rows, -1)
    tables = jnp.asarray(turn_tables(heads, lines))
    kinds = jax.ShapeDtypeStruct
    operands = (
        block_in[0],
        cotangent[0],
        qkv,
        up,
        out_weight,
        down_weight,
        attn_modulate,
        ffn_modulate,
        conditioning,
        crop_ids,
        positions,
        head_scale,
        tables,
    )
    plan = scratch_plan(lines, operands[0], qkv, up, out_weight, down_weight)
    in_vmem = pl.BlockSpec(memory_space=pltpu.VMEM)
    in_specs = [in_vmem] * len(operands)
    in_specs[11] = pl.BlockSpec(memory_space=pltpu.SMEM)
    results = pl.pallas_call(
        functools.partial(block_kernel, lines),
        out_shape=(
            kinds((rows, width), BF),
            kinds((rows, width), F32),
            kinds((8 * lines, 128), F32),
            kinds(qkv.shape, BF),
            kinds(out_weight.shape, F32),
            kinds(up.shape, BF),
            kinds(down_weight.shape, F32),
            kinds(attn_modulate.shape, F32),
            kinds(ffn_modulate.shape, F32),
            kinds((1, 128), F32),
        ),
        in_specs=in_specs,
        out_specs=[in_vmem] * 10,
        scratch_shapes=list(plan.values()),
        compiler_params=pltpu.CompilerParams(
            collective_id=0, has_side_effects=True, vmem_limit_bytes=63 * 2**20
        ),
    )(*operands)
    block_out, input_grad, cond, qkv_back, out_grad, up_back, down_grad, amod, fmod, scale = results
    mod_rows = attn_modulate.shape[0]
    cond_grad = cond[:, :mod_rows].reshape(1, -1)
    qkv_grad = qkv_back.reshape(2, 2, 2, up_rows, 3, 2, 64).transpose(3, 4, 2, 5, 0, 1, 6)
    qkv_grad = qkv_grad.reshape(qkv_weight.shape).astype(F32)
    up_grad = up_back.reshape(8, up_rows, 2, lines, own_hidden).transpose(1, 2, 3, 0, 4)
    up_grad = up_grad.reshape(up_weight.shape).astype(F32)
    return (
        block_out[None],
        input_grad[None],
        cond_grad,
        qkv_grad,
        out_grad,
        up_grad,
        down_grad,
        amod,
        fmod,
        scale[0, :heads],
    )


def in_planes(mesh):
    return mesh.shape["seq"] == 2 and mesh.shape["dp"] == 16


def solution(mesh):
    in_specs = (
        P("dp", "seq", None),
        P("dp", None),
        P("dp", "seq"),
        P("dp", None, "seq"),
        P(("dp", "seq"), None),
        P(("dp", "seq"), None),
        P(("dp", "seq"), None),
        P(("dp", "seq"), None),
        P(("dp", "seq"), None),
        P(("dp", "seq"), None),
        P(),
        P("dp", "seq", None),
    )
    out_specs = (
        P("dp", "seq", None),
        P("dp", "seq", None),
        P("dp", None),
        P(("dp", "seq"), None),
        P(("dp", "seq"), None),
        P(("dp", "seq"), None),
        P(("dp", "seq"), None),
        P(("dp", "seq"), None),
        P(("dp", "seq"), None),
        P(),
    )
    body = plane_shards if in_planes(mesh) else shards
    return jax.shard_map(body, mesh=mesh, in_specs=in_specs, out_specs=out_specs, check_vma=False)
```

```python
import functools
import math
import types

import jax
import jax.numpy as jnp
import ml_dtypes
import numpy as np
from jax import lax
from jax.experimental import pallas as pl
from jax.experimental.pallas import tpu as pltpu
from jax.sharding import PartitionSpec as P

eps_norm = 1e-06
eps_cosine = 1e-06
negative = -1e30
key_rows = 256


def block_split(count, limit):
    size_rows = math.gcd(count, limit)
    return (size_rows, count // size_rows)


def rope_tables(positions, heads):
    unit_pos = (2.0 * positions.astype(jnp.float32) + 1.0) / 16.0 - 1.0
    exponent = (
        jnp.arange(8, dtype=jnp.float32)[None, :] * heads
        + jnp.arange(heads, dtype=jnp.float32)[:, None]
    ) / (8.0 * heads)
    frequency = math.pi * 10.0**exponent
    angles = jnp.moveaxis(unit_pos[..., None, None] * frequency, -4, -2)
    return (jnp.cos(angles), jnp.sin(angles))


def rotate(vector, cosine, sine):
    leading = vector.shape[:-1]
    turned_part = vector[..., :32].reshape(leading + (2, 2, 8))
    first_half = turned_part[..., 0, :]
    second_half = turned_part[..., 1, :]
    turned = jnp.stack(
        [first_half * cosine - second_half * sine, first_half * sine + second_half * cosine],
        axis=-2,
    )
    return jnp.concatenate([turned.reshape(leading + (32,)), vector[..., 32:]], axis=-1)


def norm_forward(value, scale):
    inverse = lax.rsqrt(jnp.mean(value * value, axis=-1, keepdims=True) + eps_norm)
    return (value * inverse * scale[:, None], inverse)


def norm_backward(value, inverse, scale, grad_norm):
    scaled = grad_norm * scale[:, None]
    grad_value = inverse * scaled - value * inverse**3 * jnp.mean(
        scaled * value, axis=-1, keepdims=True
    )
    grad_scale = jnp.sum(grad_norm * value * inverse, axis=1)
    return (grad_value, grad_scale)


def cosine_forward(value, root_scale):
    factor = root_scale[:, None] * lax.rsqrt(
        jnp.sum(value * value, axis=-1, keepdims=True) + eps_cosine
    )
    return (value * factor, factor)


def cosine_backward(value, factor, grad):
    squares = jnp.sum(value * value, axis=-1, keepdims=True) + eps_cosine
    along = jnp.sum(grad * value, axis=-1, keepdims=True)
    grad_value = factor * grad - value * factor * along / squares
    return (grad_value, jnp.sum(along * factor, axis=(0, 1, 3)))


def geglu(value_part, gate_part):
    return value_part * jax.nn.gelu(gate_part, approximate=False)


def pair_grads(queries, grad_att, log_total, deltas, query_crop, key_block, value_block, key_crop):
    scores = jnp.einsum("cqhd,ckhd->cqhk", queries, key_block, preferred_element_type=jnp.float32)
    allowed = (query_crop[:, :, None] == key_crop[:, None, :])[:, :, None, :]
    probs = jnp.exp(jnp.where(allowed, scores - log_total[..., None], negative))
    probs = jnp.where(allowed, probs, 0.0)
    dotted = jnp.einsum(
        "cqhd,ckhd->cqhk", grad_att, value_block, preferred_element_type=jnp.float32
    )
    slope = (probs * (dotted - deltas[..., None])).astype(jnp.bfloat16)
    grad_q = jnp.einsum("cqhk,ckhd->cqhd", slope, key_block, preferred_element_type=jnp.float32)
    grad_k = jnp.einsum("cqhk,cqhd->ckhd", slope, queries, preferred_element_type=jnp.float32)
    grad_v = jnp.einsum(
        "cqhk,cqhd->ckhd", probs.astype(jnp.bfloat16), grad_att, preferred_element_type=jnp.float32
    )
    return (grad_q, grad_k, grad_v)


def pack_terms(terms, lead_shape):
    return jnp.concatenate([term.reshape(lead_shape + (-1,)) for term in terms], axis=-1)


def unpack_terms(packed_row, terms, owners):
    results = []
    offset = 0
    for term in terms:
        own_rows = term.shape[0] // owners
        count = own_rows * term.shape[1]
        results.append(packed_row[offset : offset + count].reshape(own_rows, term.shape[1]))
        offset = offset + count
    return results


def shards(
    block_in,
    conditioning,
    crop_ids,
    positions,
    qkv_weight,
    out_weight,
    up_weight,
    down_weight,
    attn_modulate,
    ffn_modulate,
    head_scale,
    cotangent,
):
    qkv_full, out_full, up_full, down_full, attn_mod, ffn_mod = (
        lax.all_gather(qkv_weight, ("dp", "seq"), axis=0, tiled=True),
        lax.all_gather(out_weight, ("dp", "seq"), axis=0, tiled=True),
        lax.all_gather(up_weight, ("dp", "seq"), axis=0, tiled=True),
        lax.all_gather(down_weight, ("dp", "seq"), axis=0, tiled=True),
        lax.all_gather(attn_modulate, ("dp", "seq"), axis=0, tiled=True),
        lax.all_gather(ffn_modulate, ("dp", "seq"), axis=0, tiled=True),
    )
    canvases, rows, width = block_in.shape
    heads = head_scale.shape[0]
    head_size = width // heads
    hidden_width = down_full.shape[0]
    seq_count = lax.axis_size("seq")
    inputs = block_in.astype(jnp.float32)
    scale_attn = 1.0 + jnp.dot(conditioning, attn_mod, preferred_element_type=jnp.float32)
    scale_ffn = 1.0 + jnp.dot(conditioning, ffn_mod, preferred_element_type=jnp.float32)
    normed_attn, inverse_attn = norm_forward(inputs, scale_attn)
    normed_attn = normed_attn.astype(jnp.bfloat16)
    qkv_all = jnp.einsum(
        "csd,de->cse", normed_attn, qkv_full, preferred_element_type=jnp.float32
    ).reshape(canvases, rows, 3, heads, head_size)
    root_scale = jnp.sqrt(head_scale)
    query_cos, query_factor = cosine_forward(qkv_all[:, :, 0], root_scale)
    key_cos, key_factor = cosine_forward(qkv_all[:, :, 1], root_scale)
    cosine, sine = rope_tables(positions, heads)
    queries = rotate(query_cos, cosine, sine).astype(jnp.bfloat16)
    keys_flat = rotate(key_cos, cosine, sine).astype(jnp.bfloat16).reshape(canvases, rows, width)
    values_flat = qkv_all[:, :, 2].astype(jnp.bfloat16).reshape(canvases, rows, width)
    start_state = (
        jnp.full((canvases, rows, heads), negative, jnp.float32),
        jnp.zeros((canvases, rows, heads), jnp.float32),
        jnp.zeros((canvases, rows, heads, head_size), jnp.float32),
    )
    state_now = start_state
    piece_keys = lax.all_gather(keys_flat, "seq", axis=1, tiled=True)
    piece_values = lax.all_gather(values_flat, "seq", axis=1, tiled=True)
    piece_crop = lax.all_gather(crop_ids, "seq", axis=1, tiled=True)
    size_rows, number = block_split(piece_keys.shape[1], key_rows)

    def step_block(state, block_index):
        running_max, row_total, weighted = state
        offset = block_index * size_rows
        key_block = lax.dynamic_slice_in_dim(piece_keys, offset, size_rows, 1).reshape(
            canvases, size_rows, heads, head_size
        )
        value_block = lax.dynamic_slice_in_dim(piece_values, offset, size_rows, 1).reshape(
            canvases, size_rows, heads, head_size
        )
        crop_block = lax.dynamic_slice_in_dim(piece_crop, offset, size_rows, 1)
        scores = jnp.einsum(
            "cqhd,ckhd->cqhk", queries, key_block, preferred_element_type=jnp.float32
        )
        allowed = (crop_ids[:, :, None] == crop_block[:, None, :])[:, :, None, :]
        scores = jnp.where(allowed, scores, negative)
        new_max = jnp.maximum(running_max, jnp.max(scores, axis=-1))
        weights = jnp.where(allowed, jnp.exp(scores - new_max[..., None]), 0.0)
        shrink = jnp.exp(running_max - new_max)
        row_total = row_total * shrink + jnp.sum(weights, axis=-1)
        weighted = weighted * shrink[..., None] + jnp.einsum(
            "cqhk,ckhd->cqhd",
            weights.astype(jnp.bfloat16),
            value_block,
            preferred_element_type=jnp.float32,
        )
        return ((new_max, row_total, weighted), None)

    state_now, unused = lax.scan(step_block, state_now, jnp.arange(number))
    running_max, row_total, weighted = state_now
    log_total = running_max + jnp.log(row_total)
    attended_raw = weighted / row_total[..., None]
    attended = attended_raw.astype(jnp.bfloat16).reshape(canvases, rows, width)
    middle = inputs + jnp.einsum(
        "csd,de->cse", attended, out_full, preferred_element_type=jnp.float32
    )
    normed_ffn, inverse_ffn = norm_forward(middle, scale_ffn)
    normed_ffn = normed_ffn.astype(jnp.bfloat16)
    up_all = jnp.einsum("csd,de->cse", normed_ffn, up_full, preferred_element_type=jnp.float32)
    value_part = up_all[..., :hidden_width]
    gate_part = up_all[..., hidden_width:]
    hidden = geglu(value_part, gate_part).astype(jnp.bfloat16)
    block_out = (
        middle + jnp.einsum("csf,fd->csd", hidden, down_full, preferred_element_type=jnp.float32)
    ).astype(jnp.bfloat16)
    down_term = jnp.einsum("csf,csd->fd", hidden, cotangent, preferred_element_type=jnp.float32)
    grad_hidden = jnp.einsum(
        "csd,fd->csf", cotangent, down_full, preferred_element_type=jnp.float32
    )
    unused_value, geglu_pull = jax.vjp(geglu, value_part, gate_part)
    grad_value, grad_gate = geglu_pull(grad_hidden)
    grad_up = jnp.concatenate([grad_value, grad_gate], axis=-1).astype(jnp.bfloat16)
    up_term = jnp.einsum("csd,cse->de", normed_ffn, grad_up, preferred_element_type=jnp.float32)
    grad_normed_ffn = jnp.einsum(
        "cse,de->csd", grad_up, up_full, preferred_element_type=jnp.float32
    )
    grad_mid_norm, ffn_scale_sum = norm_backward(middle, inverse_ffn, scale_ffn, grad_normed_ffn)
    grad_middle = cotangent.astype(jnp.float32) + grad_mid_norm
    grad_branch = grad_middle.astype(jnp.bfloat16)
    out_term = jnp.einsum("csd,cse->de", attended, grad_branch, preferred_element_type=jnp.float32)
    grad_attended = (
        jnp.einsum("cse,de->csd", grad_branch, out_full, preferred_element_type=jnp.float32)
        .astype(jnp.bfloat16)
        .reshape(canvases, rows, heads, head_size)
    )
    deltas = jnp.sum(grad_attended.astype(jnp.float32) * attended_raw, axis=-1)
    start_back = (
        jnp.zeros((canvases, rows, heads, head_size), jnp.float32),
        jnp.zeros((canvases, rows * seq_count, 2 * width), jnp.float32),
    )
    state_now = start_back
    fold_piece_keys = lax.all_gather(keys_flat, "seq", axis=1, tiled=True)
    fold_piece_values = lax.all_gather(values_flat, "seq", axis=1, tiled=True)
    fold_piece_crop = lax.all_gather(crop_ids, "seq", axis=1, tiled=True)
    fold_size_rows, number = block_split(fold_piece_keys.shape[1], key_rows)

    def step_block(state, block_index):
        grad_q_sum, grad_kv_all = state
        offset = block_index * fold_size_rows
        key_block = lax.dynamic_slice_in_dim(fold_piece_keys, offset, fold_size_rows, 1).reshape(
            canvases, fold_size_rows, heads, head_size
        )
        value_block = lax.dynamic_slice_in_dim(
            fold_piece_values, offset, fold_size_rows, 1
        ).reshape(canvases, fold_size_rows, heads, head_size)
        crop_block = lax.dynamic_slice_in_dim(fold_piece_crop, offset, fold_size_rows, 1)
        grad_q, grad_k, grad_v = pair_grads(
            queries, grad_attended, log_total, deltas, crop_ids, key_block, value_block, crop_block
        )
        update = jnp.concatenate(
            [
                grad_k.reshape(canvases, fold_size_rows, width),
                grad_v.reshape(canvases, fold_size_rows, width),
            ],
            axis=-1,
        )
        previous = lax.dynamic_slice_in_dim(grad_kv_all, offset, fold_size_rows, 1)
        grad_kv_all = lax.dynamic_update_slice_in_dim(grad_kv_all, previous + update, offset, 1)
        return ((grad_q_sum + grad_q, grad_kv_all), None)

    state_now, unused = lax.scan(step_block, state_now, jnp.arange(number))
    grad_queries, grad_kv_all = state_now
    grad_kv = lax.psum_scatter(
        grad_kv_all.astype(jnp.bfloat16), "seq", scatter_dimension=1, tiled=True
    ).astype(jnp.float32)
    grad_keys = grad_kv[..., :width].reshape(canvases, rows, heads, head_size)
    grad_values = grad_kv[..., width:].reshape(canvases, rows, heads, head_size)
    grad_query_cos = rotate(grad_queries, cosine, -sine)
    grad_key_cos = rotate(grad_keys, cosine, -sine)
    grad_query_raw, query_part = cosine_backward(qkv_all[:, :, 0], query_factor, grad_query_cos)
    grad_key_raw, key_part = cosine_backward(qkv_all[:, :, 1], key_factor, grad_key_cos)
    scale_local = (query_part + key_part) / (2.0 * head_scale)
    grad_qkv = (
        jnp.stack([grad_query_raw, grad_key_raw, grad_values], axis=2)
        .astype(jnp.bfloat16)
        .reshape(canvases, rows, 3 * width)
    )
    qkv_term = jnp.einsum("csd,cse->de", normed_attn, grad_qkv, preferred_element_type=jnp.float32)
    grad_normed_attn = jnp.einsum(
        "cse,de->csd", grad_qkv, qkv_full, preferred_element_type=jnp.float32
    )
    grad_in_norm, attn_scale_sum = norm_backward(inputs, inverse_attn, scale_attn, grad_normed_attn)
    input_grad = grad_middle + grad_in_norm
    attn_sums, ffn_sums = lax.psum((attn_scale_sum, ffn_scale_sum), "seq")
    attn_sums = attn_sums.astype(jnp.bfloat16)
    ffn_sums = ffn_sums.astype(jnp.bfloat16)
    cond_grad = jnp.einsum(
        "cd,nd->cn", attn_sums, attn_mod, preferred_element_type=jnp.float32
    ) + jnp.einsum("cd,nd->cn", ffn_sums, ffn_mod, preferred_element_type=jnp.float32)
    leader = lax.axis_index("seq") == 0
    attn_mod_term = jnp.where(
        leader,
        jnp.einsum("cn,cd->nd", conditioning, attn_sums, preferred_element_type=jnp.float32),
        0.0,
    )
    ffn_mod_term = jnp.where(
        leader,
        jnp.einsum("cn,cd->nd", conditioning, ffn_sums, preferred_element_type=jnp.float32),
        0.0,
    )
    terms = (qkv_term, out_term, up_term, down_term, attn_mod_term, ffn_mod_term)
    groups = lax.axis_size("dp")
    owners = groups * seq_count
    packed = pack_terms(terms, (owners,))
    summed = lax.psum_scatter(packed, ("dp", "seq"), scatter_dimension=0, tiled=True)
    packed_row = summed[0]
    qkv_grad, out_grad, up_grad, down_grad, attnmod_grad, ffnmod_grad = unpack_terms(
        packed_row, terms, owners
    )
    scale_grad = lax.psum(scale_local, ("dp", "seq"))
    return (
        block_out,
        input_grad,
        cond_grad,
        qkv_grad,
        out_grad,
        up_grad,
        down_grad,
        attnmod_grad,
        ffnmod_grad,
        scale_grad,
    )


MESH = pl.DeviceIdType.MESH
BF = jnp.bfloat16
F32 = jnp.float32
PLANE = ((1, 0, 0), (0, 0, 1), (1, 0, 1), (0, 1, 0), (1, 1, 0), (0, 1, 1), (1, 1, 1))
TO_X, TO_Y, TO_FAR = (1, 0, 0), (0, 0, 1), (1, 0, 1)
ERF_P = (
    0.00022905065861350646,
    0.0034082910107109506,
    0.050955695062380861,
    0.18520832239976145,
    1.128379143519084,
)
ERF_Q = (
    -1.1791602954361697e-7,
    0.000023547966471313185,
    0.0010179625278914885,
    0.014070470171167667,
    0.11098505178285362,
    0.49746925110067538,
    1.0,
)


def erf(value):
    value = jnp.clip(value, -3.832506856900711, 3.832506856900711)
    square = value * value
    top = jnp.full_like(value, ERF_P[0])
    for term in ERF_P[1:]:
        top = top * square + term
    bottom = jnp.full_like(value, ERF_Q[0])
    for term in ERF_Q[1:]:
        bottom = bottom * square + term
    return value * top / bottom


def dot(lhs, rhs, on_lhs=1, on_rhs=0):
    return lax.dot_general(
        lhs, rhs, (((on_lhs,), (on_rhs,)), ((), ())), preferred_element_type=F32
    )


def block_kernel(
    lines,
    x_ref,
    cot_ref,
    qkv_ref,
    up_ref,
    out_ref,
    down_ref,
    amod_ref,
    fmod_ref,
    cond_ref,
    crop_ref,
    pos_ref,
    scale_ref,
    table_ref,
    block_out,
    input_grad,
    cond_grad,
    qkv_grad,
    out_grad,
    up_grad,
    down_grad,
    amod_grad,
    fmod_grad,
    scale_grad,
    *scratch,
):
    names = list(scratch_plan(lines, x_ref, qkv_ref, up_ref, out_ref, down_ref))
    s = types.SimpleNamespace(**dict(zip(names, scratch)))
    dp = lax.axis_index("dp")
    y = lax.axis_index("seq")
    z = dp // 4
    x = (dp // 2) % 2
    c = dp % 2
    rows, width = x_ref.shape
    up_rows = up_ref.shape[0]
    own_cols = qkv_ref.shape[1] // 8
    lanes = own_cols // 3
    half_head = out_ref.shape[0]
    hidden = up_ref.shape[1] // 16
    down_rows = down_ref.shape[0]
    mod_rows = amod_ref.shape[0]
    canvas_rows = 2 * rows
    crops = canvas_rows // 16
    me = 4 * x + 2 * c + y
    device_index = 8 * z + me

    def member(step):
        return 4 * ((x + step[0]) % 2) + 2 * ((c + step[1]) % 2) + (y + step[2]) % 2

    def device(step, along=0):
        return (
            ((z + along) % lines) * 4 + ((x + step[0]) % 2) * 2 + (c + step[1]) % 2,
            (y + step[2]) % 2,
        )

    def line_device(along):
        return (jnp.clip(z + along, 0, lines - 1) * 4 + dp % 4, y)

    def inside(along):
        return z + along < lines if along > 0 else z + along >= 0

    here = (0, 0, 0)
    core = (0, 1, 0)
    sends = []

    class Copy:
        def __init__(self, src, dst_there, dst_here, sems, at, target):
            self.out = pltpu.make_async_remote_copy(
                src_ref=src,
                dst_ref=dst_there,
                send_sem=sems.at[0, at],
                recv_sem=sems.at[1, at],
                device_id=target,
                device_id_type=MESH,
            )
            self.into = pltpu.make_async_remote_copy(
                src_ref=src,
                dst_ref=dst_here,
                send_sem=sems.at[0, at],
                recv_sem=sems.at[1, at],
                device_id=target,
                device_id_type=MESH,
            )

        def start(self, when=None):
            if when is None:
                self.out.start()
            else:
                pl.when(when)(self.out.start)
            sends.append((self.out, when))

        def arrive(self):
            self.into.wait_recv()

    class Gather:
        def __init__(self, buffer, sems):
            at = lambda step: buffer.at[member(step)]
            half = buffer.shape[1] // 2
            rows_of = (pl.ds(0, half), pl.ds(half, half))
            part = lambda step, k: buffer.at[member(step), rows_of[k]]
            self.x_own = [
                Copy(part(here, k), part(here, k), part(TO_X, k), sems, k, device(TO_X))
                for k in range(2)
            ]
            self.y_own = [
                Copy(part(here, k), part(here, k), part(TO_Y, k), sems, 2 + k, device(TO_Y))
                for k in range(2)
            ]
            self.y_far = Copy(part(TO_X, 0), part(TO_X, 0), part(TO_FAR, 0), sems, 4, device(TO_Y))
            self.x_far = Copy(part(TO_Y, 1), part(TO_Y, 1), part(TO_FAR, 1), sems, 5, device(TO_X))
            self.pair = Copy(at(here), at(here), at(core), sems, 6, device(core))
            self.cross = [
                Copy(at(step), at(step), at((step[0], 1, step[2])), sems, 7 + k, device(core))
                for k, step in enumerate((TO_X, TO_Y, TO_FAR))
            ]

        def start(self):
            self.x_own[0].start()
            self.y_own[1].start()
            self.x_own[1].start()
            self.y_own[0].start()
            self.pair.start()

        def turn(self):
            self.x_own[0].arrive()
            self.y_far.start()
            self.y_own[1].arrive()
            self.x_far.start()

        def near(self):
            self.y_own[0].arrive()
            self.cross[1].start()
            self.x_own[1].arrive()
            self.cross[0].start()

        def far(self):
            self.y_far.arrive()
            self.x_far.arrive()
            self.cross[2].start()

        def pair_near(self):
            self.pair.arrive()
            self.cross[1].arrive()

        def pair_far(self):
            self.cross[0].arrive()
            self.cross[2].arrive()

        def finish(self):
            self.near()
            self.far()
            self.pair_near()
            self.pair_far()

        def steps(self):
            return {0: self.near, 1: self.pair_near, 2: self.far, 3: self.pair_far}

    class Reduce:
        def __init__(self, part, pair_in, far_in, chip_in, sems):
            self.part, self.pair_in, self.far_in, self.chip_in = part, pair_in, far_in, chip_in
            half = part.shape[1] // 2
            self.rows_of = rows_of = (pl.ds(0, half), pl.ds(half, half))
            self.steps_of = (here, TO_X, TO_Y, TO_FAR)
            self.pair = [
                Copy(
                    part.at[member((step[0], 1, step[2]))],
                    pair_in.at[k],
                    pair_in.at[k],
                    sems,
                    k,
                    device(core),
                )
                for k, step in enumerate(self.steps_of)
            ]
            piece = lambda step, k: part.at[member(step), rows_of[k]]
            self.x_far = Copy(piece(TO_FAR, 0), far_in.at[0], far_in.at[0], sems, 4, device(TO_X))
            self.y_far = Copy(piece(TO_FAR, 1), far_in.at[1], far_in.at[1], sems, 5, device(TO_Y))
            into = lambda way, k: chip_in.at[way, rows_of[k]]
            self.x_own = [
                Copy(piece(TO_X, k), into(0, k), into(0, k), sems, 6 + k, device(TO_X))
                for k in range(2)
            ]
            self.y_own = [
                Copy(piece(TO_Y, k), into(1, k), into(1, k), sems, 8 + k, device(TO_Y))
                for k in range(2)
            ]

        def add_pair(self, k):
            self.pair[k].arrive()
            slot = member(self.steps_of[k])
            total = self.part[slot].astype(F32) + self.pair_in[k].astype(F32)
            self.part[slot] = total.astype(BF)

        def add_far(self, step, k):
            slot = member(step)
            total = self.part[slot, self.rows_of[k], :].astype(F32) + self.far_in[k].astype(F32)
            self.part[slot, self.rows_of[k], :] = total.astype(BF)

        def give_far(self):
            self.pair[3].start()
            self.pair[1].start()

        def send_far(self):
            self.add_pair(3)
            self.x_far.start()
            self.y_far.start()
            self.add_pair(1)
            self.x_own[0].start()

        def give_near(self):
            self.pair[2].start()
            self.pair[0].start()

        def send_near(self):
            self.add_pair(2)
            self.y_own[1].start()

        def steps(self):
            return {0: self.give_far, 1: self.send_far, 2: self.give_near, 3: self.send_near}

        def middle(self):
            self.x_far.arrive()
            self.add_far(TO_Y, 0)
            self.y_own[0].start()
            self.y_far.arrive()
            self.add_far(TO_X, 1)
            self.x_own[1].start()

        def finish(self):
            self.pair[0].arrive()
            total = self.part[me].astype(F32) + self.pair_in[0].astype(F32)
            for copies in (self.x_own, self.y_own):
                for copy in copies:
                    copy.arrive()
            return total + self.chip_in[0].astype(F32) + self.chip_in[1].astype(F32)

    class Spread:
        def __init__(self, source, target, sems):
            self.source, self.target = source, target
            self.copies = [
                Copy(
                    source.at[member(step)],
                    target.at[me],
                    target.at[member(step)],
                    sems,
                    k,
                    device(step),
                )
                for k, step in enumerate(PLANE)
            ]

        def start(self):
            for copy in self.copies:
                copy.start()
            self.target[me] = self.source[me]

        def finish(self):
            for copy in self.copies:
                copy.arrive()

    class Share:
        def __init__(self, buffer, sems, block=None):
            self.copies = [
                Copy(
                    buffer.at[me] if block is None else block,
                    buffer.at[me],
                    buffer.at[member(step)],
                    sems,
                    k,
                    device(step),
                )
                for k, step in enumerate(PLANE)
            ]

        def start(self):
            for copy in self.copies:
                copy.start()

        def finish(self):
            for copy in self.copies:
                copy.arrive()

    class Line:
        def __init__(self, buffer, sems, first=None):
            self.copies = []
            for along in range(1, lines):
                back = (z + lines - along) % lines
                if first is None:
                    mine, theirs = buffer.at[z], buffer.at[back]
                else:
                    mine, theirs = buffer.at[pl.ds(first * z, first)], buffer.at[pl.ds(first * back, first)]
                self.copies.append(Copy(mine, mine, theirs, sems, along - 1, device(here, along)))

        def start(self):
            for copy in self.copies:
                copy.start()

        def finish(self):
            for copy in self.copies:
                copy.arrive()

    class Relay:
        def __init__(self, buffer, sems):
            self.copies = {
                along: Copy(
                    buffer.at[z],
                    buffer.at[z],
                    buffer.at[jnp.clip(z - along, 0, lines - 1)],
                    sems,
                    at,
                    line_device(along),
                )
                for at, along in enumerate((1, -1, 2, -2))
            }
            self.onward = {
                along: Copy(
                    buffer.at[far], buffer.at[far], buffer.at[far], sems, 4, line_device(along)
                )
                for along, far in ((1, 0), (-1, lines - 1))
            }

        def start(self):
            for along in (2, -2, 1, -1):
                self.copies[along].start(inside(along))

        def middle(self):
            @pl.when(z == 2)
            def up_line():
                self.copies[2].arrive()

            @pl.when(z == 1)
            def down_line():
                self.copies[-2].arrive()

            self.onward[1].start(z == 2)
            self.onward[-1].start(z == 1)

        def finish(self):
            pl.when(z >= 1)(self.copies[1].arrive)
            pl.when(z <= 2)(self.copies[-1].arrive)
            pl.when(z == 3)(self.copies[2].arrive)
            pl.when(z == 0)(self.copies[-2].arrive)
            pl.when(z == 3)(self.onward[1].arrive)
            pl.when(z == 0)(self.onward[-1].arrive)

    class Fold:
        def __init__(self, terms, landed, sems):
            self.terms, self.landed = terms, landed
            self.copies = {
                along: Copy(
                    terms.at[jnp.clip(z + along, 0, lines - 1)],
                    landed.at[min(at, 2)],
                    landed.at[min(at, 2)],
                    sems,
                    at,
                    line_device(along),
                )
                for at, along in enumerate((1, -1, 2, -2))
            }
            self.first = {
                along: Copy(
                    terms.at[far], landed.at[3], landed.at[3], sems, 4, line_device(along)
                )
                for along, far in ((1, lines - 1), (-1, 0))
            }

        def start(self):
            self.first[1].start(z == 0)
            self.first[-1].start(z == lines - 1)
            self.copies[2].start(z == 0)
            self.copies[-2].start(z == lines - 1)
            for along in (1, -1):
                self.copies[along].start(inside(along))

        def middle(self):
            for at, far, along in ((1, lines - 1, 1), (2, 0, -1)):

                @pl.when(z == at)
                def join():
                    self.first[along].arrive()
                    total = self.terms[far].astype(F32) + self.landed[3].astype(F32)
                    self.terms[far] = total.astype(BF)

                self.copies[2 * along].start(z == at)

        def finish(self, total):
            total[...] = self.terms[z].astype(F32)
            for at, (along, when) in enumerate(((1, z >= 1), (-1, z <= 2), (2, z >= 2), (-2, z <= 1))):

                @pl.when(when)
                def add():
                    self.copies[along].arrive()
                    total[...] += self.landed[min(at, 2)].astype(F32)

            return total[...]

    class Canvases:
        def __init__(self, buffer, sems):
            self.near = [
                Copy(
                    buffer.at[dp],
                    buffer.at[dp],
                    buffer.at[device(step)[0]],
                    sems,
                    k,
                    device(step),
                )
                for k, step in enumerate(((1, 0, 0), (0, 1, 0), (1, 1, 0)))
            ]
            self.far = []
            for along in range(1, lines):
                back = (z + lines - along) % lines
                mine = buffer.at[pl.ds(4 * z, 4)]
                self.far.append(
                    Copy(
                        mine,
                        mine,
                        buffer.at[pl.ds(4 * back, 4)],
                        sems,
                        2 + along,
                        device(here, along),
                    )
                )

        def start(self):
            for copy in self.near:
                copy.start()

        def middle(self):
            for copy in self.near:
                copy.arrive()
            for copy in self.far:
                copy.start()

        def finish(self):
            for copy in self.far:
                copy.arrive()

    def each_canvas(body, near=True, before=None, after=None):
        def step(t, carry):
            for k, action in (before or {}).items():
                pl.when(t == k)(action)
            turn = t if near else 3 - t
            body(2 * ((x + (turn // 2)) % 2) + (c + turn) % 2)
            for k, action in (after or {}).items():
                pl.when(t == k)(action)
            return carry

        lax.fori_loop(0, 4, step, 0)

    def slots(t):
        return pl.ds(2 * t, 2)

    lane = lax.broadcasted_iota(jnp.int32, (1, lanes), 1)
    first_head = lane < lanes // 2
    first_part = (lane % 16) < 8

    def per_head(pair):
        return jnp.where(first_head, pair[0], pair[1])

    def head_sums(value):
        left = jnp.where(first_head, value, 0.0)
        right = jnp.where(first_head, 0.0, value)
        return (
            jnp.sum(left, axis=-1, keepdims=True),
            jnp.sum(right, axis=-1, keepdims=True),
        )

    def partner(value):
        return jnp.where(
            first_part, pltpu.roll(value, lanes - 8, 1), pltpu.roll(value, 8, 1)
        )

    barrier = pltpu.get_barrier_semaphore()
    partners = [device(step) for step in PLANE] + [device(here, k) for k in range(1, lines)]
    for target in partners:
        pl.semaphore_signal(barrier, inc=1, device_id=target, device_id_type=MESH)
    ids = s.ids
    ids[me] = jnp.zeros(ids.shape[1:], jnp.int32)
    ids[me, 0:1, :] = crop_ref[...]
    ids[me, 1:3, :] = pos_ref[0]
    conds = s.conds
    conds[dp] = jnp.zeros(conds.shape[1:], F32)
    for r in range(cond_ref.shape[1] // 128):
        conds[dp, r : r + 1, :] = cond_ref[:, 128 * r : 128 * (r + 1)].astype(F32)
    s.tokens[me] = x_ref[...]
    s.cots[me] = cot_ref[...]
    s.out_line[z] = out_ref[...]
    s.down_line[z] = down_ref[...]
    mod_full = s.mod_full
    mod_full[...] = jnp.zeros(mod_full.shape, BF)
    mod_full[0:mod_rows, 0:width] = amod_ref[...]
    mod_full[0:mod_rows, width : 2 * width] = fmod_ref[...]

    size = lanes // 2
    qkv_places = [
        (m, (2 * part + k) * size, part * width + (8 * (m % 2) + 4 * k + m // 2) * size)
        for m in range(8)
        for part in range(3)
        for k in range(2)
    ]
    up_places = [
        (m, (lines * part + k) * down_rows, part * 8 * hidden + (8 * k + m) * down_rows)
        for m in range(8)
        for part in range(2)
        for k in range(lines)
    ]
    for m, own, whole in qkv_places:
        s.qkv_cols[m, :, own : own + size] = qkv_ref[:, whole : whole + size]
    for m, own, whole in up_places:
        s.up_cols[m, :, own : own + down_rows] = up_ref[:, whole : whole + down_rows]
    pl.semaphore_wait(barrier, len(partners))

    cond_copy = Canvases(conds, s.sem_cond)
    ids_copy = Share(ids, s.sem_ids)
    qkv_spread = Spread(s.qkv_cols, s.qkv_line.at[z], s.sem_qkv_spread)
    up_spread = Spread(s.up_cols, s.up_line.at[z], s.sem_up_spread)
    qkv_line = Relay(s.qkv_line, s.sem_qkv_line)
    out_line = Relay(s.out_line, s.sem_out_line)
    up_line = Relay(s.up_line, s.sem_up_line)
    down_line = Relay(s.down_line, s.sem_down_line)
    token_copy = Gather(s.tokens, s.sem_tokens)
    cot_copy = Gather(s.cots, s.sem_cots)
    cond_copy.start()
    qkv_spread.start()
    cond_copy.middle()
    out_line.start()
    qkv_spread.finish()
    qkv_line.start()
    cond_copy.finish()
    picked = jnp.zeros((conds.shape[0], 128), F32)
    for r in range(cond_ref.shape[1] // 128):
        at_row = lax.broadcasted_iota(jnp.int32, (128, 128), 0) + 128 * r
        at_col = lax.broadcasted_iota(jnp.int32, (128, 128), 1)
        choose = (at_row == at_col + mod_rows * device_index) & (at_col < mod_rows)
        picked = picked + dot(
            conds[:, r, :].astype(BF), jnp.where(choose, 1.0, 0.0).astype(BF)
        )
    cond_mine = picked.astype(BF)
    block_cols = 2 * width // 8
    mod_terms, mod_in = s.mod_terms, s.mod_in
    for m in range(8):
        mod_terms[m] = dot(cond_mine, mod_full[:, block_cols * m : block_cols * (m + 1)])
    mod_spread = Spread(mod_terms, mod_in, s.sem_mod_spread)
    mod_spread.start()
    token_copy.start()
    mod_spread.finish()
    mod_sum = mod_in[0]
    for m in range(1, 8):
        mod_sum = mod_sum + mod_in[m]
    mod_line = s.mod_line
    mod_line[z] = mod_sum
    mod_copy = Line(mod_line, s.sem_mod_line)
    mod_copy.start()
    token_copy.turn()
    out_line.middle()
    mod_copy.finish()
    mod_sum = mod_line[0]
    for k in range(1, lines):
        mod_sum = mod_sum + mod_line[k]
    s.mod_total[...] = 1.0 + mod_sum
    mod_share = Share(s.mods, s.sem_mods)
    own_rows = s.mod_total[pl.ds(8 * (z // 2), 8), :]
    s.mods[me] = own_rows
    mod_share.start()
    up_spread.start()
    ids_copy.start()
    cot_copy.start()
    mod_share.finish()
    scales = s.scales
    for m in range(8):
        scales[:, block_cols * m : block_cols * (m + 1)] = s.mods[m]

    def scale_row(canvas, ffn):
        row = scales[pl.ds(4 * (z % 2) + canvas, 1), :]
        return row[:, width:] if ffn else row[:, :width]

    own_canvas = 2 * x + c

    def inverse_rms(value):
        return lax.rsqrt(jnp.mean(value * value, axis=-1, keepdims=True) + eps_norm)

    normed = s.normed

    def norm_tokens(canvas):
        value = s.tokens[slots(canvas)].reshape(canvas_rows, width).astype(F32)
        scaled = value * inverse_rms(value) * scale_row(canvas, False)
        normed[slots(canvas)] = scaled.astype(BF).reshape(2, rows, width)

    each_canvas(norm_tokens, before=token_copy.steps())
    qkv_line.middle()
    up_spread.finish()
    up_line.start()
    down_line.start()
    out_line.finish()
    out_half = s.out_half
    half_copy = Copy(
        s.out_line.at[pl.ds(2 * (1 - y), 2)],
        out_half,
        out_half,
        s.sem_half,
        0,
        device((0, 0, 1)),
    )
    half_copy.start()
    cot_copy.turn()
    ids_copy.finish()
    qkv_line.finish()
    head_of = lambda k: 8 * y + 4 * k + 2 * x + c
    head_scales = [scale_ref[head_of(k)] for k in range(2)]
    scale_lanes = per_head(head_scales)
    root_lanes = jnp.sqrt(scale_lanes)

    def canvas_ids(canvas, row):
        return jnp.concatenate(
            [ids[2 * canvas, row : row + 1, :], ids[2 * canvas + 1, row : row + 1, :]], axis=1
        )

    def one_hot(row, count):
        return jnp.where(
            lax.broadcasted_iota(jnp.int32, (count, canvas_rows), 0) == row, 1.0, 0.0
        ).astype(BF)

    def attend(canvas):
        qkv = dot(
            normed[slots(canvas)].reshape(canvas_rows, width),
            s.qkv_line[...].reshape(width, own_cols),
        )
        places = [one_hot(canvas_ids(canvas, 1), 16), one_hot(canvas_ids(canvas, 2), 16)]
        turn = dot(jnp.concatenate(places + places, axis=0), table_ref[me], 0, 0)
        s.turns[canvas] = turn
        cosine, sine = turn[:, :lanes], turn[:, lanes:]
        rotated = []
        for part in range(2):
            raw = qkv[:, part * lanes : (part + 1) * lanes]
            s.raw[canvas, part] = raw
            sums = head_sums(raw * raw)
            factor = per_head([lax.rsqrt(value + eps_cosine) for value in sums]) * root_lanes
            turned = raw * factor
            turned = (turned * cosine + partner(turned) * sine).astype(BF)
            s.rotated[canvas, part] = turned
            rotated.append(turned)
        values = qkv[:, 2 * lanes :].astype(BF)
        s.rotated[canvas, 2] = values
        crop_hot = one_hot(canvas_ids(canvas, 0), crops)
        allowed = dot(crop_hot, crop_hot, 0, 0)
        heads = []
        for k in range(2):
            mine = first_head if k == 0 else jnp.logical_not(first_head)
            query = jnp.where(mine, rotated[0], jnp.zeros_like(rotated[0]))
            weights = jnp.exp(dot(query, rotated[1], 1, 1)) * allowed
            probs = weights / jnp.sum(weights, axis=-1, keepdims=True)
            s.probs[canvas, k] = probs
            heads.append(dot(probs.astype(BF), values))
        attended = per_head(heads)
        s.raw_attended[canvas] = attended
        s.attended[canvas] = attended.astype(BF)

    each_canvas(attend)
    half_copy.arrive()
    out_full = s.out_full
    for k in range(2):
        out_full[k, y] = s.out_line[2 * y + k]
        out_full[k, 1 - y] = out_half[k]

    def to_middle(canvas):
        value = dot(s.attended[canvas], out_full[...].reshape(lanes, width))
        s.mid_part[slots(canvas)] = value.astype(BF).reshape(2, rows, width)

    mid_reduce = Reduce(
        s.mid_part, s.mid_pair, s.mid_far, s.mid_chip, s.sem_mid
    )
    each_canvas(to_middle, False, after=mid_reduce.steps())
    mid_reduce.middle()
    cot_copy.finish()
    up_line.middle()
    middle = x_ref[...].astype(F32) + mid_reduce.finish()
    s.middle[...] = middle
    ffn_row = scale_row(own_canvas, True)
    s.ffn[me] = (middle * inverse_rms(middle) * ffn_row).astype(BF)
    ffn_copy = Gather(s.ffn, s.sem_ffn)
    ffn_copy.start()
    ffn_copy.turn()
    up_line.finish()

    def feed(canvas):
        up = dot(
            s.ffn[slots(canvas)].reshape(canvas_rows, width),
            s.up_line[...].reshape(width, 2 * hidden),
        )
        value, gate = up[:, :hidden], up[:, hidden:]
        cdf = 0.5 + 0.5 * erf(gate * math.sqrt(0.5))
        act = gate * cdf
        s.hidden[canvas] = (value * act).astype(BF)
        s.act[canvas] = act
        density = jnp.exp(-0.5 * gate * gate) * (1.0 / math.sqrt(2.0 * math.pi))
        s.slope[canvas] = value * (cdf + gate * density)

    each_canvas(feed, before=ffn_copy.steps())
    down_line.middle()

    def cots_of(canvas):
        return s.cots[slots(canvas)].reshape(canvas_rows, width)

    all_rows = 8 * rows
    chunk = 256

    def down_term(n, carry):
        cols = pl.ds(pl.multiple_of(n * chunk, chunk), chunk)
        term = dot(
            s.hidden[...].reshape(all_rows, hidden),
            s.cots[:, :, cols].reshape(all_rows, chunk),
            0,
            0,
        )
        s.down_term[:, :, cols] = term.astype(BF).reshape(lines, down_rows, chunk)
        return carry

    lax.fori_loop(0, width // chunk, down_term, 0)
    down_fold = Fold(s.down_term, s.down_in, s.sem_down_fold)
    down_fold.start()
    down_line.finish()

    def feed_back(canvas):
        grad_hidden = dot(cots_of(canvas), s.down_line[...].reshape(hidden, width), 1, 1)
        grad_up = jnp.concatenate(
            [grad_hidden * s.act[canvas], grad_hidden * s.slope[canvas]], axis=1
        ).astype(BF)
        s.grad_up[canvas] = grad_up
        part = dot(grad_up, s.up_line[...].reshape(width, 2 * hidden), 1, 1)
        s.gnf_part[slots(canvas)] = part.astype(BF).reshape(2, rows, width)

    gnf_reduce = Reduce(
        s.gnf_part, s.gnf_pair, s.gnf_far, s.gnf_chip, s.sem_gnf
    )
    each_canvas(feed_back, False, after=gnf_reduce.steps())
    gnf_reduce.middle()

    def up_term(k, carry):
        cols = pl.ds(pl.multiple_of(k * 8 * up_rows, 8 * up_rows), 8 * up_rows)
        term = dot(
            s.ffn[:, :, cols].reshape(all_rows, 8 * up_rows),
            s.grad_up[...].reshape(all_rows, 2 * hidden),
            0,
            0,
        )
        s.up_term[k] = term.astype(BF).reshape(8, up_rows, 2 * hidden)
        return carry

    lax.fori_loop(0, lines, up_term, 0)
    up_fold = Fold(s.up_term, s.up_in, s.sem_up_fold)
    up_fold.start()
    down_fold.middle()

    def norm_back(value, row, grad):
        inverse = inverse_rms(value)
        scaled = grad * row
        along = jnp.mean(scaled * value, axis=-1, keepdims=True)
        grad_value = inverse * scaled - value * (inverse * inverse * inverse) * along
        return grad_value, jnp.sum(grad * value * inverse, axis=0, keepdims=True)

    def put_row(target, offset, row):
        for r in range(width // 128):
            target[offset + r : offset + r + 1, :] = row[:, 128 * r : 128 * (r + 1)]

    grad_mid, ffn_sum = norm_back(s.middle[...], ffn_row, gnf_reduce.finish())
    grad_middle = cot_ref[...].astype(F32) + grad_mid
    s.grad_middle[...] = grad_middle
    s.branch[me] = grad_middle.astype(BF)
    branch_copy = Gather(s.branch, s.sem_branch)
    branch_copy.start()
    sums_own = s.sums_own
    put_row(sums_own, 8, ffn_sum)

    def to_out(canvas):
        part = dot(s.hidden[canvas], s.down_line[...].reshape(hidden, width))
        s.out_part[slots(canvas)] = part.astype(BF).reshape(2, rows, width)

    out_reduce = Reduce(
        s.out_part, s.out_pair, s.out_far, s.out_chip, s.sem_out
    )
    branch_copy.turn()
    each_canvas(to_out)
    up_fold.middle()
    branch_copy.finish()
    out_reduce.give_far()
    out_reduce.give_near()

    def attend_back(canvas):
        branch = s.branch[slots(canvas)].reshape(canvas_rows, width)
        grad_att = dot(branch, out_full[...].reshape(lanes, width), 1, 1).astype(BF)
        turn = s.turns[canvas]
        cosine, sine = turn[:, :lanes], turn[:, lanes:]
        query, key, values = (s.rotated[canvas, part] for part in range(3))
        deltas = head_sums(grad_att.astype(F32) * s.raw_attended[canvas])
        grads = [[], [], []]
        for k in range(2):
            mine = first_head if k == 0 else jnp.logical_not(first_head)
            probs = s.probs[canvas, k]
            one_head = jnp.where(mine, grad_att, jnp.zeros_like(grad_att))
            dotted = dot(one_head, values, 1, 1)
            slope = (probs * (dotted - deltas[k])).astype(BF)
            grads[0].append(dot(slope, key))
            grads[1].append(dot(slope, query, 0, 0))
            grads[2].append(dot(probs.astype(BF), grad_att, 0, 0))
        pieces = []
        for part in range(2):
            grad = per_head(grads[part])
            grad = grad * cosine - partner(grad) * sine
            raw = s.raw[canvas, part]
            squares = [value + eps_cosine for value in head_sums(raw * raw)]
            along = head_sums(grad * raw)
            inverse = [lax.rsqrt(value) for value in squares]
            factor = per_head(inverse) * root_lanes
            shrink = per_head([along[k] * inverse[k] * inverse[k] for k in range(2)])
            pieces.append(factor * grad - raw * factor * shrink)
            term = per_head([jnp.sum(along[k] * inverse[k], axis=0, keepdims=True) for k in range(2)])
            s.head_terms[...] += term * root_lanes / (2.0 * scale_lanes)
        pieces.append(per_head(grads[2]))
        grad_qkv = jnp.concatenate(pieces, axis=1).astype(BF)
        s.grad_qkv[canvas] = grad_qkv
        part = dot(grad_qkv, s.qkv_line[...].reshape(width, own_cols), 1, 1)
        s.gna_part[slots(canvas)] = part.astype(BF).reshape(2, rows, width)

    s.head_terms[...] = jnp.zeros((1, lanes), F32)
    gna_reduce = Reduce(
        s.gna_part, s.gna_pair, s.gna_far, s.gna_chip, s.sem_gna
    )
    each_canvas(attend_back, False, after=gna_reduce.steps())
    out_reduce.send_far()
    out_reduce.send_near()
    gna_reduce.middle()

    def qkv_term(k, carry):
        cols = pl.ds(pl.multiple_of(k * 8 * up_rows, 8 * up_rows), 8 * up_rows)
        term = dot(
            normed[:, :, cols].reshape(all_rows, 8 * up_rows),
            s.grad_qkv[...].reshape(all_rows, own_cols),
            0,
            0,
        )
        s.qkv_term[k] = term.astype(BF).reshape(8, up_rows, own_cols)
        return carry

    lax.fori_loop(0, lines, qkv_term, 0)
    qkv_fold = Fold(s.qkv_term, s.qkv_in, s.sem_qkv_fold)
    qkv_fold.start()

    term = dot(
        s.attended[...].reshape(all_rows, lanes),
        s.branch[...].reshape(all_rows, width),
        0,
        0,
    ).astype(BF).reshape(2, 2, half_head, width)
    halves = s.out_halves
    for k in range(2):
        for half in range(2):
            halves[half, k] = term[k, half]
    swap = Copy(
        halves.at[1 - y], s.out_swap, s.out_swap, s.sem_half, 1, device((0, 0, 1))
    )
    swap.start()

    grad_in, attn_sum = norm_back(x_ref[...].astype(F32), scale_row(own_canvas, False), gna_reduce.finish())
    input_grad[...] = s.grad_middle[...] + grad_in
    put_row(sums_own, 0, attn_sum)
    head_rows = lax.broadcasted_iota(jnp.int32, (8, lanes), 0)
    head_lane = lax.broadcasted_iota(jnp.int32, (8, lanes), 1)
    head_tile = jnp.zeros((8, lanes), F32)
    for k in range(2):
        value = jnp.sum(
            jnp.where(lane == k * (lanes // 2), s.head_terms[...], 0.0), axis=1, keepdims=True
        )
        head_tile = head_tile + jnp.where(
            (head_rows == 0) & (head_lane == head_of(k)), value, 0.0
        )
    sums_own[16:24, :] = head_tile
    sums_copy = Copy(
        sums_own, s.sums_pair, s.sums_pair, s.sem_half, 2, device((0, 0, 1))
    )
    sums_copy.start()
    out_reduce.middle()
    swap.arrive()
    out_terms = s.out_terms
    for k in range(2):
        out_terms[2 * y + k] = halves[y, k]
        out_terms[2 * (1 - y) + k] = s.out_swap[k]
    out_fold = Fold(out_terms, s.out_in, s.sem_out_fold)
    out_fold.start()
    qkv_fold.middle()
    sums_copy.arrive()
    sums = s.sums
    sums[dp] = sums_own[...] + s.sums_pair[...]
    all_sums = Canvases(sums, s.sem_sums)
    all_sums.start()
    down_grad[...] = down_fold.finish(s.down_total).reshape(down_rows, width)
    all_sums.middle()
    out_fold.middle()
    block_out[...] = (s.middle[...] + out_reduce.finish()).astype(BF)
    s.up_sum[...] = up_fold.finish(s.up_total).astype(BF)
    up_return = Spread(s.up_sum, s.up_back, s.sem_up_back)
    up_return.start()
    s.qkv_sum[...] = qkv_fold.finish(s.qkv_total).astype(BF)
    qkv_return = Spread(s.qkv_sum, s.qkv_back, s.sem_qkv_back)
    qkv_return.start()

    all_sums.finish()
    rounded = [
        jnp.concatenate([sums[:, offset + r, :] for r in range(width // 128)], axis=1).astype(BF)
        for offset in (0, 8)
    ]
    mine_for = dot(rounded[0], mod_full[:, :width], 1, 1) + dot(
        rounded[1], mod_full[:, width:], 1, 1
    )
    cond_line, cond_in = s.cond_line, s.cond_in
    s.cond_all[...] = mine_for
    for k in range(lines):
        cond_line[k] = s.cond_all[8 * (k // 2) : 8 * (k // 2) + 8, :]
    cond_send = [
        Copy(
            cond_line.at[(z + along) % lines],
            cond_in.at[me, z],
            cond_in.at[me, (z + lines - along) % lines],
            s.sem_cond_line,
            along - 1,
            device(here, along),
        )
        for along in range(1, lines)
    ]
    for copy in cond_send:
        copy.start()
    cond_in[me, z] = cond_line[z]
    amod_grad[...] = dot(cond_mine, rounded[0], 0, 0)[:mod_rows]
    fmod_grad[...] = dot(cond_mine, rounded[1], 0, 0)[:mod_rows]
    head_sum = sums[0, 16:17, :]
    for k in range(1, sums.shape[0]):
        head_sum = head_sum + sums[k, 16:17, :]
    scale_grad[...] = head_sum[:, : scale_grad.shape[1]]
    for copy in cond_send:
        copy.arrive()
    cond_share = Share(cond_in, s.sem_cond_share)
    cond_share.start()
    out_grad[...] = out_fold.finish(s.out_total)
    cond_share.finish()
    for k in range(lines):
        for m in range(8):
            at_row = 8 * k + m
            row = cond_in[m, k, pl.ds(4 * (z % 2) + own_canvas, 1), :]
            cond_grad[:, at_row * mod_rows : (at_row + 1) * mod_rows] = row[:, :mod_rows]
    up_return.finish()
    for m, own, whole in up_places:
        up_grad[:, whole : whole + down_rows] = s.up_back[m, :, own : own + down_rows].astype(F32)
    qkv_return.finish()
    for m, own, whole in qkv_places:
        qkv_grad[:, whole : whole + size] = s.qkv_back[m, :, own : own + size].astype(F32)
    for copy, when in sends:
        if when is None:
            copy.wait_send()
        else:
            pl.when(when)(copy.wait_send)


def scratch_plan(lines, x_ref, qkv_ref, up_ref, out_ref, down_ref):
    rows, width = x_ref.shape
    up_rows = up_ref.shape[0]
    own_cols, up_cols = qkv_ref.shape[1] // 8, up_ref.shape[1] // 8
    hidden = up_cols // 2
    half_head = out_ref.shape[0]
    down_rows = down_ref.shape[0]
    lanes = own_cols // 3
    groups = 4 * lines
    plane = (8, rows, width)
    vm = lambda shape, kind=BF: pltpu.VMEM(shape, kind)
    sem = lambda count: pltpu.SemaphoreType.DMA((2, count))
    plan = dict(
        ids=vm((8, 8, rows), jnp.int32),
        conds=vm((groups, 8, 128), F32),
        tokens=vm(plane),
        cots=vm(plane),
        normed=vm(plane),
        ffn=vm(plane),
        branch=vm(plane),
        qkv_cols=vm((8, up_rows, own_cols)),
        up_cols=vm((8, up_rows, up_cols)),
        qkv_line=vm((lines, 8, up_rows, own_cols)),
        up_line=vm((lines, 8, up_rows, up_cols)),
        out_line=vm((lines, half_head, width)),
        down_line=vm((lines, down_rows, width)),
        out_half=vm((2, half_head, width)),
        out_full=vm((2, 2, half_head, width)),
        mod_full=vm((128, 2 * width)),
        mod_terms=vm((8, groups, width // 4), F32),
        mod_in=vm((8, groups, width // 4), F32),
        mod_line=vm((lines, groups, width // 4), F32),
        mod_total=vm((groups, width // 4), F32),
        mods=vm((8, 8, width // 4), F32),
        scales=vm((8, 2 * width), F32),
        turns=vm((4, 2 * rows, 2 * lanes), F32),
        raw=vm((4, 2, 2 * rows, lanes), F32),
        rotated=vm((4, 3, 2 * rows, lanes)),
        probs=vm((4, 2, 2 * rows, 2 * rows), F32),
        raw_attended=vm((4, 2 * rows, lanes), F32),
        attended=vm((4, 2 * rows, lanes)),
        middle=vm((rows, width), F32),
        grad_middle=vm((rows, width), F32),
        hidden=vm((4, 2 * rows, hidden)),
        act=vm((4, 2 * rows, hidden), F32),
        slope=vm((4, 2 * rows, hidden), F32),
        grad_up=vm((4, 2 * rows, up_cols)),
        grad_qkv=vm((4, 2 * rows, own_cols)),
        head_terms=vm((1, lanes), F32),
        sums_own=vm((24, 128), F32),
        sums_pair=vm((24, 128), F32),
        sums=vm((groups, 24, 128), F32),
        cond_all=vm((groups, 128), F32),
        cond_line=vm((lines, 8, 128), F32),
        cond_in=vm((8, lines, 8, 128), F32),
        down_total=vm((down_rows, width), F32),
        up_total=vm((8, up_rows, up_cols), F32),
        qkv_total=vm((8, up_rows, own_cols), F32),
        out_total=vm((half_head, width), F32),
        down_term=vm((lines, down_rows, width)),
        down_in=vm((4, down_rows, width)),
        up_term=vm((lines, 8, up_rows, up_cols)),
        up_in=vm((4, 8, up_rows, up_cols)),
        up_sum=vm((8, up_rows, up_cols)),
        up_back=vm((8, up_rows, up_cols)),
        qkv_term=vm((lines, 8, up_rows, own_cols)),
        qkv_in=vm((4, 8, up_rows, own_cols)),
        qkv_sum=vm((8, up_rows, own_cols)),
        qkv_back=vm((8, up_rows, own_cols)),
        out_halves=vm((2, 2, half_head, width)),
        out_swap=vm((2, half_head, width)),
        out_terms=vm((lines, half_head, width)),
        out_in=vm((4, half_head, width)),
    )
    for name in ("mid", "gnf", "out", "gna"):
        plan[name + "_part"] = vm(plane)
        plan[name + "_pair"] = vm((4, rows, width))
        plan[name + "_far"] = vm((2, rows // 2, width))
        plan[name + "_chip"] = vm((2, rows, width))
        plan["sem_" + name] = sem(10)
    plan.update(
        sem_tokens=sem(10),
        sem_cots=sem(10),
        sem_ffn=sem(10),
        sem_branch=sem(10),
        sem_ids=sem(7),
        sem_qkv_spread=sem(7),
        sem_up_spread=sem(7),
        sem_mod_spread=sem(7),
        sem_mods=sem(7),
        sem_up_back=sem(7),
        sem_qkv_back=sem(7),
        sem_cond_share=sem(7),
        sem_qkv_line=sem(5),
        sem_up_line=sem(5),
        sem_out_line=sem(5),
        sem_down_line=sem(5),
        sem_mod_line=sem(lines - 1),
        sem_cond_line=sem(lines - 1),
        sem_down_fold=sem(5),
        sem_up_fold=sem(5),
        sem_qkv_fold=sem(5),
        sem_out_fold=sem(5),
        sem_cond=sem(lines + 2),
        sem_sums=sem(lines + 2),
        sem_half=sem(3),
    )
    return plan


def turn_tables(heads, lines):
    head_size = 64
    table = np.zeros((heads, 2, 16, 2, head_size), np.float64)
    for axis in range(2):
        for j in range(8):
            freq = math.pi * 10.0 ** ((j * heads + np.arange(heads)) / (8.0 * heads))
            unit = (2.0 * np.arange(16) + 1.0) / 16.0 - 1.0
            angle = freq[:, None].astype(np.float32) * unit[None, :].astype(np.float32)
            angle = angle.astype(np.float64)
            for half in range(2):
                at = axis * 16 + half * 8 + j
                table[:, axis, :, 0, at] = np.cos(angle)
                table[:, axis, :, 1, at] = np.sin(angle) * (1.0 if half else -1.0)
    table[:, 0, :, 0, 32:] = 1.0
    high = table.astype(ml_dtypes.bfloat16)
    low = (table - high.astype(np.float64)).astype(ml_dtypes.bfloat16)
    parts = []
    for term in (high, low):
        term = term.reshape(2, 2, 2, 2, 2, 16, 2, head_size)
        term = term.transpose(2, 3, 0, 4, 5, 6, 1, 7)
        parts.append(term.reshape(8, 32, 4 * head_size))
    return np.concatenate(parts, axis=1)


def plane_shards(
    block_in,
    conditioning,
    crop_ids,
    positions,
    qkv_weight,
    out_weight,
    up_weight,
    down_weight,
    attn_modulate,
    ffn_modulate,
    head_scale,
    cotangent,
):
    lines = lax.axis_size("dp") // 4
    rows, width = block_in.shape[1:]
    heads = head_scale.shape[0]
    tables = jnp.asarray(turn_tables(heads, lines))
    kinds = jax.ShapeDtypeStruct
    operands = (
        block_in[0],
        cotangent[0],
        qkv_weight,
        up_weight,
        out_weight,
        down_weight,
        attn_modulate,
        ffn_modulate,
        conditioning,
        crop_ids,
        positions,
        head_scale,
        tables,
    )
    plan = scratch_plan(lines, operands[0], qkv_weight, up_weight, out_weight, down_weight)
    in_vmem = pl.BlockSpec(memory_space=pltpu.VMEM)
    in_specs = [in_vmem] * len(operands)
    in_specs[11] = pl.BlockSpec(memory_space=pltpu.SMEM)
    results = pl.pallas_call(
        functools.partial(block_kernel, lines),
        out_shape=(
            kinds((rows, width), BF),
            kinds((rows, width), F32),
            kinds(conditioning.shape, F32),
            kinds(qkv_weight.shape, F32),
            kinds(out_weight.shape, F32),
            kinds(up_weight.shape, F32),
            kinds(down_weight.shape, F32),
            kinds(attn_modulate.shape, F32),
            kinds(ffn_modulate.shape, F32),
            kinds((1, heads), F32),
        ),
        in_specs=in_specs,
        out_specs=[in_vmem] * 10,
        scratch_shapes=list(plan.values()),
        compiler_params=pltpu.CompilerParams(
            collective_id=0, has_side_effects=True, vmem_limit_bytes=63 * 2**20
        ),
    )(*operands)
    results = settle(results)
    return tuple(item[None] for item in results[:2]) + tuple(results[2:-1]) + (results[-1][0],)


def settle(results):
    count = len(results)

    def kernel(*refs):
        copies = [
            pltpu.make_async_copy(refs[k], refs[count + k], refs[-1].at[k]) for k in range(count)
        ]
        for copy in copies:
            copy.start()
        for copy in copies:
            copy.wait()

    anywhere = pl.BlockSpec(memory_space=pl.ANY)
    return pl.pallas_call(
        kernel,
        out_shape=tuple(jax.ShapeDtypeStruct(item.shape, item.dtype) for item in results),
        in_specs=[pl.BlockSpec(memory_space=pltpu.VMEM)] * count,
        out_specs=[anywhere] * count,
        scratch_shapes=[pltpu.SemaphoreType.DMA((count,))],
    )(*results)


def in_planes(mesh):
    return mesh.shape["seq"] == 2 and mesh.shape["dp"] == 16


def solution(mesh):
    in_specs = (
        P("dp", "seq", None),
        P("dp", None),
        P("dp", "seq"),
        P("dp", None, "seq"),
        P(("dp", "seq"), None),
        P(("dp", "seq"), None),
        P(("dp", "seq"), None),
        P(("dp", "seq"), None),
        P(("dp", "seq"), None),
        P(("dp", "seq"), None),
        P(),
        P("dp", "seq", None),
    )
    out_specs = (
        P("dp", "seq", None),
        P("dp", "seq", None),
        P("dp", None),
        P(("dp", "seq"), None),
        P(("dp", "seq"), None),
        P(("dp", "seq"), None),
        P(("dp", "seq"), None),
        P(("dp", "seq"), None),
        P(("dp", "seq"), None),
        P(),
    )
    body = plane_shards if in_planes(mesh) else shards
    return jax.shard_map(body, mesh=mesh, in_specs=in_specs, out_specs=out_specs, check_vma=False)
```

```python
import functools
import math
import types

import jax
import jax.numpy as jnp
import ml_dtypes
import numpy as np
from jax import lax
from jax.experimental import pallas as pl
from jax.experimental.pallas import tpu as pltpu
from jax.sharding import PartitionSpec as P

eps_norm = 1e-06
eps_cosine = 1e-06
negative = -1e30
key_rows = 256


def block_split(count, limit):
    size_rows = math.gcd(count, limit)
    return (size_rows, count // size_rows)


def rope_tables(positions, heads):
    unit_pos = (2.0 * positions.astype(jnp.float32) + 1.0) / 16.0 - 1.0
    exponent = (
        jnp.arange(8, dtype=jnp.float32)[None, :] * heads
        + jnp.arange(heads, dtype=jnp.float32)[:, None]
    ) / (8.0 * heads)
    frequency = math.pi * 10.0**exponent
    angles = jnp.moveaxis(unit_pos[..., None, None] * frequency, -4, -2)
    return (jnp.cos(angles), jnp.sin(angles))


def rotate(vector, cosine, sine):
    leading = vector.shape[:-1]
    turned_part = vector[..., :32].reshape(leading + (2, 2, 8))
    first_half = turned_part[..., 0, :]
    second_half = turned_part[..., 1, :]
    turned = jnp.stack(
        [first_half * cosine - second_half * sine, first_half * sine + second_half * cosine],
        axis=-2,
    )
    return jnp.concatenate([turned.reshape(leading + (32,)), vector[..., 32:]], axis=-1)


def norm_forward(value, scale):
    inverse = lax.rsqrt(jnp.mean(value * value, axis=-1, keepdims=True) + eps_norm)
    return (value * inverse * scale[:, None], inverse)


def norm_backward(value, inverse, scale, grad_norm):
    scaled = grad_norm * scale[:, None]
    grad_value = inverse * scaled - value * inverse**3 * jnp.mean(
        scaled * value, axis=-1, keepdims=True
    )
    grad_scale = jnp.sum(grad_norm * value * inverse, axis=1)
    return (grad_value, grad_scale)


def cosine_forward(value, root_scale):
    factor = root_scale[:, None] * lax.rsqrt(
        jnp.sum(value * value, axis=-1, keepdims=True) + eps_cosine
    )
    return (value * factor, factor)


def cosine_backward(value, factor, grad):
    squares = jnp.sum(value * value, axis=-1, keepdims=True) + eps_cosine
    along = jnp.sum(grad * value, axis=-1, keepdims=True)
    grad_value = factor * grad - value * factor * along / squares
    return (grad_value, jnp.sum(along * factor, axis=(0, 1, 3)))


def geglu(value_part, gate_part):
    return value_part * jax.nn.gelu(gate_part, approximate=False)


def pair_grads(queries, grad_att, log_total, deltas, query_crop, key_block, value_block, key_crop):
    scores = jnp.einsum("cqhd,ckhd->cqhk", queries, key_block, preferred_element_type=jnp.float32)
    allowed = (query_crop[:, :, None] == key_crop[:, None, :])[:, :, None, :]
    probs = jnp.exp(jnp.where(allowed, scores - log_total[..., None], negative))
    probs = jnp.where(allowed, probs, 0.0)
    dotted = jnp.einsum(
        "cqhd,ckhd->cqhk", grad_att, value_block, preferred_element_type=jnp.float32
    )
    slope = (probs * (dotted - deltas[..., None])).astype(jnp.bfloat16)
    grad_q = jnp.einsum("cqhk,ckhd->cqhd", slope, key_block, preferred_element_type=jnp.float32)
    grad_k = jnp.einsum("cqhk,cqhd->ckhd", slope, queries, preferred_element_type=jnp.float32)
    grad_v = jnp.einsum(
        "cqhk,cqhd->ckhd", probs.astype(jnp.bfloat16), grad_att, preferred_element_type=jnp.float32
    )
    return (grad_q, grad_k, grad_v)


def pack_terms(terms, lead_shape):
    return jnp.concatenate([term.reshape(lead_shape + (-1,)) for term in terms], axis=-1)


def unpack_terms(packed_row, terms, owners):
    results = []
    offset = 0
    for term in terms:
        own_rows = term.shape[0] // owners
        count = own_rows * term.shape[1]
        results.append(packed_row[offset : offset + count].reshape(own_rows, term.shape[1]))
        offset = offset + count
    return results


def shards(
    block_in,
    conditioning,
    crop_ids,
    positions,
    qkv_weight,
    out_weight,
    up_weight,
    down_weight,
    attn_modulate,
    ffn_modulate,
    head_scale,
    cotangent,
):
    qkv_full, out_full, up_full, down_full, attn_mod, ffn_mod = (
        lax.all_gather(qkv_weight, ("dp", "seq"), axis=0, tiled=True),
        lax.all_gather(out_weight, ("dp", "seq"), axis=0, tiled=True),
        lax.all_gather(up_weight, ("dp", "seq"), axis=0, tiled=True),
        lax.all_gather(down_weight, ("dp", "seq"), axis=0, tiled=True),
        lax.all_gather(attn_modulate, ("dp", "seq"), axis=0, tiled=True),
        lax.all_gather(ffn_modulate, ("dp", "seq"), axis=0, tiled=True),
    )
    canvases, rows, width = block_in.shape
    heads = head_scale.shape[0]
    head_size = width // heads
    hidden_width = down_full.shape[0]
    seq_count = lax.axis_size("seq")
    inputs = block_in.astype(jnp.float32)
    scale_attn = 1.0 + jnp.dot(conditioning, attn_mod, preferred_element_type=jnp.float32)
    scale_ffn = 1.0 + jnp.dot(conditioning, ffn_mod, preferred_element_type=jnp.float32)
    normed_attn, inverse_attn = norm_forward(inputs, scale_attn)
    normed_attn = normed_attn.astype(jnp.bfloat16)
    qkv_all = jnp.einsum(
        "csd,de->cse", normed_attn, qkv_full, preferred_element_type=jnp.float32
    ).reshape(canvases, rows, 3, heads, head_size)
    root_scale = jnp.sqrt(head_scale)
    query_cos, query_factor = cosine_forward(qkv_all[:, :, 0], root_scale)
    key_cos, key_factor = cosine_forward(qkv_all[:, :, 1], root_scale)
    cosine, sine = rope_tables(positions, heads)
    queries = rotate(query_cos, cosine, sine).astype(jnp.bfloat16)
    keys_flat = rotate(key_cos, cosine, sine).astype(jnp.bfloat16).reshape(canvases, rows, width)
    values_flat = qkv_all[:, :, 2].astype(jnp.bfloat16).reshape(canvases, rows, width)
    start_state = (
        jnp.full((canvases, rows, heads), negative, jnp.float32),
        jnp.zeros((canvases, rows, heads), jnp.float32),
        jnp.zeros((canvases, rows, heads, head_size), jnp.float32),
    )
    state_now = start_state
    piece_keys = lax.all_gather(keys_flat, "seq", axis=1, tiled=True)
    piece_values = lax.all_gather(values_flat, "seq", axis=1, tiled=True)
    piece_crop = lax.all_gather(crop_ids, "seq", axis=1, tiled=True)
    size_rows, number = block_split(piece_keys.shape[1], key_rows)

    def step_block(state, block_index):
        running_max, row_total, weighted = state
        offset = block_index * size_rows
        key_block = lax.dynamic_slice_in_dim(piece_keys, offset, size_rows, 1).reshape(
            canvases, size_rows, heads, head_size
        )
        value_block = lax.dynamic_slice_in_dim(piece_values, offset, size_rows, 1).reshape(
            canvases, size_rows, heads, head_size
        )
        crop_block = lax.dynamic_slice_in_dim(piece_crop, offset, size_rows, 1)
        scores = jnp.einsum(
            "cqhd,ckhd->cqhk", queries, key_block, preferred_element_type=jnp.float32
        )
        allowed = (crop_ids[:, :, None] == crop_block[:, None, :])[:, :, None, :]
        scores = jnp.where(allowed, scores, negative)
        new_max = jnp.maximum(running_max, jnp.max(scores, axis=-1))
        weights = jnp.where(allowed, jnp.exp(scores - new_max[..., None]), 0.0)
        shrink = jnp.exp(running_max - new_max)
        row_total = row_total * shrink + jnp.sum(weights, axis=-1)
        weighted = weighted * shrink[..., None] + jnp.einsum(
            "cqhk,ckhd->cqhd",
            weights.astype(jnp.bfloat16),
            value_block,
            preferred_element_type=jnp.float32,
        )
        return ((new_max, row_total, weighted), None)

    state_now, unused = lax.scan(step_block, state_now, jnp.arange(number))
    running_max, row_total, weighted = state_now
    log_total = running_max + jnp.log(row_total)
    attended_raw = weighted / row_total[..., None]
    attended = attended_raw.astype(jnp.bfloat16).reshape(canvases, rows, width)
    middle = inputs + jnp.einsum(
        "csd,de->cse", attended, out_full, preferred_element_type=jnp.float32
    )
    normed_ffn, inverse_ffn = norm_forward(middle, scale_ffn)
    normed_ffn = normed_ffn.astype(jnp.bfloat16)
    up_all = jnp.einsum("csd,de->cse", normed_ffn, up_full, preferred_element_type=jnp.float32)
    value_part = up_all[..., :hidden_width]
    gate_part = up_all[..., hidden_width:]
    hidden = geglu(value_part, gate_part).astype(jnp.bfloat16)
    block_out = (
        middle + jnp.einsum("csf,fd->csd", hidden, down_full, preferred_element_type=jnp.float32)
    ).astype(jnp.bfloat16)
    down_term = jnp.einsum("csf,csd->fd", hidden, cotangent, preferred_element_type=jnp.float32)
    grad_hidden = jnp.einsum(
        "csd,fd->csf", cotangent, down_full, preferred_element_type=jnp.float32
    )
    unused_value, geglu_pull = jax.vjp(geglu, value_part, gate_part)
    grad_value, grad_gate = geglu_pull(grad_hidden)
    grad_up = jnp.concatenate([grad_value, grad_gate], axis=-1).astype(jnp.bfloat16)
    up_term = jnp.einsum("csd,cse->de", normed_ffn, grad_up, preferred_element_type=jnp.float32)
    grad_normed_ffn = jnp.einsum(
        "cse,de->csd", grad_up, up_full, preferred_element_type=jnp.float32
    )
    grad_mid_norm, ffn_scale_sum = norm_backward(middle, inverse_ffn, scale_ffn, grad_normed_ffn)
    grad_middle = cotangent.astype(jnp.float32) + grad_mid_norm
    grad_branch = grad_middle.astype(jnp.bfloat16)
    out_term = jnp.einsum("csd,cse->de", attended, grad_branch, preferred_element_type=jnp.float32)
    grad_attended = (
        jnp.einsum("cse,de->csd", grad_branch, out_full, preferred_element_type=jnp.float32)
        .astype(jnp.bfloat16)
        .reshape(canvases, rows, heads, head_size)
    )
    deltas = jnp.sum(grad_attended.astype(jnp.float32) * attended_raw, axis=-1)
    start_back = (
        jnp.zeros((canvases, rows, heads, head_size), jnp.float32),
        jnp.zeros((canvases, rows * seq_count, 2 * width), jnp.float32),
    )
    state_now = start_back
    fold_piece_keys = lax.all_gather(keys_flat, "seq", axis=1, tiled=True)
    fold_piece_values = lax.all_gather(values_flat, "seq", axis=1, tiled=True)
    fold_piece_crop = lax.all_gather(crop_ids, "seq", axis=1, tiled=True)
    fold_size_rows, number = block_split(fold_piece_keys.shape[1], key_rows)

    def step_block(state, block_index):
        grad_q_sum, grad_kv_all = state
        offset = block_index * fold_size_rows
        key_block = lax.dynamic_slice_in_dim(fold_piece_keys, offset, fold_size_rows, 1).reshape(
            canvases, fold_size_rows, heads, head_size
        )
        value_block = lax.dynamic_slice_in_dim(
            fold_piece_values, offset, fold_size_rows, 1
        ).reshape(canvases, fold_size_rows, heads, head_size)
        crop_block = lax.dynamic_slice_in_dim(fold_piece_crop, offset, fold_size_rows, 1)
        grad_q, grad_k, grad_v = pair_grads(
            queries, grad_attended, log_total, deltas, crop_ids, key_block, value_block, crop_block
        )
        update = jnp.concatenate(
            [
                grad_k.reshape(canvases, fold_size_rows, width),
                grad_v.reshape(canvases, fold_size_rows, width),
            ],
            axis=-1,
        )
        previous = lax.dynamic_slice_in_dim(grad_kv_all, offset, fold_size_rows, 1)
        grad_kv_all = lax.dynamic_update_slice_in_dim(grad_kv_all, previous + update, offset, 1)
        return ((grad_q_sum + grad_q, grad_kv_all), None)

    state_now, unused = lax.scan(step_block, state_now, jnp.arange(number))
    grad_queries, grad_kv_all = state_now
    grad_kv = lax.psum_scatter(
        grad_kv_all.astype(jnp.bfloat16), "seq", scatter_dimension=1, tiled=True
    ).astype(jnp.float32)
    grad_keys = grad_kv[..., :width].reshape(canvases, rows, heads, head_size)
    grad_values = grad_kv[..., width:].reshape(canvases, rows, heads, head_size)
    grad_query_cos = rotate(grad_queries, cosine, -sine)
    grad_key_cos = rotate(grad_keys, cosine, -sine)
    grad_query_raw, query_part = cosine_backward(qkv_all[:, :, 0], query_factor, grad_query_cos)
    grad_key_raw, key_part = cosine_backward(qkv_all[:, :, 1], key_factor, grad_key_cos)
    scale_local = (query_part + key_part) / (2.0 * head_scale)
    grad_qkv = (
        jnp.stack([grad_query_raw, grad_key_raw, grad_values], axis=2)
        .astype(jnp.bfloat16)
        .reshape(canvases, rows, 3 * width)
    )
    qkv_term = jnp.einsum("csd,cse->de", normed_attn, grad_qkv, preferred_element_type=jnp.float32)
    grad_normed_attn = jnp.einsum(
        "cse,de->csd", grad_qkv, qkv_full, preferred_element_type=jnp.float32
    )
    grad_in_norm, attn_scale_sum = norm_backward(inputs, inverse_attn, scale_attn, grad_normed_attn)
    input_grad = grad_middle + grad_in_norm
    attn_sums, ffn_sums = lax.psum((attn_scale_sum, ffn_scale_sum), "seq")
    attn_sums = attn_sums.astype(jnp.bfloat16)
    ffn_sums = ffn_sums.astype(jnp.bfloat16)
    cond_grad = jnp.einsum(
        "cd,nd->cn", attn_sums, attn_mod, preferred_element_type=jnp.float32
    ) + jnp.einsum("cd,nd->cn", ffn_sums, ffn_mod, preferred_element_type=jnp.float32)
    leader = lax.axis_index("seq") == 0
    attn_mod_term = jnp.where(
        leader,
        jnp.einsum("cn,cd->nd", conditioning, attn_sums, preferred_element_type=jnp.float32),
        0.0,
    )
    ffn_mod_term = jnp.where(
        leader,
        jnp.einsum("cn,cd->nd", conditioning, ffn_sums, preferred_element_type=jnp.float32),
        0.0,
    )
    terms = (qkv_term, out_term, up_term, down_term, attn_mod_term, ffn_mod_term)
    groups = lax.axis_size("dp")
    owners = groups * seq_count
    packed = pack_terms(terms, (owners,))
    summed = lax.psum_scatter(packed, ("dp", "seq"), scatter_dimension=0, tiled=True)
    packed_row = summed[0]
    qkv_grad, out_grad, up_grad, down_grad, attnmod_grad, ffnmod_grad = unpack_terms(
        packed_row, terms, owners
    )
    scale_grad = lax.psum(scale_local, ("dp", "seq"))
    return (
        block_out,
        input_grad,
        cond_grad,
        qkv_grad,
        out_grad,
        up_grad,
        down_grad,
        attnmod_grad,
        ffnmod_grad,
        scale_grad,
    )


MESH = pl.DeviceIdType.MESH
BF = jnp.bfloat16
F32 = jnp.float32
PLANE = ((1, 0, 0), (0, 0, 1), (1, 0, 1), (0, 1, 0), (1, 1, 0), (0, 1, 1), (1, 1, 1))
TO_X, TO_Y, TO_FAR = (1, 0, 0), (0, 0, 1), (1, 0, 1)
ERF_P = (
    0.00022905065861350646,
    0.0034082910107109506,
    0.050955695062380861,
    0.18520832239976145,
    1.128379143519084,
)
ERF_Q = (
    -1.1791602954361697e-7,
    0.000023547966471313185,
    0.0010179625278914885,
    0.014070470171167667,
    0.11098505178285362,
    0.49746925110067538,
    1.0,
)


def erf(value):
    value = jnp.clip(value, -3.832506856900711, 3.832506856900711)
    square = value * value
    top = jnp.full_like(value, ERF_P[0])
    for term in ERF_P[1:]:
        top = top * square + term
    bottom = jnp.full_like(value, ERF_Q[0])
    for term in ERF_Q[1:]:
        bottom = bottom * square + term
    return value * top / bottom


def dot(lhs, rhs, on_lhs=1, on_rhs=0):
    return lax.dot_general(
        lhs, rhs, (((on_lhs,), (on_rhs,)), ((), ())), preferred_element_type=F32
    )


def block_kernel(
    lines,
    x_ref,
    cot_ref,
    qkv_ref,
    up_ref,
    out_ref,
    down_ref,
    amod_ref,
    fmod_ref,
    cond_ref,
    crop_ref,
    pos_ref,
    scale_ref,
    table_ref,
    block_out,
    input_grad,
    cond_grad,
    qkv_grad,
    out_grad,
    up_grad,
    down_grad,
    amod_grad,
    fmod_grad,
    scale_grad,
    *scratch,
):
    names = list(scratch_plan(lines, x_ref, qkv_ref, up_ref, out_ref, down_ref))
    s = types.SimpleNamespace(**dict(zip(names, scratch)))
    dp = lax.axis_index("dp")
    y = lax.axis_index("seq")
    z = dp // 4
    x = (dp // 2) % 2
    c = dp % 2
    rows, width = x_ref.shape
    up_rows = up_ref.shape[0]
    own_cols = qkv_ref.shape[1] // 8
    lanes = own_cols // 3
    half_head = out_ref.shape[0]
    hidden = up_ref.shape[1] // 16
    down_rows = down_ref.shape[0]
    mod_rows = amod_ref.shape[0]
    canvas_rows = 2 * rows
    crops = canvas_rows // 16
    me = 4 * x + 2 * c + y
    device_index = 8 * z + me

    def member(step):
        return 4 * ((x + step[0]) % 2) + 2 * ((c + step[1]) % 2) + (y + step[2]) % 2

    def device(step, along=0):
        return (
            ((z + along) % lines) * 4 + ((x + step[0]) % 2) * 2 + (c + step[1]) % 2,
            (y + step[2]) % 2,
        )

    def line_device(along):
        return (jnp.clip(z + along, 0, lines - 1) * 4 + dp % 4, y)

    def inside(along):
        return z + along < lines if along > 0 else z + along >= 0

    here = (0, 0, 0)
    core = (0, 1, 0)
    sends = []

    class Copy:
        def __init__(self, src, dst_there, dst_here, sems, at, target):
            self.out = pltpu.make_async_remote_copy(
                src_ref=src,
                dst_ref=dst_there,
                send_sem=sems.at[0, at],
                recv_sem=sems.at[1, at],
                device_id=target,
                device_id_type=MESH,
            )
            self.into = pltpu.make_async_remote_copy(
                src_ref=src,
                dst_ref=dst_here,
                send_sem=sems.at[0, at],
                recv_sem=sems.at[1, at],
                device_id=target,
                device_id_type=MESH,
            )

        def start(self, when=None):
            if when is None:
                self.out.start()
            else:
                pl.when(when)(self.out.start)
            sends.append((self.out, when))

        def arrive(self):
            self.into.wait_recv()

    class Gather:
        def __init__(self, buffer, sems):
            at = lambda step: buffer.at[member(step)]
            half = buffer.shape[1] // 2
            rows_of = (pl.ds(0, half), pl.ds(half, half))
            part = lambda step, k: buffer.at[member(step), rows_of[k]]
            self.x_own = [
                Copy(part(here, k), part(here, k), part(TO_X, k), sems, k, device(TO_X))
                for k in range(2)
            ]
            self.y_own = [
                Copy(part(here, k), part(here, k), part(TO_Y, k), sems, 2 + k, device(TO_Y))
                for k in range(2)
            ]
            self.y_far = Copy(part(TO_X, 0), part(TO_X, 0), part(TO_FAR, 0), sems, 4, device(TO_Y))
            self.x_far = Copy(part(TO_Y, 1), part(TO_Y, 1), part(TO_FAR, 1), sems, 5, device(TO_X))
            self.pair = Copy(at(here), at(here), at(core), sems, 6, device(core))
            self.cross = [
                Copy(at(step), at(step), at((step[0], 1, step[2])), sems, 7 + k, device(core))
                for k, step in enumerate((TO_X, TO_Y, TO_FAR))
            ]

        def start(self):
            self.x_own[0].start()
            self.y_own[1].start()
            self.x_own[1].start()
            self.y_own[0].start()
            self.pair.start()

        def turn(self):
            self.x_own[0].arrive()
            self.y_far.start()
            self.y_own[1].arrive()
            self.x_far.start()

        def near(self):
            self.y_own[0].arrive()
            self.cross[1].start()
            self.x_own[1].arrive()
            self.cross[0].start()

        def far(self):
            self.y_far.arrive()
            self.x_far.arrive()
            self.cross[2].start()

        def pair_near(self):
            self.pair.arrive()
            self.cross[1].arrive()

        def pair_far(self):
            self.cross[0].arrive()
            self.cross[2].arrive()

        def finish(self):
            self.near()
            self.far()
            self.pair_near()
            self.pair_far()

        def steps(self):
            return {0: self.near, 1: self.pair_near, 2: self.far, 3: self.pair_far}

    class Reduce:
        def __init__(self, part, pair_in, far_in, chip_in, sems):
            self.part, self.pair_in, self.far_in, self.chip_in = part, pair_in, far_in, chip_in
            half = part.shape[1] // 2
            self.rows_of = rows_of = (pl.ds(0, half), pl.ds(half, half))
            self.steps_of = (here, TO_X, TO_Y, TO_FAR)
            self.pair = [
                Copy(
                    part.at[member((step[0], 1, step[2]))],
                    pair_in.at[k],
                    pair_in.at[k],
                    sems,
                    k,
                    device(core),
                )
                for k, step in enumerate(self.steps_of)
            ]
            piece = lambda step, k: part.at[member(step), rows_of[k]]
            self.x_far = Copy(piece(TO_FAR, 0), far_in.at[0], far_in.at[0], sems, 4, device(TO_X))
            self.y_far = Copy(piece(TO_FAR, 1), far_in.at[1], far_in.at[1], sems, 5, device(TO_Y))
            into = lambda way, k: chip_in.at[way, rows_of[k]]
            self.x_own = [
                Copy(piece(TO_X, k), into(0, k), into(0, k), sems, 6 + k, device(TO_X))
                for k in range(2)
            ]
            self.y_own = [
                Copy(piece(TO_Y, k), into(1, k), into(1, k), sems, 8 + k, device(TO_Y))
                for k in range(2)
            ]

        def add_pair(self, k):
            self.pair[k].arrive()
            slot = member(self.steps_of[k])
            total = self.part[slot].astype(F32) + self.pair_in[k].astype(F32)
            self.part[slot] = total.astype(BF)

        def add_far(self, step, k):
            slot = member(step)
            total = self.part[slot, self.rows_of[k], :].astype(F32) + self.far_in[k].astype(F32)
            self.part[slot, self.rows_of[k], :] = total.astype(BF)

        def give_far(self):
            self.pair[3].start()
            self.pair[1].start()

        def send_far(self):
            self.add_pair(3)
            self.x_far.start()
            self.y_far.start()
            self.add_pair(1)
            self.x_own[0].start()

        def give_near(self):
            self.pair[2].start()
            self.pair[0].start()

        def send_near(self):
            self.add_pair(2)
            self.y_own[1].start()

        def steps(self):
            return {0: self.give_far, 1: self.send_far, 2: self.give_near, 3: self.send_near}

        def middle(self):
            self.x_far.arrive()
            self.add_far(TO_Y, 0)
            self.y_own[0].start()
            self.y_far.arrive()
            self.add_far(TO_X, 1)
            self.x_own[1].start()

        def finish(self):
            self.pair[0].arrive()
            total = self.part[me].astype(F32) + self.pair_in[0].astype(F32)
            for copies in (self.x_own, self.y_own):
                for copy in copies:
                    copy.arrive()
            return total + self.chip_in[0].astype(F32) + self.chip_in[1].astype(F32)

    class Spread:
        def __init__(self, source, target, sems):
            self.source, self.target = source, target
            self.copies = [
                Copy(
                    source.at[member(step)],
                    target.at[me],
                    target.at[member(step)],
                    sems,
                    k,
                    device(step),
                )
                for k, step in enumerate(PLANE)
            ]

        def start(self):
            for copy in self.copies:
                copy.start()
            self.target[me] = self.source[me]

        def finish(self):
            for copy in self.copies:
                copy.arrive()

    class Share:
        def __init__(self, buffer, sems, block=None):
            self.copies = [
                Copy(
                    buffer.at[me] if block is None else block,
                    buffer.at[me],
                    buffer.at[member(step)],
                    sems,
                    k,
                    device(step),
                )
                for k, step in enumerate(PLANE)
            ]

        def start(self):
            for copy in self.copies:
                copy.start()

        def finish(self):
            for copy in self.copies:
                copy.arrive()

    class Line:
        def __init__(self, buffer, sems, first=None):
            self.copies = []
            for along in range(1, lines):
                back = (z + lines - along) % lines
                if first is None:
                    mine, theirs = buffer.at[z], buffer.at[back]
                else:
                    mine, theirs = buffer.at[pl.ds(first * z, first)], buffer.at[pl.ds(first * back, first)]
                self.copies.append(Copy(mine, mine, theirs, sems, along - 1, device(here, along)))

        def start(self):
            for copy in self.copies:
                copy.start()

        def finish(self):
            for copy in self.copies:
                copy.arrive()

    class Relay:
        def __init__(self, buffer, sems):
            self.copies = {
                along: Copy(
                    buffer.at[z],
                    buffer.at[z],
                    buffer.at[jnp.clip(z - along, 0, lines - 1)],
                    sems,
                    at,
                    line_device(along),
                )
                for at, along in enumerate((1, -1, 2, -2))
            }
            self.onward = {
                along: Copy(
                    buffer.at[far], buffer.at[far], buffer.at[far], sems, 4, line_device(along)
                )
                for along, far in ((1, 0), (-1, lines - 1))
            }

        def start(self, steps=(2, -2, 1, -1)):
            for along in steps:
                self.copies[along].start(inside(along))

        def middle(self):
            @pl.when(z == 2)
            def up_line():
                self.copies[2].arrive()

            @pl.when(z == 1)
            def down_line():
                self.copies[-2].arrive()

            self.onward[1].start(z == 2)
            self.onward[-1].start(z == 1)

        def finish(self):
            pl.when(z >= 1)(self.copies[1].arrive)
            pl.when(z <= 2)(self.copies[-1].arrive)
            pl.when(z == 3)(self.copies[2].arrive)
            pl.when(z == 0)(self.copies[-2].arrive)
            pl.when(z == 3)(self.onward[1].arrive)
            pl.when(z == 0)(self.onward[-1].arrive)

    class Fold:
        def __init__(self, terms, landed, sems):
            self.terms, self.landed = terms, landed
            self.copies = {
                along: Copy(
                    terms.at[jnp.clip(z + along, 0, lines - 1)],
                    landed.at[min(at, 2)],
                    landed.at[min(at, 2)],
                    sems,
                    at,
                    line_device(along),
                )
                for at, along in enumerate((1, -1, 2, -2))
            }
            self.first = {
                along: Copy(
                    terms.at[far], landed.at[3], landed.at[3], sems, 4, line_device(along)
                )
                for along, far in ((1, lines - 1), (-1, 0))
            }

        def start(self):
            self.first[1].start(z == 0)
            self.first[-1].start(z == lines - 1)
            self.copies[2].start(z == 0)
            self.copies[-2].start(z == lines - 1)
            for along in (1, -1):
                self.copies[along].start(inside(along))

        def middle(self):
            for at, far, along in ((1, lines - 1, 1), (2, 0, -1)):

                @pl.when(z == at)
                def join():
                    self.first[along].arrive()
                    total = self.terms[far].astype(F32) + self.landed[3].astype(F32)
                    self.terms[far] = total.astype(BF)

                self.copies[2 * along].start(z == at)

        def finish(self, total):
            total[...] = self.terms[z].astype(F32)
            for at, (along, when) in enumerate(((1, z >= 1), (-1, z <= 2), (2, z >= 2), (-2, z <= 1))):

                @pl.when(when)
                def add():
                    self.copies[along].arrive()
                    total[...] += self.landed[min(at, 2)].astype(F32)

            return total[...]

    class Canvases:
        def __init__(self, buffer, sems):
            self.near = [
                Copy(
                    buffer.at[dp],
                    buffer.at[dp],
                    buffer.at[device(step)[0]],
                    sems,
                    k,
                    device(step),
                )
                for k, step in enumerate(((1, 0, 0), (0, 1, 0), (1, 1, 0)))
            ]
            self.far = []
            for along in range(1, lines):
                back = (z + lines - along) % lines
                mine = buffer.at[pl.ds(4 * z, 4)]
                self.far.append(
                    Copy(
                        mine,
                        mine,
                        buffer.at[pl.ds(4 * back, 4)],
                        sems,
                        2 + along,
                        device(here, along),
                    )
                )

        def start(self):
            for copy in self.near:
                copy.start()

        def middle(self):
            for copy in self.near:
                copy.arrive()
            for copy in self.far:
                copy.start()

        def finish(self):
            for copy in self.far:
                copy.arrive()

    def each_canvas(body, near=True, before=None, after=None):
        def step(t, carry):
            for k, action in (before or {}).items():
                pl.when(t == k)(action)
            turn = t if near else 3 - t
            body(2 * ((x + (turn // 2)) % 2) + (c + turn) % 2)
            for k, action in (after or {}).items():
                pl.when(t == k)(action)
            return carry

        lax.fori_loop(0, 4, step, 0)

    def slots(t):
        return pl.ds(2 * t, 2)

    lane = lax.broadcasted_iota(jnp.int32, (1, lanes), 1)
    first_head = lane < lanes // 2
    first_part = (lane % 16) < 8

    def per_head(pair):
        return jnp.where(first_head, pair[0], pair[1])

    def head_sums(value):
        left = jnp.where(first_head, value, 0.0)
        right = jnp.where(first_head, 0.0, value)
        return (
            jnp.sum(left, axis=-1, keepdims=True),
            jnp.sum(right, axis=-1, keepdims=True),
        )

    def partner(value):
        return jnp.where(
            first_part, pltpu.roll(value, lanes - 8, 1), pltpu.roll(value, 8, 1)
        )

    barrier = pltpu.get_barrier_semaphore()
    partners = [device(step) for step in PLANE] + [device(here, k) for k in range(1, lines)]
    for target in partners:
        pl.semaphore_signal(barrier, inc=1, device_id=target, device_id_type=MESH)
    ids = s.ids
    ids[me] = jnp.zeros(ids.shape[1:], jnp.int32)
    ids[me, 0:1, :] = crop_ref[...]
    ids[me, 1:3, :] = pos_ref[0]
    conds = s.conds
    conds[dp] = jnp.zeros(conds.shape[1:], F32)
    for r in range(cond_ref.shape[1] // 128):
        conds[dp, r : r + 1, :] = cond_ref[:, 128 * r : 128 * (r + 1)].astype(F32)
    s.tokens[me] = x_ref[...]
    s.cots[me] = cot_ref[...]
    s.out_line[z] = out_ref[...]
    s.down_line[z] = down_ref[...]
    mod_full = s.mod_full
    mod_full[...] = jnp.zeros(mod_full.shape, BF)
    mod_full[0:mod_rows, 0:width] = amod_ref[...]
    mod_full[0:mod_rows, width : 2 * width] = fmod_ref[...]

    size = lanes // 2
    qkv_places = [
        (m, (2 * part + k) * size, part * width + (8 * (m % 2) + 4 * k + m // 2) * size)
        for m in range(8)
        for part in range(3)
        for k in range(2)
    ]
    up_places = [
        (m, (lines * part + k) * down_rows, part * 8 * hidden + (8 * k + m) * down_rows)
        for m in range(8)
        for part in range(2)
        for k in range(lines)
    ]
    for m, own, whole in qkv_places:
        s.qkv_cols[m, :, own : own + size] = qkv_ref[:, whole : whole + size]
    for m, own, whole in up_places:
        s.up_cols[m, :, own : own + down_rows] = up_ref[:, whole : whole + down_rows]
    pl.semaphore_wait(barrier, len(partners))

    cond_copy = Canvases(conds, s.sem_cond)
    ids_copy = Share(ids, s.sem_ids)
    qkv_spread = Spread(s.qkv_cols, s.qkv_line.at[z], s.sem_qkv_spread)
    up_spread = Spread(s.up_cols, s.up_line.at[z], s.sem_up_spread)
    qkv_line = [
        Relay(s.qkv_line.at[:, pl.ds(4 * k, 4)], s.sem_qkv_line.at[k]) for k in range(2)
    ]
    out_line = Relay(s.out_line, s.sem_out_line)
    up_line = [Relay(s.up_line.at[:, pl.ds(4 * k, 4)], s.sem_up_line.at[k]) for k in range(2)]
    down_line = Relay(s.down_line, s.sem_down_line)
    token_copy = Gather(s.tokens, s.sem_tokens)
    cot_copy = Gather(s.cots, s.sem_cots)
    cond_copy.start()
    qkv_spread.start()
    token_copy.start()
    cond_copy.middle()
    out_line.start()
    qkv_spread.finish()
    qkv_line[0].start()
    cond_copy.finish()
    picked = jnp.zeros((conds.shape[0], 128), F32)
    for r in range(cond_ref.shape[1] // 128):
        at_row = lax.broadcasted_iota(jnp.int32, (128, 128), 0) + 128 * r
        at_col = lax.broadcasted_iota(jnp.int32, (128, 128), 1)
        choose = (at_row == at_col + mod_rows * device_index) & (at_col < mod_rows)
        picked = picked + dot(
            conds[:, r, :].astype(BF), jnp.where(choose, 1.0, 0.0).astype(BF)
        )
    cond_mine = picked.astype(BF)
    block_cols = 2 * width // 8
    mod_terms, mod_in = s.mod_terms, s.mod_in
    for m in range(8):
        mod_terms[m] = dot(cond_mine, mod_full[:, block_cols * m : block_cols * (m + 1)])
    mod_spread = Spread(mod_terms, mod_in, s.sem_mod_spread)
    mod_spread.start()
    token_copy.turn()
    mod_spread.finish()
    mod_sum = mod_in[0]
    for m in range(1, 8):
        mod_sum = mod_sum + mod_in[m]
    mod_line = s.mod_line
    mod_line[z] = mod_sum
    mod_copy = Line(mod_line, s.sem_mod_line)
    mod_copy.start()
    qkv_line[1].start()
    up_spread.start()
    ids_copy.start()
    qkv_line[0].middle()
    mod_copy.finish()
    mod_sum = mod_line[0]
    for k in range(1, lines):
        mod_sum = mod_sum + mod_line[k]
    s.mod_total[...] = 1.0 + mod_sum
    mod_share = Share(s.mods, s.sem_mods)
    own_rows = s.mod_total[pl.ds(8 * (z // 2), 8), :]
    s.mods[me] = own_rows
    mod_share.start()
    cot_copy.start()
    out_line.middle()
    mod_share.finish()
    scales = s.scales
    for m in range(8):
        scales[:, block_cols * m : block_cols * (m + 1)] = s.mods[m]

    def scale_row(canvas, ffn):
        row = scales[pl.ds(4 * (z % 2) + canvas, 1), :]
        return row[:, width:] if ffn else row[:, :width]

    own_canvas = 2 * x + c

    def inverse_rms(value):
        return lax.rsqrt(jnp.mean(value * value, axis=-1, keepdims=True) + eps_norm)

    normed = s.normed

    def norm_tokens(canvas):
        value = s.tokens[slots(canvas)].reshape(canvas_rows, width).astype(F32)
        scaled = value * inverse_rms(value) * scale_row(canvas, False)
        normed[slots(canvas)] = scaled.astype(BF).reshape(2, rows, width)

    each_canvas(norm_tokens, before=token_copy.steps())
    qkv_line[1].middle()
    up_spread.finish()
    for line in up_line:
        line.start()
    out_line.finish()
    out_half = s.out_half
    half_copy = Copy(
        s.out_line.at[pl.ds(2 * (1 - y), 2)],
        out_half,
        out_half,
        s.sem_half,
        0,
        device((0, 0, 1)),
    )
    half_copy.start()
    cot_copy.turn()
    ids_copy.finish()
    for line in qkv_line:
        line.finish()
    head_of = lambda k: 8 * y + 4 * k + 2 * x + c
    head_scales = [scale_ref[head_of(k)] for k in range(2)]
    scale_lanes = per_head(head_scales)
    root_lanes = jnp.sqrt(scale_lanes)

    def canvas_ids(canvas, row):
        return jnp.concatenate(
            [ids[2 * canvas, row : row + 1, :], ids[2 * canvas + 1, row : row + 1, :]], axis=1
        )

    def one_hot(row, count):
        return jnp.where(
            lax.broadcasted_iota(jnp.int32, (count, canvas_rows), 0) == row, 1.0, 0.0
        ).astype(BF)

    def attend(canvas):
        qkv = dot(
            normed[slots(canvas)].reshape(canvas_rows, width),
            s.qkv_line[...].reshape(width, own_cols),
        )
        places = [one_hot(canvas_ids(canvas, 1), 16), one_hot(canvas_ids(canvas, 2), 16)]
        turn = dot(jnp.concatenate(places + places, axis=0), table_ref[me], 0, 0)
        s.turns[canvas] = turn
        cosine, sine = turn[:, :lanes], turn[:, lanes:]
        rotated = []
        for part in range(2):
            raw = qkv[:, part * lanes : (part + 1) * lanes]
            s.raw[canvas, part] = raw
            sums = head_sums(raw * raw)
            factor = per_head([lax.rsqrt(value + eps_cosine) for value in sums]) * root_lanes
            turned = raw * factor
            turned = (turned * cosine + partner(turned) * sine).astype(BF)
            s.rotated[canvas, part] = turned
            rotated.append(turned)
        values = qkv[:, 2 * lanes :].astype(BF)
        s.rotated[canvas, 2] = values
        crop_hot = one_hot(canvas_ids(canvas, 0), crops)
        allowed = dot(crop_hot, crop_hot, 0, 0)
        heads = []
        for k in range(2):
            mine = first_head if k == 0 else jnp.logical_not(first_head)
            query = jnp.where(mine, rotated[0], jnp.zeros_like(rotated[0]))
            weights = jnp.exp(dot(query, rotated[1], 1, 1)) * allowed
            probs = weights / jnp.sum(weights, axis=-1, keepdims=True)
            s.probs[canvas, k] = probs
            heads.append(dot(probs.astype(BF), values))
        attended = per_head(heads)
        s.raw_attended[canvas] = attended
        attended = attended.astype(BF)
        s.attended[canvas] = attended
        value = dot(attended, out_full[...].reshape(lanes, width))
        s.mid_part[slots(canvas)] = value.astype(BF).reshape(2, rows, width)

    half_copy.arrive()
    out_full = s.out_full
    for k in range(2):
        out_full[k, y] = s.out_line[2 * y + k]
        out_full[k, 1 - y] = out_half[k]

    mid_reduce = Reduce(
        s.mid_part, s.mid_pair, s.mid_far, s.mid_chip, s.sem_mid
    )
    each_canvas(attend, False, after=mid_reduce.steps())
    mid_reduce.middle()
    cot_copy.finish()
    up_line[0].middle()
    middle = x_ref[...].astype(F32) + mid_reduce.finish()
    s.middle[...] = middle
    ffn_row = scale_row(own_canvas, True)
    s.ffn[me] = (middle * inverse_rms(middle) * ffn_row).astype(BF)
    ffn_copy = Gather(s.ffn, s.sem_ffn)
    ffn_copy.start()
    ffn_copy.turn()
    up_line[1].middle()
    down_line.start()
    for line in up_line:
        line.finish()

    def feed(canvas):
        up = dot(
            s.ffn[slots(canvas)].reshape(canvas_rows, width),
            s.up_line[...].reshape(width, 2 * hidden),
        )
        value, gate = up[:, :hidden], up[:, hidden:]
        cdf = 0.5 + 0.5 * erf(gate * math.sqrt(0.5))
        act = gate * cdf
        s.hidden[canvas] = (value * act).astype(BF)
        s.act[canvas] = act
        density = jnp.exp(-0.5 * gate * gate) * (1.0 / math.sqrt(2.0 * math.pi))
        s.slope[canvas] = value * (cdf + gate * density)

    each_canvas(feed, before=ffn_copy.steps())
    down_line.middle()

    def cots_of(canvas):
        return s.cots[slots(canvas)].reshape(canvas_rows, width)

    all_rows = 8 * rows
    chunk = 256

    def down_term(n, carry):
        cols = pl.ds(pl.multiple_of(n * chunk, chunk), chunk)
        term = dot(
            s.hidden[...].reshape(all_rows, hidden),
            s.cots[:, :, cols].reshape(all_rows, chunk),
            0,
            0,
        )
        s.down_term[:, :, cols] = term.astype(BF).reshape(lines, down_rows, chunk)
        return carry

    lax.fori_loop(0, width // chunk, down_term, 0)
    down_fold = Fold(s.down_term, s.down_in, s.sem_down_fold)
    down_fold.start()
    down_line.finish()

    def feed_back(canvas):
        grad_hidden = dot(cots_of(canvas), s.down_line[...].reshape(hidden, width), 1, 1)
        grad_up = jnp.concatenate(
            [grad_hidden * s.act[canvas], grad_hidden * s.slope[canvas]], axis=1
        ).astype(BF)
        s.grad_up[canvas] = grad_up
        part = dot(grad_up, s.up_line[...].reshape(width, 2 * hidden), 1, 1)
        s.gnf_part[slots(canvas)] = part.astype(BF).reshape(2, rows, width)

    gnf_reduce = Reduce(
        s.gnf_part, s.gnf_pair, s.gnf_far, s.gnf_chip, s.sem_gnf
    )
    each_canvas(feed_back, False, after=gnf_reduce.steps())
    gnf_reduce.middle()

    def up_term(k, carry):
        cols = pl.ds(pl.multiple_of(k * 8 * up_rows, 8 * up_rows), 8 * up_rows)
        term = dot(
            s.ffn[:, :, cols].reshape(all_rows, 8 * up_rows),
            s.grad_up[...].reshape(all_rows, 2 * hidden),
            0,
            0,
        )
        s.up_term[k] = term.astype(BF).reshape(8, up_rows, 2 * hidden)
        return carry

    lax.fori_loop(0, lines, up_term, 0)
    up_fold = Fold(s.up_term, s.up_in, s.sem_up_fold)
    up_fold.start()
    down_fold.middle()

    def norm_back(value, row, grad):
        inverse = inverse_rms(value)
        scaled = grad * row
        along = jnp.mean(scaled * value, axis=-1, keepdims=True)
        grad_value = inverse * scaled - value * (inverse * inverse * inverse) * along
        return grad_value, jnp.sum(grad * value * inverse, axis=0, keepdims=True)

    def put_row(target, offset, row):
        for r in range(width // 128):
            target[offset + r : offset + r + 1, :] = row[:, 128 * r : 128 * (r + 1)]

    grad_mid, ffn_sum = norm_back(s.middle[...], ffn_row, gnf_reduce.finish())
    grad_middle = cot_ref[...].astype(F32) + grad_mid
    s.grad_middle[...] = grad_middle
    s.branch[me] = grad_middle.astype(BF)
    branch_copy = Gather(s.branch, s.sem_branch)
    branch_copy.start()
    sums_own = s.sums_own
    put_row(sums_own, 8, ffn_sum)

    def to_out(canvas):
        part = dot(s.hidden[canvas], s.down_line[...].reshape(hidden, width))
        s.out_part[slots(canvas)] = part.astype(BF).reshape(2, rows, width)

    out_reduce = Reduce(
        s.out_part, s.out_pair, s.out_far, s.out_chip, s.sem_out
    )
    branch_copy.turn()
    each_canvas(to_out)
    branch_copy.finish()
    out_reduce.give_far()
    out_reduce.give_near()

    def attend_back(canvas):
        branch = s.branch[slots(canvas)].reshape(canvas_rows, width)
        grad_att = dot(branch, out_full[...].reshape(lanes, width), 1, 1).astype(BF)
        turn = s.turns[canvas]
        cosine, sine = turn[:, :lanes], turn[:, lanes:]
        query, key, values = (s.rotated[canvas, part] for part in range(3))
        deltas = head_sums(grad_att.astype(F32) * s.raw_attended[canvas])
        grads = [[], [], []]
        for k in range(2):
            mine = first_head if k == 0 else jnp.logical_not(first_head)
            probs = s.probs[canvas, k]
            one_head = jnp.where(mine, grad_att, jnp.zeros_like(grad_att))
            dotted = dot(one_head, values, 1, 1)
            slope = (probs * (dotted - deltas[k])).astype(BF)
            grads[0].append(dot(slope, key))
            grads[1].append(dot(slope, query, 0, 0))
            grads[2].append(dot(probs.astype(BF), grad_att, 0, 0))
        pieces = []
        for part in range(2):
            grad = per_head(grads[part])
            grad = grad * cosine - partner(grad) * sine
            raw = s.raw[canvas, part]
            squares = [value + eps_cosine for value in head_sums(raw * raw)]
            along = head_sums(grad * raw)
            inverse = [lax.rsqrt(value) for value in squares]
            factor = per_head(inverse) * root_lanes
            shrink = per_head([along[k] * inverse[k] * inverse[k] for k in range(2)])
            pieces.append(factor * grad - raw * factor * shrink)
            term = per_head([jnp.sum(along[k] * inverse[k], axis=0, keepdims=True) for k in range(2)])
            s.head_terms[...] += term * root_lanes / (2.0 * scale_lanes)
        pieces.append(per_head(grads[2]))
        grad_qkv = jnp.concatenate(pieces, axis=1).astype(BF)
        s.grad_qkv[canvas] = grad_qkv
        part = dot(grad_qkv, s.qkv_line[...].reshape(width, own_cols), 1, 1)
        s.gna_part[slots(canvas)] = part.astype(BF).reshape(2, rows, width)

    term = dot(
        s.attended[...].reshape(all_rows, lanes),
        s.branch[...].reshape(all_rows, width),
        0,
        0,
    ).astype(BF).reshape(2, 2, half_head, width)
    halves = s.out_halves
    for k in range(2):
        for half in range(2):
            halves[half, k] = term[k, half]
    swap = Copy(
        halves.at[1 - y], s.out_swap, s.out_swap, s.sem_half, 1, device((0, 0, 1))
    )
    swap.start()

    s.head_terms[...] = jnp.zeros((1, lanes), F32)
    gna_reduce = Reduce(
        s.gna_part, s.gna_pair, s.gna_far, s.gna_chip, s.sem_gna
    )
    each_canvas(attend_back, False, after=gna_reduce.steps())
    up_fold.middle()
    out_reduce.send_far()
    out_reduce.send_near()
    gna_reduce.middle()

    swap.arrive()
    out_terms = s.out_terms
    for k in range(2):
        out_terms[2 * y + k] = halves[y, k]
        out_terms[2 * (1 - y) + k] = s.out_swap[k]
    out_fold = Fold(out_terms, s.out_in, s.sem_out_fold)
    out_fold.start()
    def qkv_term(k, carry):
        cols = pl.ds(pl.multiple_of(k * 8 * up_rows, 8 * up_rows), 8 * up_rows)
        term = dot(
            normed[:, :, cols].reshape(all_rows, 8 * up_rows),
            s.grad_qkv[...].reshape(all_rows, own_cols),
            0,
            0,
        )
        s.qkv_term[k] = term.astype(BF).reshape(8, up_rows, own_cols)
        return carry

    lax.fori_loop(0, lines, qkv_term, 0)
    qkv_fold = Fold(s.qkv_term, s.qkv_in, s.sem_qkv_fold)
    qkv_fold.start()

    grad_in, attn_sum = norm_back(x_ref[...].astype(F32), scale_row(own_canvas, False), gna_reduce.finish())
    input_grad[...] = s.grad_middle[...] + grad_in
    put_row(sums_own, 0, attn_sum)
    head_rows = lax.broadcasted_iota(jnp.int32, (8, lanes), 0)
    head_lane = lax.broadcasted_iota(jnp.int32, (8, lanes), 1)
    head_tile = jnp.zeros((8, lanes), F32)
    for k in range(2):
        value = jnp.sum(
            jnp.where(lane == k * (lanes // 2), s.head_terms[...], 0.0), axis=1, keepdims=True
        )
        head_tile = head_tile + jnp.where(
            (head_rows == 0) & (head_lane == head_of(k)), value, 0.0
        )
    sums_own[16:24, :] = head_tile
    sums_copy = Copy(
        sums_own, s.sums_pair, s.sums_pair, s.sem_half, 2, device((0, 0, 1))
    )
    sums_copy.start()
    out_reduce.middle()
    qkv_fold.middle()
    sums_copy.arrive()
    sums = s.sums
    sums[dp] = sums_own[...] + s.sums_pair[...]
    all_sums = Canvases(sums, s.sem_sums)
    all_sums.start()
    down_grad[...] = down_fold.finish(s.down_total).reshape(down_rows, width)
    all_sums.middle()
    out_fold.middle()
    block_out[...] = (s.middle[...] + out_reduce.finish()).astype(BF)
    s.up_sum[...] = up_fold.finish(s.up_total).astype(BF)
    up_return = Spread(s.up_sum, s.up_back, s.sem_up_back)
    up_return.start()
    up_return.finish()
    for m, own, whole in up_places:
        up_grad[:, whole : whole + down_rows] = s.up_back[m, :, own : own + down_rows].astype(F32)
    s.qkv_sum[...] = qkv_fold.finish(s.qkv_total).astype(BF)
    qkv_return = Spread(s.qkv_sum, s.qkv_back, s.sem_qkv_back)
    qkv_return.start()

    all_sums.finish()
    rounded = [
        jnp.concatenate([sums[:, offset + r, :] for r in range(width // 128)], axis=1).astype(BF)
        for offset in (0, 8)
    ]
    mine_for = dot(rounded[0], mod_full[:, :width], 1, 1) + dot(
        rounded[1], mod_full[:, width:], 1, 1
    )
    cond_line, cond_in = s.cond_line, s.cond_in
    s.cond_all[...] = mine_for
    for k in range(lines):
        cond_line[k] = s.cond_all[8 * (k // 2) : 8 * (k // 2) + 8, :]
    cond_send = [
        Copy(
            cond_line.at[(z + along) % lines],
            cond_in.at[me, z],
            cond_in.at[me, (z + lines - along) % lines],
            s.sem_cond_line,
            along - 1,
            device(here, along),
        )
        for along in range(1, lines)
    ]
    for copy in cond_send:
        copy.start()
    cond_in[me, z] = cond_line[z]
    amod_grad[...] = dot(cond_mine, rounded[0], 0, 0)[:mod_rows]
    fmod_grad[...] = dot(cond_mine, rounded[1], 0, 0)[:mod_rows]
    head_sum = sums[0, 16:17, :]
    for k in range(1, sums.shape[0]):
        head_sum = head_sum + sums[k, 16:17, :]
    scale_grad[...] = head_sum[:, : scale_grad.shape[1]]
    for copy in cond_send:
        copy.arrive()
    cond_share = Share(cond_in, s.sem_cond_share)
    cond_share.start()
    out_grad[...] = out_fold.finish(s.out_total)
    qkv_return.finish()
    for m, own, whole in qkv_places:
        qkv_grad[:, whole : whole + size] = s.qkv_back[m, :, own : own + size].astype(F32)
    cond_share.finish()
    for k in range(lines):
        for m in range(8):
            at_row = 8 * k + m
            row = cond_in[m, k, pl.ds(4 * (z % 2) + own_canvas, 1), :]
            cond_grad[:, at_row * mod_rows : (at_row + 1) * mod_rows] = row[:, :mod_rows]
    for copy, when in sends:
        if when is None:
            copy.wait_send()
        else:
            pl.when(when)(copy.wait_send)


def scratch_plan(lines, x_ref, qkv_ref, up_ref, out_ref, down_ref):
    rows, width = x_ref.shape
    up_rows = up_ref.shape[0]
    own_cols, up_cols = qkv_ref.shape[1] // 8, up_ref.shape[1] // 8
    hidden = up_cols // 2
    half_head = out_ref.shape[0]
    down_rows = down_ref.shape[0]
    lanes = own_cols // 3
    groups = 4 * lines
    plane = (8, rows, width)
    vm = lambda shape, kind=BF: pltpu.VMEM(shape, kind)
    sem = lambda count: pltpu.SemaphoreType.DMA((2, count))
    plan = dict(
        ids=vm((8, 8, rows), jnp.int32),
        conds=vm((groups, 8, 128), F32),
        tokens=vm(plane),
        cots=vm(plane),
        normed=vm(plane),
        ffn=vm(plane),
        branch=vm(plane),
        qkv_cols=vm((8, up_rows, own_cols)),
        up_cols=vm((8, up_rows, up_cols)),
        qkv_line=vm((lines, 8, up_rows, own_cols)),
        up_line=vm((lines, 8, up_rows, up_cols)),
        out_line=vm((lines, half_head, width)),
        down_line=vm((lines, down_rows, width)),
        out_half=vm((2, half_head, width)),
        out_full=vm((2, 2, half_head, width)),
        mod_full=vm((128, 2 * width)),
        mod_terms=vm((8, groups, width // 4), F32),
        mod_in=vm((8, groups, width // 4), F32),
        mod_line=vm((lines, groups, width // 4), F32),
        mod_total=vm((groups, width // 4), F32),
        mods=vm((8, 8, width // 4), F32),
        scales=vm((8, 2 * width), F32),
        turns=vm((4, 2 * rows, 2 * lanes), F32),
        raw=vm((4, 2, 2 * rows, lanes), F32),
        rotated=vm((4, 3, 2 * rows, lanes)),
        probs=vm((4, 2, 2 * rows, 2 * rows), F32),
        raw_attended=vm((4, 2 * rows, lanes), F32),
        attended=vm((4, 2 * rows, lanes)),
        middle=vm((rows, width), F32),
        grad_middle=vm((rows, width), F32),
        hidden=vm((4, 2 * rows, hidden)),
        act=vm((4, 2 * rows, hidden), F32),
        slope=vm((4, 2 * rows, hidden), F32),
        grad_up=vm((4, 2 * rows, up_cols)),
        grad_qkv=vm((4, 2 * rows, own_cols)),
        head_terms=vm((1, lanes), F32),
        sums_own=vm((24, 128), F32),
        sums_pair=vm((24, 128), F32),
        sums=vm((groups, 24, 128), F32),
        cond_all=vm((groups, 128), F32),
        cond_line=vm((lines, 8, 128), F32),
        cond_in=vm((8, lines, 8, 128), F32),
        down_total=vm((down_rows, width), F32),
        up_total=vm((8, up_rows, up_cols), F32),
        qkv_total=vm((8, up_rows, own_cols), F32),
        out_total=vm((half_head, width), F32),
        down_term=vm((lines, down_rows, width)),
        down_in=vm((4, down_rows, width)),
        up_term=vm((lines, 8, up_rows, up_cols)),
        up_in=vm((4, 8, up_rows, up_cols)),
        up_sum=vm((8, up_rows, up_cols)),
        up_back=vm((8, up_rows, up_cols)),
        qkv_term=vm((lines, 8, up_rows, own_cols)),
        qkv_in=vm((4, 8, up_rows, own_cols)),
        qkv_sum=vm((8, up_rows, own_cols)),
        qkv_back=vm((8, up_rows, own_cols)),
        out_halves=vm((2, 2, half_head, width)),
        out_swap=vm((2, half_head, width)),
        out_terms=vm((lines, half_head, width)),
        out_in=vm((4, half_head, width)),
    )
    for name in ("mid", "gnf", "out", "gna"):
        plan[name + "_part"] = vm(plane)
        plan[name + "_pair"] = vm((4, rows, width))
        plan[name + "_far"] = vm((2, rows // 2, width))
        plan[name + "_chip"] = vm((2, rows, width))
        plan["sem_" + name] = sem(10)
    plan.update(
        sem_tokens=sem(10),
        sem_cots=sem(10),
        sem_ffn=sem(10),
        sem_branch=sem(10),
        sem_ids=sem(7),
        sem_qkv_spread=sem(7),
        sem_up_spread=sem(7),
        sem_mod_spread=sem(7),
        sem_mods=sem(7),
        sem_up_back=sem(7),
        sem_qkv_back=sem(7),
        sem_cond_share=sem(7),
        sem_qkv_line=pltpu.SemaphoreType.DMA((2, 2, 5)),
        sem_up_line=pltpu.SemaphoreType.DMA((2, 2, 5)),
        sem_out_line=sem(5),
        sem_down_line=sem(5),
        sem_mod_line=sem(lines - 1),
        sem_cond_line=sem(lines - 1),
        sem_down_fold=sem(5),
        sem_up_fold=sem(5),
        sem_qkv_fold=sem(5),
        sem_out_fold=sem(5),
        sem_cond=sem(lines + 2),
        sem_sums=sem(lines + 2),
        sem_half=sem(3),
    )
    return plan


def turn_tables(heads, lines):
    head_size = 64
    table = np.zeros((heads, 2, 16, 2, head_size), np.float64)
    for axis in range(2):
        for j in range(8):
            freq = math.pi * 10.0 ** ((j * heads + np.arange(heads)) / (8.0 * heads))
            unit = (2.0 * np.arange(16) + 1.0) / 16.0 - 1.0
            angle = freq[:, None].astype(np.float32) * unit[None, :].astype(np.float32)
            angle = angle.astype(np.float64)
            for half in range(2):
                at = axis * 16 + half * 8 + j
                table[:, axis, :, 0, at] = np.cos(angle)
                table[:, axis, :, 1, at] = np.sin(angle) * (1.0 if half else -1.0)
    table[:, 0, :, 0, 32:] = 1.0
    high = table.astype(ml_dtypes.bfloat16)
    low = (table - high.astype(np.float64)).astype(ml_dtypes.bfloat16)
    parts = []
    for term in (high, low):
        term = term.reshape(2, 2, 2, 2, 2, 16, 2, head_size)
        term = term.transpose(2, 3, 0, 4, 5, 6, 1, 7)
        parts.append(term.reshape(8, 32, 4 * head_size))
    return np.concatenate(parts, axis=1)


def plane_shards(
    block_in,
    conditioning,
    crop_ids,
    positions,
    qkv_weight,
    out_weight,
    up_weight,
    down_weight,
    attn_modulate,
    ffn_modulate,
    head_scale,
    cotangent,
):
    lines = lax.axis_size("dp") // 4
    rows, width = block_in.shape[1:]
    heads = head_scale.shape[0]
    tables = jnp.asarray(turn_tables(heads, lines))
    kinds = jax.ShapeDtypeStruct
    operands = (
        block_in[0],
        cotangent[0],
        qkv_weight,
        up_weight,
        out_weight,
        down_weight,
        attn_modulate,
        ffn_modulate,
        conditioning,
        crop_ids,
        positions,
        head_scale,
        tables,
    )
    plan = scratch_plan(lines, operands[0], qkv_weight, up_weight, out_weight, down_weight)
    in_vmem = pl.BlockSpec(memory_space=pltpu.VMEM)
    in_specs = [in_vmem] * len(operands)
    in_specs[11] = pl.BlockSpec(memory_space=pltpu.SMEM)
    results = pl.pallas_call(
        functools.partial(block_kernel, lines),
        out_shape=(
            kinds((rows, width), BF),
            kinds((rows, width), F32),
            kinds(conditioning.shape, F32),
            kinds(qkv_weight.shape, F32),
            kinds(out_weight.shape, F32),
            kinds(up_weight.shape, F32),
            kinds(down_weight.shape, F32),
            kinds(attn_modulate.shape, F32),
            kinds(ffn_modulate.shape, F32),
            kinds((1, heads), F32),
        ),
        in_specs=in_specs,
        out_specs=[in_vmem] * 10,
        scratch_shapes=list(plan.values()),
        compiler_params=pltpu.CompilerParams(
            collective_id=0, has_side_effects=True, vmem_limit_bytes=63 * 2**20
        ),
    )(*operands)
    results = settle(results)
    return tuple(item[None] for item in results[:2]) + tuple(results[2:-1]) + (results[-1][0],)


def settle(results):
    count = len(results)

    def kernel(*refs):
        copies = [
            pltpu.make_async_copy(refs[k], refs[count + k], refs[-1].at[k]) for k in range(count)
        ]
        for copy in copies:
            copy.start()
        for copy in copies:
            copy.wait()

    anywhere = pl.BlockSpec(memory_space=pl.ANY)
    return pl.pallas_call(
        kernel,
        out_shape=tuple(jax.ShapeDtypeStruct(item.shape, item.dtype) for item in results),
        in_specs=[pl.BlockSpec(memory_space=pltpu.VMEM)] * count,
        out_specs=[anywhere] * count,
        scratch_shapes=[pltpu.SemaphoreType.DMA((count,))],
    )(*results)


def in_planes(mesh):
    return mesh.shape["seq"] == 2 and mesh.shape["dp"] == 16


def solution(mesh):
    in_specs = (
        P("dp", "seq", None),
        P("dp", None),
        P("dp", "seq"),
        P("dp", None, "seq"),
        P(("dp", "seq"), None),
        P(("dp", "seq"), None),
        P(("dp", "seq"), None),
        P(("dp", "seq"), None),
        P(("dp", "seq"), None),
        P(("dp", "seq"), None),
        P(),
        P("dp", "seq", None),
    )
    out_specs = (
        P("dp", "seq", None),
        P("dp", "seq", None),
        P("dp", None),
        P(("dp", "seq"), None),
        P(("dp", "seq"), None),
        P(("dp", "seq"), None),
        P(("dp", "seq"), None),
        P(("dp", "seq"), None),
        P(("dp", "seq"), None),
        P(),
    )
    body = plane_shards if in_planes(mesh) else shards
    return jax.shard_map(body, mesh=mesh, in_specs=in_specs, out_specs=out_specs, check_vma=False)
```

```python
import functools
import math
import types

import jax
import jax.numpy as jnp
import ml_dtypes
import numpy as np
from jax import lax
from jax.experimental import pallas as pl
from jax.experimental.pallas import tpu as pltpu
from jax.sharding import PartitionSpec as P

eps_norm = 1e-06
eps_cosine = 1e-06
negative = -1e30
key_rows = 256


def block_split(count, limit):
    size_rows = math.gcd(count, limit)
    return (size_rows, count // size_rows)


def rope_tables(positions, heads):
    unit_pos = (2.0 * positions.astype(jnp.float32) + 1.0) / 16.0 - 1.0
    exponent = (
        jnp.arange(8, dtype=jnp.float32)[None, :] * heads
        + jnp.arange(heads, dtype=jnp.float32)[:, None]
    ) / (8.0 * heads)
    frequency = math.pi * 10.0**exponent
    angles = jnp.moveaxis(unit_pos[..., None, None] * frequency, -4, -2)
    return (jnp.cos(angles), jnp.sin(angles))


def rotate(vector, cosine, sine):
    leading = vector.shape[:-1]
    turned_part = vector[..., :32].reshape(leading + (2, 2, 8))
    first_half = turned_part[..., 0, :]
    second_half = turned_part[..., 1, :]
    turned = jnp.stack(
        [first_half * cosine - second_half * sine, first_half * sine + second_half * cosine],
        axis=-2,
    )
    return jnp.concatenate([turned.reshape(leading + (32,)), vector[..., 32:]], axis=-1)


def norm_forward(value, scale):
    inverse = lax.rsqrt(jnp.mean(value * value, axis=-1, keepdims=True) + eps_norm)
    return (value * inverse * scale[:, None], inverse)


def norm_backward(value, inverse, scale, grad_norm):
    scaled = grad_norm * scale[:, None]
    grad_value = inverse * scaled - value * inverse**3 * jnp.mean(
        scaled * value, axis=-1, keepdims=True
    )
    grad_scale = jnp.sum(grad_norm * value * inverse, axis=1)
    return (grad_value, grad_scale)


def cosine_forward(value, root_scale):
    factor = root_scale[:, None] * lax.rsqrt(
        jnp.sum(value * value, axis=-1, keepdims=True) + eps_cosine
    )
    return (value * factor, factor)


def cosine_backward(value, factor, grad):
    squares = jnp.sum(value * value, axis=-1, keepdims=True) + eps_cosine
    along = jnp.sum(grad * value, axis=-1, keepdims=True)
    grad_value = factor * grad - value * factor * along / squares
    return (grad_value, jnp.sum(along * factor, axis=(0, 1, 3)))


def geglu(value_part, gate_part):
    return value_part * jax.nn.gelu(gate_part, approximate=False)


def pair_grads(queries, grad_att, log_total, deltas, query_crop, key_block, value_block, key_crop):
    scores = jnp.einsum("cqhd,ckhd->cqhk", queries, key_block, preferred_element_type=jnp.float32)
    allowed = (query_crop[:, :, None] == key_crop[:, None, :])[:, :, None, :]
    probs = jnp.exp(jnp.where(allowed, scores - log_total[..., None], negative))
    probs = jnp.where(allowed, probs, 0.0)
    dotted = jnp.einsum(
        "cqhd,ckhd->cqhk", grad_att, value_block, preferred_element_type=jnp.float32
    )
    slope = (probs * (dotted - deltas[..., None])).astype(jnp.bfloat16)
    grad_q = jnp.einsum("cqhk,ckhd->cqhd", slope, key_block, preferred_element_type=jnp.float32)
    grad_k = jnp.einsum("cqhk,cqhd->ckhd", slope, queries, preferred_element_type=jnp.float32)
    grad_v = jnp.einsum(
        "cqhk,cqhd->ckhd", probs.astype(jnp.bfloat16), grad_att, preferred_element_type=jnp.float32
    )
    return (grad_q, grad_k, grad_v)


def pack_terms(terms, lead_shape):
    return jnp.concatenate([term.reshape(lead_shape + (-1,)) for term in terms], axis=-1)


def unpack_terms(packed_row, terms, owners):
    results = []
    offset = 0
    for term in terms:
        own_rows = term.shape[0] // owners
        count = own_rows * term.shape[1]
        results.append(packed_row[offset : offset + count].reshape(own_rows, term.shape[1]))
        offset = offset + count
    return results


def shards(
    block_in,
    conditioning,
    crop_ids,
    positions,
    qkv_weight,
    out_weight,
    up_weight,
    down_weight,
    attn_modulate,
    ffn_modulate,
    head_scale,
    cotangent,
):
    qkv_full, out_full, up_full, down_full, attn_mod, ffn_mod = (
        lax.all_gather(qkv_weight, ("dp", "seq"), axis=0, tiled=True),
        lax.all_gather(out_weight, ("dp", "seq"), axis=0, tiled=True),
        lax.all_gather(up_weight, ("dp", "seq"), axis=0, tiled=True),
        lax.all_gather(down_weight, ("dp", "seq"), axis=0, tiled=True),
        lax.all_gather(attn_modulate, ("dp", "seq"), axis=0, tiled=True),
        lax.all_gather(ffn_modulate, ("dp", "seq"), axis=0, tiled=True),
    )
    canvases, rows, width = block_in.shape
    heads = head_scale.shape[0]
    head_size = width // heads
    hidden_width = down_full.shape[0]
    seq_count = lax.axis_size("seq")
    inputs = block_in.astype(jnp.float32)
    scale_attn = 1.0 + jnp.dot(conditioning, attn_mod, preferred_element_type=jnp.float32)
    scale_ffn = 1.0 + jnp.dot(conditioning, ffn_mod, preferred_element_type=jnp.float32)
    normed_attn, inverse_attn = norm_forward(inputs, scale_attn)
    normed_attn = normed_attn.astype(jnp.bfloat16)
    qkv_all = jnp.einsum(
        "csd,de->cse", normed_attn, qkv_full, preferred_element_type=jnp.float32
    ).reshape(canvases, rows, 3, heads, head_size)
    root_scale = jnp.sqrt(head_scale)
    query_cos, query_factor = cosine_forward(qkv_all[:, :, 0], root_scale)
    key_cos, key_factor = cosine_forward(qkv_all[:, :, 1], root_scale)
    cosine, sine = rope_tables(positions, heads)
    queries = rotate(query_cos, cosine, sine).astype(jnp.bfloat16)
    keys_flat = rotate(key_cos, cosine, sine).astype(jnp.bfloat16).reshape(canvases, rows, width)
    values_flat = qkv_all[:, :, 2].astype(jnp.bfloat16).reshape(canvases, rows, width)
    start_state = (
        jnp.full((canvases, rows, heads), negative, jnp.float32),
        jnp.zeros((canvases, rows, heads), jnp.float32),
        jnp.zeros((canvases, rows, heads, head_size), jnp.float32),
    )
    state_now = start_state
    piece_keys = lax.all_gather(keys_flat, "seq", axis=1, tiled=True)
    piece_values = lax.all_gather(values_flat, "seq", axis=1, tiled=True)
    piece_crop = lax.all_gather(crop_ids, "seq", axis=1, tiled=True)
    size_rows, number = block_split(piece_keys.shape[1], key_rows)

    def step_block(state, block_index):
        running_max, row_total, weighted = state
        offset = block_index * size_rows
        key_block = lax.dynamic_slice_in_dim(piece_keys, offset, size_rows, 1).reshape(
            canvases, size_rows, heads, head_size
        )
        value_block = lax.dynamic_slice_in_dim(piece_values, offset, size_rows, 1).reshape(
            canvases, size_rows, heads, head_size
        )
        crop_block = lax.dynamic_slice_in_dim(piece_crop, offset, size_rows, 1)
        scores = jnp.einsum(
            "cqhd,ckhd->cqhk", queries, key_block, preferred_element_type=jnp.float32
        )
        allowed = (crop_ids[:, :, None] == crop_block[:, None, :])[:, :, None, :]
        scores = jnp.where(allowed, scores, negative)
        new_max = jnp.maximum(running_max, jnp.max(scores, axis=-1))
        weights = jnp.where(allowed, jnp.exp(scores - new_max[..., None]), 0.0)
        shrink = jnp.exp(running_max - new_max)
        row_total = row_total * shrink + jnp.sum(weights, axis=-1)
        weighted = weighted * shrink[..., None] + jnp.einsum(
            "cqhk,ckhd->cqhd",
            weights.astype(jnp.bfloat16),
            value_block,
            preferred_element_type=jnp.float32,
        )
        return ((new_max, row_total, weighted), None)

    state_now, unused = lax.scan(step_block, state_now, jnp.arange(number))
    running_max, row_total, weighted = state_now
    log_total = running_max + jnp.log(row_total)
    attended_raw = weighted / row_total[..., None]
    attended = attended_raw.astype(jnp.bfloat16).reshape(canvases, rows, width)
    middle = inputs + jnp.einsum(
        "csd,de->cse", attended, out_full, preferred_element_type=jnp.float32
    )
    normed_ffn, inverse_ffn = norm_forward(middle, scale_ffn)
    normed_ffn = normed_ffn.astype(jnp.bfloat16)
    up_all = jnp.einsum("csd,de->cse", normed_ffn, up_full, preferred_element_type=jnp.float32)
    value_part = up_all[..., :hidden_width]
    gate_part = up_all[..., hidden_width:]
    hidden = geglu(value_part, gate_part).astype(jnp.bfloat16)
    block_out = (
        middle + jnp.einsum("csf,fd->csd", hidden, down_full, preferred_element_type=jnp.float32)
    ).astype(jnp.bfloat16)
    down_term = jnp.einsum("csf,csd->fd", hidden, cotangent, preferred_element_type=jnp.float32)
    grad_hidden = jnp.einsum(
        "csd,fd->csf", cotangent, down_full, preferred_element_type=jnp.float32
    )
    unused_value, geglu_pull = jax.vjp(geglu, value_part, gate_part)
    grad_value, grad_gate = geglu_pull(grad_hidden)
    grad_up = jnp.concatenate([grad_value, grad_gate], axis=-1).astype(jnp.bfloat16)
    up_term = jnp.einsum("csd,cse->de", normed_ffn, grad_up, preferred_element_type=jnp.float32)
    grad_normed_ffn = jnp.einsum(
        "cse,de->csd", grad_up, up_full, preferred_element_type=jnp.float32
    )
    grad_mid_norm, ffn_scale_sum = norm_backward(middle, inverse_ffn, scale_ffn, grad_normed_ffn)
    grad_middle = cotangent.astype(jnp.float32) + grad_mid_norm
    grad_branch = grad_middle.astype(jnp.bfloat16)
    out_term = jnp.einsum("csd,cse->de", attended, grad_branch, preferred_element_type=jnp.float32)
    grad_attended = (
        jnp.einsum("cse,de->csd", grad_branch, out_full, preferred_element_type=jnp.float32)
        .astype(jnp.bfloat16)
        .reshape(canvases, rows, heads, head_size)
    )
    deltas = jnp.sum(grad_attended.astype(jnp.float32) * attended_raw, axis=-1)
    start_back = (
        jnp.zeros((canvases, rows, heads, head_size), jnp.float32),
        jnp.zeros((canvases, rows * seq_count, 2 * width), jnp.float32),
    )
    state_now = start_back
    fold_piece_keys = lax.all_gather(keys_flat, "seq", axis=1, tiled=True)
    fold_piece_values = lax.all_gather(values_flat, "seq", axis=1, tiled=True)
    fold_piece_crop = lax.all_gather(crop_ids, "seq", axis=1, tiled=True)
    fold_size_rows, number = block_split(fold_piece_keys.shape[1], key_rows)

    def step_block(state, block_index):
        grad_q_sum, grad_kv_all = state
        offset = block_index * fold_size_rows
        key_block = lax.dynamic_slice_in_dim(fold_piece_keys, offset, fold_size_rows, 1).reshape(
            canvases, fold_size_rows, heads, head_size
        )
        value_block = lax.dynamic_slice_in_dim(
            fold_piece_values, offset, fold_size_rows, 1
        ).reshape(canvases, fold_size_rows, heads, head_size)
        crop_block = lax.dynamic_slice_in_dim(fold_piece_crop, offset, fold_size_rows, 1)
        grad_q, grad_k, grad_v = pair_grads(
            queries, grad_attended, log_total, deltas, crop_ids, key_block, value_block, crop_block
        )
        update = jnp.concatenate(
            [
                grad_k.reshape(canvases, fold_size_rows, width),
                grad_v.reshape(canvases, fold_size_rows, width),
            ],
            axis=-1,
        )
        previous = lax.dynamic_slice_in_dim(grad_kv_all, offset, fold_size_rows, 1)
        grad_kv_all = lax.dynamic_update_slice_in_dim(grad_kv_all, previous + update, offset, 1)
        return ((grad_q_sum + grad_q, grad_kv_all), None)

    state_now, unused = lax.scan(step_block, state_now, jnp.arange(number))
    grad_queries, grad_kv_all = state_now
    grad_kv = lax.psum_scatter(
        grad_kv_all.astype(jnp.bfloat16), "seq", scatter_dimension=1, tiled=True
    ).astype(jnp.float32)
    grad_keys = grad_kv[..., :width].reshape(canvases, rows, heads, head_size)
    grad_values = grad_kv[..., width:].reshape(canvases, rows, heads, head_size)
    grad_query_cos = rotate(grad_queries, cosine, -sine)
    grad_key_cos = rotate(grad_keys, cosine, -sine)
    grad_query_raw, query_part = cosine_backward(qkv_all[:, :, 0], query_factor, grad_query_cos)
    grad_key_raw, key_part = cosine_backward(qkv_all[:, :, 1], key_factor, grad_key_cos)
    scale_local = (query_part + key_part) / (2.0 * head_scale)
    grad_qkv = (
        jnp.stack([grad_query_raw, grad_key_raw, grad_values], axis=2)
        .astype(jnp.bfloat16)
        .reshape(canvases, rows, 3 * width)
    )
    qkv_term = jnp.einsum("csd,cse->de", normed_attn, grad_qkv, preferred_element_type=jnp.float32)
    grad_normed_attn = jnp.einsum(
        "cse,de->csd", grad_qkv, qkv_full, preferred_element_type=jnp.float32
    )
    grad_in_norm, attn_scale_sum = norm_backward(inputs, inverse_attn, scale_attn, grad_normed_attn)
    input_grad = grad_middle + grad_in_norm
    attn_sums, ffn_sums = lax.psum((attn_scale_sum, ffn_scale_sum), "seq")
    attn_sums = attn_sums.astype(jnp.bfloat16)
    ffn_sums = ffn_sums.astype(jnp.bfloat16)
    cond_grad = jnp.einsum(
        "cd,nd->cn", attn_sums, attn_mod, preferred_element_type=jnp.float32
    ) + jnp.einsum("cd,nd->cn", ffn_sums, ffn_mod, preferred_element_type=jnp.float32)
    leader = lax.axis_index("seq") == 0
    attn_mod_term = jnp.where(
        leader,
        jnp.einsum("cn,cd->nd", conditioning, attn_sums, preferred_element_type=jnp.float32),
        0.0,
    )
    ffn_mod_term = jnp.where(
        leader,
        jnp.einsum("cn,cd->nd", conditioning, ffn_sums, preferred_element_type=jnp.float32),
        0.0,
    )
    terms = (qkv_term, out_term, up_term, down_term, attn_mod_term, ffn_mod_term)
    groups = lax.axis_size("dp")
    owners = groups * seq_count
    packed = pack_terms(terms, (owners,))
    summed = lax.psum_scatter(packed, ("dp", "seq"), scatter_dimension=0, tiled=True)
    packed_row = summed[0]
    qkv_grad, out_grad, up_grad, down_grad, attnmod_grad, ffnmod_grad = unpack_terms(
        packed_row, terms, owners
    )
    scale_grad = lax.psum(scale_local, ("dp", "seq"))
    return (
        block_out,
        input_grad,
        cond_grad,
        qkv_grad,
        out_grad,
        up_grad,
        down_grad,
        attnmod_grad,
        ffnmod_grad,
        scale_grad,
    )


MESH = pl.DeviceIdType.MESH
BF = jnp.bfloat16
F32 = jnp.float32
PLANE = ((1, 0, 0), (0, 0, 1), (1, 0, 1), (0, 1, 0), (1, 1, 0), (0, 1, 1), (1, 1, 1))
SAME_Y = tuple(
    (step, along)
    for along in (1, 3, 2, 0)
    for step in ((0, 0, 0), (1, 0, 0), (0, 1, 0), (1, 1, 0))
    if along or step != (0, 0, 0)
)
TO_X, TO_Y, TO_FAR = (1, 0, 0), (0, 0, 1), (1, 0, 1)
ERF_P = (
    0.00022905065861350646,
    0.0034082910107109506,
    0.050955695062380861,
    0.18520832239976145,
    1.128379143519084,
)
ERF_Q = (
    -1.1791602954361697e-7,
    0.000023547966471313185,
    0.0010179625278914885,
    0.014070470171167667,
    0.11098505178285362,
    0.49746925110067538,
    1.0,
)


def erf(value):
    value = jnp.clip(value, -3.832506856900711, 3.832506856900711)
    square = value * value
    top = jnp.full_like(value, ERF_P[0])
    for term in ERF_P[1:]:
        top = top * square + term
    bottom = jnp.full_like(value, ERF_Q[0])
    for term in ERF_Q[1:]:
        bottom = bottom * square + term
    return value * top / bottom


def dot(lhs, rhs, on_lhs=1, on_rhs=0):
    return lax.dot_general(
        lhs, rhs, (((on_lhs,), (on_rhs,)), ((), ())), preferred_element_type=F32
    )


def block_kernel(
    lines,
    x_ref,
    cot_ref,
    qkv_ref,
    up_ref,
    out_ref,
    down_ref,
    amod_ref,
    fmod_ref,
    cond_ref,
    crop_ref,
    pos_ref,
    scale_ref,
    table_ref,
    block_out,
    input_grad,
    cond_grad,
    qkv_grad,
    out_grad,
    up_grad,
    down_grad,
    amod_grad,
    fmod_grad,
    scale_grad,
    *scratch,
):
    names = list(scratch_plan(lines, x_ref, qkv_ref, up_ref, out_ref, down_ref))
    s = types.SimpleNamespace(**dict(zip(names, scratch)))
    dp = lax.axis_index("dp")
    y = lax.axis_index("seq")
    z = dp // 4
    x = (dp // 2) % 2
    c = dp % 2
    rows, width = x_ref.shape
    up_rows = up_ref.shape[0]
    own_cols = qkv_ref.shape[1] // 8
    lanes = own_cols // 3
    half_head = out_ref.shape[0]
    hidden = up_ref.shape[1] // 16
    down_rows = down_ref.shape[0]
    mod_rows = amod_ref.shape[0]
    canvas_rows = 2 * rows
    crops = canvas_rows // 16
    me = 4 * x + 2 * c + y
    device_index = 8 * z + me

    def member(step):
        return 4 * ((x + step[0]) % 2) + 2 * ((c + step[1]) % 2) + (y + step[2]) % 2

    def device(step, along=0):
        return (
            ((z + along) % lines) * 4 + ((x + step[0]) % 2) * 2 + (c + step[1]) % 2,
            (y + step[2]) % 2,
        )

    def line_device(along):
        return (jnp.clip(z + along, 0, lines - 1) * 4 + dp % 4, y)

    def inside(along):
        return z + along < lines if along > 0 else z + along >= 0

    here = (0, 0, 0)
    core = (0, 1, 0)
    sends = []

    class Copy:
        def __init__(self, src, dst_there, dst_here, sems, at, target):
            self.out = pltpu.make_async_remote_copy(
                src_ref=src,
                dst_ref=dst_there,
                send_sem=sems.at[0, at],
                recv_sem=sems.at[1, at],
                device_id=target,
                device_id_type=MESH,
            )
            self.into = pltpu.make_async_remote_copy(
                src_ref=src,
                dst_ref=dst_here,
                send_sem=sems.at[0, at],
                recv_sem=sems.at[1, at],
                device_id=target,
                device_id_type=MESH,
            )

        def start(self, when=None):
            if when is None:
                self.out.start()
            else:
                pl.when(when)(self.out.start)
            sends.append((self.out, when))

        def arrive(self):
            self.into.wait_recv()

    class Gather:
        def __init__(self, buffer, sems):
            at = lambda step: buffer.at[member(step)]
            half = buffer.shape[1] // 2
            rows_of = (pl.ds(0, half), pl.ds(half, half))
            part = lambda step, k: buffer.at[member(step), rows_of[k]]
            self.x_own = [
                Copy(part(here, k), part(here, k), part(TO_X, k), sems, k, device(TO_X))
                for k in range(2)
            ]
            self.y_own = [
                Copy(part(here, k), part(here, k), part(TO_Y, k), sems, 2 + k, device(TO_Y))
                for k in range(2)
            ]
            self.y_far = Copy(part(TO_X, 0), part(TO_X, 0), part(TO_FAR, 0), sems, 4, device(TO_Y))
            self.x_far = Copy(part(TO_Y, 1), part(TO_Y, 1), part(TO_FAR, 1), sems, 5, device(TO_X))
            self.pair = Copy(at(here), at(here), at(core), sems, 6, device(core))
            self.cross = [
                Copy(at(step), at(step), at((step[0], 1, step[2])), sems, 7 + k, device(core))
                for k, step in enumerate((TO_X, TO_Y, TO_FAR))
            ]

        def start(self):
            self.x_own[0].start()
            self.y_own[1].start()
            self.x_own[1].start()
            self.y_own[0].start()
            self.pair.start()

        def turn(self):
            self.x_own[0].arrive()
            self.y_far.start()
            self.y_own[1].arrive()
            self.x_far.start()

        def near(self):
            self.y_own[0].arrive()
            self.cross[1].start()
            self.x_own[1].arrive()
            self.cross[0].start()

        def far(self):
            self.y_far.arrive()
            self.x_far.arrive()
            self.cross[2].start()

        def pair_near(self):
            self.pair.arrive()
            self.cross[1].arrive()

        def pair_far(self):
            self.cross[0].arrive()
            self.cross[2].arrive()

        def finish(self):
            self.near()
            self.far()
            self.pair_near()
            self.pair_far()

        def steps(self):
            return {0: self.near, 1: self.pair_near, 2: self.far, 3: self.pair_far}

    class Reduce:
        def __init__(self, part, pair_in, far_in, chip_in, sems):
            self.part, self.pair_in, self.far_in, self.chip_in = part, pair_in, far_in, chip_in
            half = part.shape[1] // 2
            self.rows_of = rows_of = (pl.ds(0, half), pl.ds(half, half))
            self.steps_of = (here, TO_X, TO_Y, TO_FAR)
            self.pair = [
                Copy(
                    part.at[member((step[0], 1, step[2]))],
                    pair_in.at[k],
                    pair_in.at[k],
                    sems,
                    k,
                    device(core),
                )
                for k, step in enumerate(self.steps_of)
            ]
            piece = lambda step, k: part.at[member(step), rows_of[k]]
            self.x_far = Copy(piece(TO_FAR, 0), far_in.at[0], far_in.at[0], sems, 4, device(TO_X))
            self.y_far = Copy(piece(TO_FAR, 1), far_in.at[1], far_in.at[1], sems, 5, device(TO_Y))
            into = lambda way, k: chip_in.at[way, rows_of[k]]
            self.x_own = [
                Copy(piece(TO_X, k), into(0, k), into(0, k), sems, 6 + k, device(TO_X))
                for k in range(2)
            ]
            self.y_own = [
                Copy(piece(TO_Y, k), into(1, k), into(1, k), sems, 8 + k, device(TO_Y))
                for k in range(2)
            ]

        def add_pair(self, k):
            self.pair[k].arrive()
            slot = member(self.steps_of[k])
            total = self.part[slot].astype(F32) + self.pair_in[k].astype(F32)
            self.part[slot] = total.astype(BF)

        def add_far(self, step, k):
            slot = member(step)
            total = self.part[slot, self.rows_of[k], :].astype(F32) + self.far_in[k].astype(F32)
            self.part[slot, self.rows_of[k], :] = total.astype(BF)

        def give_far(self):
            self.pair[3].start()
            self.pair[1].start()

        def send_far(self):
            self.add_pair(3)
            self.x_far.start()
            self.y_far.start()
            self.add_pair(1)
            self.x_own[0].start()

        def give_near(self):
            self.pair[2].start()
            self.pair[0].start()

        def send_near(self):
            self.add_pair(2)
            self.y_own[1].start()

        def steps(self):
            return {0: self.give_far, 1: self.send_far, 2: self.give_near, 3: self.send_near}

        def middle(self):
            self.x_far.arrive()
            self.add_far(TO_Y, 0)
            self.y_own[0].start()
            self.y_far.arrive()
            self.add_far(TO_X, 1)
            self.x_own[1].start()

        def finish(self):
            self.pair[0].arrive()
            total = self.part[me].astype(F32) + self.pair_in[0].astype(F32)
            for copies in (self.x_own, self.y_own):
                for copy in copies:
                    copy.arrive()
            return total + self.chip_in[0].astype(F32) + self.chip_in[1].astype(F32)

    class Spread:
        def __init__(self, source, target, sems):
            self.source, self.target = source, target
            self.copies = [
                Copy(
                    source.at[member(step)],
                    target.at[me],
                    target.at[member(step)],
                    sems,
                    k,
                    device(step),
                )
                for k, step in enumerate(PLANE)
            ]

        def start(self):
            for copy in self.copies:
                copy.start()
            self.target[me] = self.source[me]

        def finish(self):
            for copy in self.copies:
                copy.arrive()

    class Share:
        def __init__(self, buffer, sems, block=None):
            self.copies = [
                Copy(
                    buffer.at[me] if block is None else block,
                    buffer.at[me],
                    buffer.at[member(step)],
                    sems,
                    k,
                    device(step),
                )
                for k, step in enumerate(PLANE)
            ]

        def start(self):
            for copy in self.copies:
                copy.start()

        def finish(self):
            for copy in self.copies:
                copy.arrive()

    class Line:
        def __init__(self, buffer, sems, first=None):
            self.copies = []
            for along in range(1, lines):
                back = (z + lines - along) % lines
                if first is None:
                    mine, theirs = buffer.at[z], buffer.at[back]
                else:
                    mine, theirs = buffer.at[pl.ds(first * z, first)], buffer.at[pl.ds(first * back, first)]
                self.copies.append(Copy(mine, mine, theirs, sems, along - 1, device(here, along)))

        def start(self):
            for copy in self.copies:
                copy.start()

        def finish(self):
            for copy in self.copies:
                copy.arrive()

    class Relay:
        def __init__(self, buffer, sems):
            self.copies = {
                along: Copy(
                    buffer.at[z],
                    buffer.at[z],
                    buffer.at[jnp.clip(z - along, 0, lines - 1)],
                    sems,
                    at,
                    line_device(along),
                )
                for at, along in enumerate((1, -1, 2, -2))
            }
            self.onward = {
                along: Copy(
                    buffer.at[far], buffer.at[far], buffer.at[far], sems, 4, line_device(along)
                )
                for along, far in ((1, 0), (-1, lines - 1))
            }

        def start(self, steps=(2, -2, 1, -1)):
            for along in steps:
                self.copies[along].start(inside(along))

        def middle(self):
            @pl.when(z == 2)
            def up_line():
                self.copies[2].arrive()

            @pl.when(z == 1)
            def down_line():
                self.copies[-2].arrive()

            self.onward[1].start(z == 2)
            self.onward[-1].start(z == 1)

        def finish(self):
            pl.when(z >= 1)(self.copies[1].arrive)
            pl.when(z <= 2)(self.copies[-1].arrive)
            pl.when(z == 3)(self.copies[2].arrive)
            pl.when(z == 0)(self.copies[-2].arrive)
            pl.when(z == 3)(self.onward[1].arrive)
            pl.when(z == 0)(self.onward[-1].arrive)

    class Fold:
        def __init__(self, terms, landed, sems):
            self.terms, self.landed = terms, landed
            self.copies = {
                along: Copy(
                    terms.at[jnp.clip(z + along, 0, lines - 1)],
                    landed.at[min(at, 2)],
                    landed.at[min(at, 2)],
                    sems,
                    at,
                    line_device(along),
                )
                for at, along in enumerate((1, -1, 2, -2))
            }
            self.first = {
                along: Copy(
                    terms.at[far], landed.at[3], landed.at[3], sems, 4, line_device(along)
                )
                for along, far in ((1, lines - 1), (-1, 0))
            }

        def start(self):
            self.first[1].start(z == 0)
            self.first[-1].start(z == lines - 1)
            self.copies[2].start(z == 0)
            self.copies[-2].start(z == lines - 1)
            for along in (1, -1):
                self.copies[along].start(inside(along))

        def middle(self):
            for at, far, along in ((1, lines - 1, 1), (2, 0, -1)):

                @pl.when(z == at)
                def join():
                    self.first[along].arrive()
                    total = self.terms[far].astype(F32) + self.landed[3].astype(F32)
                    self.terms[far] = total.astype(BF)

                self.copies[2 * along].start(z == at)

        def finish(self, total):
            total[...] = self.terms[z].astype(F32)
            for at, (along, when) in enumerate(((1, z >= 1), (-1, z <= 2), (2, z >= 2), (-2, z <= 1))):

                @pl.when(when)
                def add():
                    self.copies[along].arrive()
                    total[...] += self.landed[min(at, 2)].astype(F32)

            return total[...]

    class Canvases:
        def __init__(self, buffer, sems):
            self.copies = []
            for at, (step, along) in enumerate(SAME_Y):
                from_there = device(step, lines - along)[0]
                self.copies.append(
                    Copy(
                        buffer.at[dp],
                        buffer.at[dp],
                        buffer.at[from_there],
                        sems,
                        at,
                        device(step, along),
                    )
                )

        def start(self):
            for copy in self.copies:
                copy.start()

        def finish(self):
            for copy in self.copies:
                copy.arrive()

    def each_canvas(body, near=True, before=None, after=None):
        def step(t, carry):
            for k, action in (before or {}).items():
                pl.when(t == k)(action)
            turn = t if near else 3 - t
            body(2 * ((x + (turn // 2)) % 2) + (c + turn) % 2)
            for k, action in (after or {}).items():
                pl.when(t == k)(action)
            return carry

        lax.fori_loop(0, 4, step, 0)

    def slots(t):
        return pl.ds(2 * t, 2)

    lane = lax.broadcasted_iota(jnp.int32, (1, lanes), 1)
    first_head = lane < lanes // 2
    first_part = (lane % 16) < 8

    def per_head(pair):
        return jnp.where(first_head, pair[0], pair[1])

    def head_sums(value):
        left = jnp.where(first_head, value, 0.0)
        right = jnp.where(first_head, 0.0, value)
        return (
            jnp.sum(left, axis=-1, keepdims=True),
            jnp.sum(right, axis=-1, keepdims=True),
        )

    def partner(value):
        return jnp.where(
            first_part, pltpu.roll(value, lanes - 8, 1), pltpu.roll(value, 8, 1)
        )

    barrier = pltpu.get_barrier_semaphore()
    partners = [device(step) for step in PLANE if step[2]]
    partners += [device(step, along) for step, along in SAME_Y]
    for target in partners:
        pl.semaphore_signal(barrier, inc=1, device_id=target, device_id_type=MESH)
    ids = s.ids
    ids[me] = jnp.zeros(ids.shape[1:], jnp.int32)
    ids[me, 0:1, :] = crop_ref[...]
    ids[me, 1:3, :] = pos_ref[0]
    conds = s.conds
    conds[dp] = jnp.zeros(conds.shape[1:], F32)
    for r in range(cond_ref.shape[1] // 128):
        conds[dp, r : r + 1, :] = cond_ref[:, 128 * r : 128 * (r + 1)].astype(F32)
    s.tokens[me] = x_ref[...]
    s.cots[me] = cot_ref[...]
    s.out_line[z] = out_ref[...]
    s.down_line[z] = down_ref[...]
    mod_full = s.mod_full
    mod_full[...] = jnp.zeros(mod_full.shape, BF)
    mod_full[0:mod_rows, 0:width] = amod_ref[...]
    mod_full[0:mod_rows, width : 2 * width] = fmod_ref[...]

    size = lanes // 2
    qkv_places = [
        (m, (2 * part + k) * size, part * width + (8 * (m % 2) + 4 * k + m // 2) * size)
        for m in range(8)
        for part in range(3)
        for k in range(2)
    ]
    up_places = [
        (m, (lines * part + k) * down_rows, part * 8 * hidden + (8 * k + m) * down_rows)
        for m in range(8)
        for part in range(2)
        for k in range(lines)
    ]
    for m, own, whole in qkv_places:
        s.qkv_cols[m, :, own : own + size] = qkv_ref[:, whole : whole + size]
    for m, own, whole in up_places:
        s.up_cols[m, :, own : own + down_rows] = up_ref[:, whole : whole + down_rows]
    pl.semaphore_wait(barrier, len(partners))

    cond_copy = Canvases(conds, s.sem_cond)
    ids_copy = Share(ids, s.sem_ids)
    qkv_spread = Spread(s.qkv_cols, s.qkv_line.at[z], s.sem_qkv_spread)
    up_spread = Spread(s.up_cols, s.up_line.at[z], s.sem_up_spread)
    qkv_line = [
        Relay(s.qkv_line.at[:, pl.ds(4 * k, 4)], s.sem_qkv_line.at[k]) for k in range(2)
    ]
    out_line = Relay(s.out_line, s.sem_out_line)
    up_line = [Relay(s.up_line.at[:, pl.ds(4 * k, 4)], s.sem_up_line.at[k]) for k in range(2)]
    down_line = Relay(s.down_line, s.sem_down_line)
    token_copy = Gather(s.tokens, s.sem_tokens)
    cot_copy = Gather(s.cots, s.sem_cots)
    cond_copy.start()
    qkv_spread.start()
    token_copy.start()
    out_line.start()
    qkv_spread.finish()
    qkv_line[0].start()
    cond_copy.finish()
    picked = jnp.zeros((conds.shape[0], 128), F32)
    for r in range(cond_ref.shape[1] // 128):
        at_row = lax.broadcasted_iota(jnp.int32, (128, 128), 0) + 128 * r
        at_col = lax.broadcasted_iota(jnp.int32, (128, 128), 1)
        choose = (at_row == at_col + mod_rows * device_index) & (at_col < mod_rows)
        picked = picked + dot(
            conds[:, r, :].astype(BF), jnp.where(choose, 1.0, 0.0).astype(BF)
        )
    cond_mine = picked.astype(BF)
    block_cols = 2 * width // 8
    mod_terms, mod_in = s.mod_terms, s.mod_in
    for m in range(8):
        mod_terms[m] = dot(cond_mine, mod_full[:, block_cols * m : block_cols * (m + 1)])
    mod_spread = Spread(mod_terms, mod_in, s.sem_mod_spread)
    mod_spread.start()
    token_copy.turn()
    mod_spread.finish()
    mod_sum = mod_in[0]
    for m in range(1, 8):
        mod_sum = mod_sum + mod_in[m]
    mod_line = s.mod_line
    mod_line[z] = mod_sum
    mod_copy = Line(mod_line, s.sem_mod_line)
    mod_copy.start()
    qkv_line[1].start()
    up_spread.start()
    ids_copy.start()
    qkv_line[0].middle()
    mod_copy.finish()
    mod_sum = mod_line[0]
    for k in range(1, lines):
        mod_sum = mod_sum + mod_line[k]
    s.mod_total[...] = 1.0 + mod_sum
    mod_share = Share(s.mods, s.sem_mods)
    own_rows = s.mod_total[pl.ds(8 * (z // 2), 8), :]
    s.mods[me] = own_rows
    mod_share.start()
    cot_copy.start()
    out_line.middle()
    mod_share.finish()
    scales = s.scales
    for m in range(8):
        scales[:, block_cols * m : block_cols * (m + 1)] = s.mods[m]

    def scale_row(canvas, ffn):
        row = scales[pl.ds(4 * (z % 2) + canvas, 1), :]
        return row[:, width:] if ffn else row[:, :width]

    own_canvas = 2 * x + c

    def inverse_rms(value):
        return lax.rsqrt(jnp.mean(value * value, axis=-1, keepdims=True) + eps_norm)

    normed = s.normed

    def norm_tokens(canvas):
        value = s.tokens[slots(canvas)].reshape(canvas_rows, width).astype(F32)
        scaled = value * inverse_rms(value) * scale_row(canvas, False)
        normed[slots(canvas)] = scaled.astype(BF).reshape(2, rows, width)

    each_canvas(norm_tokens, before=token_copy.steps())
    qkv_line[1].middle()
    up_spread.finish()
    for line in up_line:
        line.start()
    out_line.finish()
    out_half = s.out_half
    half_copy = Copy(
        s.out_line.at[pl.ds(2 * (1 - y), 2)],
        out_half,
        out_half,
        s.sem_half,
        0,
        device((0, 0, 1)),
    )
    half_copy.start()
    cot_copy.turn()
    ids_copy.finish()
    for line in qkv_line:
        line.finish()
    head_of = lambda k: 8 * y + 4 * k + 2 * x + c
    head_scales = [scale_ref[head_of(k)] for k in range(2)]
    scale_lanes = per_head(head_scales)
    root_lanes = jnp.sqrt(scale_lanes)

    def canvas_ids(canvas, row):
        return jnp.concatenate(
            [ids[2 * canvas, row : row + 1, :], ids[2 * canvas + 1, row : row + 1, :]], axis=1
        )

    def one_hot(row, count):
        return jnp.where(
            lax.broadcasted_iota(jnp.int32, (count, canvas_rows), 0) == row, 1.0, 0.0
        ).astype(BF)

    def attend(canvas):
        qkv = dot(
            normed[slots(canvas)].reshape(canvas_rows, width),
            s.qkv_line[...].reshape(width, own_cols),
        )
        places = [one_hot(canvas_ids(canvas, 1), 16), one_hot(canvas_ids(canvas, 2), 16)]
        turn = dot(jnp.concatenate(places + places, axis=0), table_ref[me], 0, 0)
        s.turns[canvas] = turn
        cosine, sine = turn[:, :lanes], turn[:, lanes:]
        rotated = []
        for part in range(2):
            raw = qkv[:, part * lanes : (part + 1) * lanes]
            s.raw[canvas, part] = raw
            sums = head_sums(raw * raw)
            factor = per_head([lax.rsqrt(value + eps_cosine) for value in sums]) * root_lanes
            turned = raw * factor
            turned = (turned * cosine + partner(turned) * sine).astype(BF)
            s.rotated[canvas, part] = turned
            rotated.append(turned)
        values = qkv[:, 2 * lanes :].astype(BF)
        s.rotated[canvas, 2] = values
        crop_hot = one_hot(canvas_ids(canvas, 0), crops)
        allowed = dot(crop_hot, crop_hot, 0, 0)
        heads = []
        for k in range(2):
            mine = first_head if k == 0 else jnp.logical_not(first_head)
            query = jnp.where(mine, rotated[0], jnp.zeros_like(rotated[0]))
            weights = jnp.exp(dot(query, rotated[1], 1, 1)) * allowed
            probs = weights / jnp.sum(weights, axis=-1, keepdims=True)
            s.probs[canvas, k] = probs
            heads.append(dot(probs.astype(BF), values))
        attended = per_head(heads)
        s.raw_attended[canvas] = attended
        attended = attended.astype(BF)
        s.attended[canvas] = attended
        value = dot(attended, out_full[...].reshape(lanes, width))
        s.mid_part[slots(canvas)] = value.astype(BF).reshape(2, rows, width)

    half_copy.arrive()
    out_full = s.out_full
    for k in range(2):
        out_full[k, y] = s.out_line[2 * y + k]
        out_full[k, 1 - y] = out_half[k]

    mid_reduce = Reduce(
        s.mid_part, s.mid_pair, s.mid_far, s.mid_chip, s.sem_mid
    )
    each_canvas(attend, False, after=mid_reduce.steps())
    mid_reduce.middle()
    cot_copy.finish()
    up_line[0].middle()
    middle = x_ref[...].astype(F32) + mid_reduce.finish()
    s.middle[...] = middle
    ffn_row = scale_row(own_canvas, True)
    s.ffn[me] = (middle * inverse_rms(middle) * ffn_row).astype(BF)
    ffn_copy = Gather(s.ffn, s.sem_ffn)
    ffn_copy.start()
    ffn_copy.turn()
    up_line[1].middle()
    down_line.start()
    for line in up_line:
        line.finish()

    def feed(canvas):
        up = dot(
            s.ffn[slots(canvas)].reshape(canvas_rows, width),
            s.up_line[...].reshape(width, 2 * hidden),
        )
        value, gate = up[:, :hidden], up[:, hidden:]
        cdf = 0.5 + 0.5 * erf(gate * math.sqrt(0.5))
        act = gate * cdf
        s.hidden[canvas] = (value * act).astype(BF)
        s.act[canvas] = act
        density = jnp.exp(-0.5 * gate * gate) * (1.0 / math.sqrt(2.0 * math.pi))
        s.slope[canvas] = value * (cdf + gate * density)

    each_canvas(feed, before=ffn_copy.steps())
    down_line.middle()

    def cots_of(canvas):
        return s.cots[slots(canvas)].reshape(canvas_rows, width)

    all_rows = 8 * rows
    chunk = 256

    def down_term(n, carry):
        cols = pl.ds(pl.multiple_of(n * chunk, chunk), chunk)
        term = dot(
            s.hidden[...].reshape(all_rows, hidden),
            s.cots[:, :, cols].reshape(all_rows, chunk),
            0,
            0,
        )
        s.down_term[:, :, cols] = term.astype(BF).reshape(lines, down_rows, chunk)
        return carry

    lax.fori_loop(0, width // chunk, down_term, 0)
    down_fold = Fold(s.down_term, s.down_in, s.sem_down_fold)
    down_fold.start()
    down_line.finish()

    def feed_back(canvas):
        grad_hidden = dot(cots_of(canvas), s.down_line[...].reshape(hidden, width), 1, 1)
        grad_up = jnp.concatenate(
            [grad_hidden * s.act[canvas], grad_hidden * s.slope[canvas]], axis=1
        ).astype(BF)
        s.grad_up[canvas] = grad_up
        part = dot(grad_up, s.up_line[...].reshape(width, 2 * hidden), 1, 1)
        s.gnf_part[slots(canvas)] = part.astype(BF).reshape(2, rows, width)

    gnf_reduce = Reduce(
        s.gnf_part, s.gnf_pair, s.gnf_far, s.gnf_chip, s.sem_gnf
    )
    each_canvas(feed_back, False, after=gnf_reduce.steps())
    gnf_reduce.middle()

    def up_term(k, carry):
        cols = pl.ds(pl.multiple_of(k * 8 * up_rows, 8 * up_rows), 8 * up_rows)
        term = dot(
            s.ffn[:, :, cols].reshape(all_rows, 8 * up_rows),
            s.grad_up[...].reshape(all_rows, 2 * hidden),
            0,
            0,
        )
        s.up_term[k] = term.astype(BF).reshape(8, up_rows, 2 * hidden)
        return carry

    lax.fori_loop(0, lines, up_term, 0)
    up_fold = Fold(s.up_term, s.up_in, s.sem_up_fold)
    up_fold.start()
    down_fold.middle()

    def norm_back(value, row, grad):
        inverse = inverse_rms(value)
        scaled = grad * row
        along = jnp.mean(scaled * value, axis=-1, keepdims=True)
        grad_value = inverse * scaled - value * (inverse * inverse * inverse) * along
        return grad_value, jnp.sum(grad * value * inverse, axis=0, keepdims=True)

    def put_row(target, offset, row):
        for r in range(width // 128):
            target[offset + r : offset + r + 1, :] = row[:, 128 * r : 128 * (r + 1)]

    grad_mid, ffn_sum = norm_back(s.middle[...], ffn_row, gnf_reduce.finish())
    grad_middle = cot_ref[...].astype(F32) + grad_mid
    s.grad_middle[...] = grad_middle
    s.branch[me] = grad_middle.astype(BF)
    branch_copy = Gather(s.branch, s.sem_branch)
    branch_copy.start()
    sums_own = s.sums_own
    put_row(sums_own, 8, ffn_sum)

    def to_out(canvas):
        part = dot(s.hidden[canvas], s.down_line[...].reshape(hidden, width))
        s.out_part[slots(canvas)] = part.astype(BF).reshape(2, rows, width)

    out_reduce = Reduce(
        s.out_part, s.out_pair, s.out_far, s.out_chip, s.sem_out
    )
    branch_copy.turn()
    each_canvas(to_out)
    branch_copy.finish()
    out_reduce.give_far()
    out_reduce.give_near()

    def attend_back(canvas):
        branch = s.branch[slots(canvas)].reshape(canvas_rows, width)
        grad_att = dot(branch, out_full[...].reshape(lanes, width), 1, 1).astype(BF)
        turn = s.turns[canvas]
        cosine, sine = turn[:, :lanes], turn[:, lanes:]
        query, key, values = (s.rotated[canvas, part] for part in range(3))
        deltas = head_sums(grad_att.astype(F32) * s.raw_attended[canvas])
        grads = [[], [], []]
        for k in range(2):
            mine = first_head if k == 0 else jnp.logical_not(first_head)
            probs = s.probs[canvas, k]
            one_head = jnp.where(mine, grad_att, jnp.zeros_like(grad_att))
            dotted = dot(one_head, values, 1, 1)
            slope = (probs * (dotted - deltas[k])).astype(BF)
            grads[0].append(dot(slope, key))
            grads[1].append(dot(slope, query, 0, 0))
            grads[2].append(dot(probs.astype(BF), grad_att, 0, 0))
        pieces = []
        for part in range(2):
            grad = per_head(grads[part])
            grad = grad * cosine - partner(grad) * sine
            raw = s.raw[canvas, part]
            squares = [value + eps_cosine for value in head_sums(raw * raw)]
            along = head_sums(grad * raw)
            inverse = [lax.rsqrt(value) for value in squares]
            factor = per_head(inverse) * root_lanes
            shrink = per_head([along[k] * inverse[k] * inverse[k] for k in range(2)])
            pieces.append(factor * grad - raw * factor * shrink)
            term = per_head([jnp.sum(along[k] * inverse[k], axis=0, keepdims=True) for k in range(2)])
            s.head_terms[...] += term * root_lanes / (2.0 * scale_lanes)
        pieces.append(per_head(grads[2]))
        grad_qkv = jnp.concatenate(pieces, axis=1).astype(BF)
        s.grad_qkv[canvas] = grad_qkv
        part = dot(grad_qkv, s.qkv_line[...].reshape(width, own_cols), 1, 1)
        s.gna_part[slots(canvas)] = part.astype(BF).reshape(2, rows, width)

    term = dot(
        s.attended[...].reshape(all_rows, lanes),
        s.branch[...].reshape(all_rows, width),
        0,
        0,
    ).astype(BF).reshape(2, 2, half_head, width)
    halves = s.out_halves
    for k in range(2):
        for half in range(2):
            halves[half, k] = term[k, half]
    swap = Copy(
        halves.at[1 - y], s.out_swap, s.out_swap, s.sem_half, 1, device((0, 0, 1))
    )
    swap.start()

    s.head_terms[...] = jnp.zeros((1, lanes), F32)
    gna_reduce = Reduce(
        s.gna_part, s.gna_pair, s.gna_far, s.gna_chip, s.sem_gna
    )
    each_canvas(attend_back, False, after=gna_reduce.steps())
    up_fold.middle()
    out_reduce.send_far()
    out_reduce.send_near()
    gna_reduce.middle()

    swap.arrive()
    out_terms = s.out_terms
    for k in range(2):
        out_terms[2 * y + k] = halves[y, k]
        out_terms[2 * (1 - y) + k] = s.out_swap[k]
    out_fold = Fold(out_terms, s.out_in, s.sem_out_fold)
    out_fold.start()
    def qkv_term(k, carry):
        cols = pl.ds(pl.multiple_of(k * 8 * up_rows, 8 * up_rows), 8 * up_rows)
        term = dot(
            normed[:, :, cols].reshape(all_rows, 8 * up_rows),
            s.grad_qkv[...].reshape(all_rows, own_cols),
            0,
            0,
        )
        s.qkv_term[k] = term.astype(BF).reshape(8, up_rows, own_cols)
        return carry

    lax.fori_loop(0, lines, qkv_term, 0)
    cuts = (pl.ds(0, 6), pl.ds(6, 2))
    qkv_fold = [
        Fold(s.qkv_term.at[:, cut], s.qkv_in.at[:, cut], s.sem_qkv_fold.at[k])
        for k, cut in enumerate(cuts)
    ]
    qkv_fold[0].start()

    grad_in, attn_sum = norm_back(x_ref[...].astype(F32), scale_row(own_canvas, False), gna_reduce.finish())
    input_grad[...] = s.grad_middle[...] + grad_in
    put_row(sums_own, 0, attn_sum)
    head_rows = lax.broadcasted_iota(jnp.int32, (8, lanes), 0)
    head_lane = lax.broadcasted_iota(jnp.int32, (8, lanes), 1)
    head_tile = jnp.zeros((8, lanes), F32)
    for k in range(2):
        value = jnp.sum(
            jnp.where(lane == k * (lanes // 2), s.head_terms[...], 0.0), axis=1, keepdims=True
        )
        head_tile = head_tile + jnp.where(
            (head_rows == 0) & (head_lane == head_of(k)), value, 0.0
        )
    sums_own[16:24, :] = head_tile
    s.sums_plane[me] = sums_own[...]
    sums_share = Share(s.sums_plane, s.sem_sums_share)
    sums_share.start()
    out_reduce.middle()
    out_fold.middle()
    sums_share.finish()
    sums = s.sums
    for k in range(4):
        sums[4 * z + k] = s.sums_plane[2 * k] + s.sums_plane[2 * k + 1]
    all_sums = Line(sums, s.sem_sums, 4)
    all_sums.start()
    qkv_fold[1].start()
    qkv_fold[0].middle()
    down_grad[...] = down_fold.finish(s.down_total).reshape(down_rows, width)
    block_out[...] = (s.middle[...] + out_reduce.finish()).astype(BF)
    s.up_sum[...] = up_fold.finish(s.up_total).astype(BF)
    up_return = Spread(s.up_sum, s.up_back, s.sem_up_back)
    up_return.start()
    up_return.finish()
    for m, own, whole in up_places:
        up_grad[:, whole : whole + down_rows] = s.up_back[m, :, own : own + down_rows].astype(F32)
    qkv_fold[1].middle()
    for fold, cut in zip(qkv_fold, cuts):
        s.qkv_sum[cut] = fold.finish(s.qkv_total.at[cut]).astype(BF)
    qkv_return = Spread(s.qkv_sum, s.qkv_back, s.sem_qkv_back)
    qkv_return.start()

    all_sums.finish()
    rounded = [
        jnp.concatenate([sums[:, offset + r, :] for r in range(width // 128)], axis=1).astype(BF)
        for offset in (0, 8)
    ]
    mine_for = dot(rounded[0], mod_full[:, :width], 1, 1) + dot(
        rounded[1], mod_full[:, width:], 1, 1
    )
    cond_line, cond_in = s.cond_line, s.cond_in
    s.cond_all[...] = mine_for
    for k in range(lines):
        cond_line[k] = s.cond_all[8 * (k // 2) : 8 * (k // 2) + 8, :]
    cond_send = [
        Copy(
            cond_line.at[(z + along) % lines],
            cond_in.at[me, z],
            cond_in.at[me, (z + lines - along) % lines],
            s.sem_cond_line,
            along - 1,
            device(here, along),
        )
        for along in range(1, lines)
    ]
    for copy in cond_send:
        copy.start()
    cond_in[me, z] = cond_line[z]
    amod_grad[...] = dot(cond_mine, rounded[0], 0, 0)[:mod_rows]
    fmod_grad[...] = dot(cond_mine, rounded[1], 0, 0)[:mod_rows]
    head_sum = sums[0, 16:17, :]
    for k in range(1, sums.shape[0]):
        head_sum = head_sum + sums[k, 16:17, :]
    scale_grad[...] = head_sum[:, : scale_grad.shape[1]]
    for copy in cond_send:
        copy.arrive()
    cond_share = Share(cond_in, s.sem_cond_share)
    cond_share.start()
    out_grad[...] = out_fold.finish(s.out_total)
    qkv_return.finish()
    for m, own, whole in qkv_places:
        qkv_grad[:, whole : whole + size] = s.qkv_back[m, :, own : own + size].astype(F32)
    cond_share.finish()
    for k in range(lines):
        for m in range(8):
            at_row = 8 * k + m
            row = cond_in[m, k, pl.ds(4 * (z % 2) + own_canvas, 1), :]
            cond_grad[:, at_row * mod_rows : (at_row + 1) * mod_rows] = row[:, :mod_rows]
    for copy, when in sends:
        if when is None:
            copy.wait_send()
        else:
            pl.when(when)(copy.wait_send)


def scratch_plan(lines, x_ref, qkv_ref, up_ref, out_ref, down_ref):
    rows, width = x_ref.shape
    up_rows = up_ref.shape[0]
    own_cols, up_cols = qkv_ref.shape[1] // 8, up_ref.shape[1] // 8
    hidden = up_cols // 2
    half_head = out_ref.shape[0]
    down_rows = down_ref.shape[0]
    lanes = own_cols // 3
    groups = 4 * lines
    plane = (8, rows, width)
    vm = lambda shape, kind=BF: pltpu.VMEM(shape, kind)
    sem = lambda count: pltpu.SemaphoreType.DMA((2, count))
    plan = dict(
        ids=vm((8, 8, rows), jnp.int32),
        conds=vm((groups, 8, 128), F32),
        tokens=vm(plane),
        cots=vm(plane),
        normed=vm(plane),
        ffn=vm(plane),
        branch=vm(plane),
        qkv_cols=vm((8, up_rows, own_cols)),
        up_cols=vm((8, up_rows, up_cols)),
        qkv_line=vm((lines, 8, up_rows, own_cols)),
        up_line=vm((lines, 8, up_rows, up_cols)),
        out_line=vm((lines, half_head, width)),
        down_line=vm((lines, down_rows, width)),
        out_half=vm((2, half_head, width)),
        out_full=vm((2, 2, half_head, width)),
        mod_full=vm((128, 2 * width)),
        mod_terms=vm((8, groups, width // 4), F32),
        mod_in=vm((8, groups, width // 4), F32),
        mod_line=vm((lines, groups, width // 4), F32),
        mod_total=vm((groups, width // 4), F32),
        mods=vm((8, 8, width // 4), F32),
        scales=vm((8, 2 * width), F32),
        turns=vm((4, 2 * rows, 2 * lanes), F32),
        raw=vm((4, 2, 2 * rows, lanes), F32),
        rotated=vm((4, 3, 2 * rows, lanes)),
        probs=vm((4, 2, 2 * rows, 2 * rows), F32),
        raw_attended=vm((4, 2 * rows, lanes), F32),
        attended=vm((4, 2 * rows, lanes)),
        middle=vm((rows, width), F32),
        grad_middle=vm((rows, width), F32),
        hidden=vm((4, 2 * rows, hidden)),
        act=vm((4, 2 * rows, hidden), F32),
        slope=vm((4, 2 * rows, hidden), F32),
        grad_up=vm((4, 2 * rows, up_cols)),
        grad_qkv=vm((4, 2 * rows, own_cols)),
        head_terms=vm((1, lanes), F32),
        sums_own=vm((24, 128), F32),
        sums_plane=vm((8, 24, 128), F32),
        sums=vm((groups, 24, 128), F32),
        cond_all=vm((groups, 128), F32),
        cond_line=vm((lines, 8, 128), F32),
        cond_in=vm((8, lines, 8, 128), F32),
        down_total=vm((down_rows, width), F32),
        up_total=vm((8, up_rows, up_cols), F32),
        qkv_total=vm((8, up_rows, own_cols), F32),
        out_total=vm((half_head, width), F32),
        down_term=vm((lines, down_rows, width)),
        down_in=vm((4, down_rows, width)),
        up_term=vm((lines, 8, up_rows, up_cols)),
        up_in=vm((4, 8, up_rows, up_cols)),
        up_sum=vm((8, up_rows, up_cols)),
        up_back=vm((8, up_rows, up_cols)),
        qkv_term=vm((lines, 8, up_rows, own_cols)),
        qkv_in=vm((4, 8, up_rows, own_cols)),
        qkv_sum=vm((8, up_rows, own_cols)),
        qkv_back=vm((8, up_rows, own_cols)),
        out_halves=vm((2, 2, half_head, width)),
        out_swap=vm((2, half_head, width)),
        out_terms=vm((lines, half_head, width)),
        out_in=vm((4, half_head, width)),
    )
    for name in ("mid", "gnf", "out", "gna"):
        plan[name + "_part"] = vm(plane)
        plan[name + "_pair"] = vm((4, rows, width))
        plan[name + "_far"] = vm((2, rows // 2, width))
        plan[name + "_chip"] = vm((2, rows, width))
        plan["sem_" + name] = sem(10)
    plan.update(
        sem_tokens=sem(10),
        sem_cots=sem(10),
        sem_ffn=sem(10),
        sem_branch=sem(10),
        sem_ids=sem(7),
        sem_qkv_spread=sem(7),
        sem_up_spread=sem(7),
        sem_mod_spread=sem(7),
        sem_mods=sem(7),
        sem_up_back=sem(7),
        sem_qkv_back=sem(7),
        sem_cond_share=sem(7),
        sem_qkv_line=pltpu.SemaphoreType.DMA((2, 2, 5)),
        sem_up_line=pltpu.SemaphoreType.DMA((2, 2, 5)),
        sem_out_line=sem(5),
        sem_down_line=sem(5),
        sem_mod_line=sem(lines - 1),
        sem_cond_line=sem(lines - 1),
        sem_down_fold=sem(5),
        sem_up_fold=sem(5),
        sem_qkv_fold=pltpu.SemaphoreType.DMA((2, 2, 5)),
        sem_out_fold=sem(5),
        sem_cond=sem(15),
        sem_sums=sem(lines - 1),
        sem_sums_share=sem(7),
        sem_half=sem(2),
    )
    return plan


def turn_tables(heads, lines):
    head_size = 64
    table = np.zeros((heads, 2, 16, 2, head_size), np.float64)
    for axis in range(2):
        for j in range(8):
            freq = math.pi * 10.0 ** ((j * heads + np.arange(heads)) / (8.0 * heads))
            unit = (2.0 * np.arange(16) + 1.0) / 16.0 - 1.0
            angle = freq[:, None].astype(np.float32) * unit[None, :].astype(np.float32)
            angle = angle.astype(np.float64)
            for half in range(2):
                at = axis * 16 + half * 8 + j
                table[:, axis, :, 0, at] = np.cos(angle)
                table[:, axis, :, 1, at] = np.sin(angle) * (1.0 if half else -1.0)
    table[:, 0, :, 0, 32:] = 1.0
    high = table.astype(ml_dtypes.bfloat16)
    low = (table - high.astype(np.float64)).astype(ml_dtypes.bfloat16)
    parts = []
    for term in (high, low):
        term = term.reshape(2, 2, 2, 2, 2, 16, 2, head_size)
        term = term.transpose(2, 3, 0, 4, 5, 6, 1, 7)
        parts.append(term.reshape(8, 32, 4 * head_size))
    return np.concatenate(parts, axis=1)


def plane_shards(
    block_in,
    conditioning,
    crop_ids,
    positions,
    qkv_weight,
    out_weight,
    up_weight,
    down_weight,
    attn_modulate,
    ffn_modulate,
    head_scale,
    cotangent,
):
    lines = lax.axis_size("dp") // 4
    rows, width = block_in.shape[1:]
    heads = head_scale.shape[0]
    tables = jnp.asarray(turn_tables(heads, lines))
    kinds = jax.ShapeDtypeStruct
    operands = (
        block_in[0],
        cotangent[0],
        qkv_weight,
        up_weight,
        out_weight,
        down_weight,
        attn_modulate,
        ffn_modulate,
        conditioning,
        crop_ids,
        positions,
        head_scale,
        tables,
    )
    plan = scratch_plan(lines, operands[0], qkv_weight, up_weight, out_weight, down_weight)
    in_vmem = pl.BlockSpec(memory_space=pltpu.VMEM)
    in_specs = [in_vmem] * len(operands)
    in_specs[11] = pl.BlockSpec(memory_space=pltpu.SMEM)
    results = pl.pallas_call(
        functools.partial(block_kernel, lines),
        out_shape=(
            kinds((rows, width), BF),
            kinds((rows, width), F32),
            kinds(conditioning.shape, F32),
            kinds(qkv_weight.shape, F32),
            kinds(out_weight.shape, F32),
            kinds(up_weight.shape, F32),
            kinds(down_weight.shape, F32),
            kinds(attn_modulate.shape, F32),
            kinds(ffn_modulate.shape, F32),
            kinds((1, heads), F32),
        ),
        in_specs=in_specs,
        out_specs=[in_vmem] * 10,
        scratch_shapes=list(plan.values()),
        compiler_params=pltpu.CompilerParams(
            collective_id=0, has_side_effects=True, vmem_limit_bytes=63 * 2**20
        ),
    )(*operands)
    results = settle(results)
    return tuple(item[None] for item in results[:2]) + tuple(results[2:-1]) + (results[-1][0],)


def settle(results):
    count = len(results)

    def kernel(*refs):
        held, sems = refs[2 * count : -1], refs[-1]
        loads = [
            pltpu.make_async_copy(refs[k], held[k], sems.at[0, k]) for k in range(count)
        ]
        stores = [
            pltpu.make_async_copy(held[k], refs[count + k], sems.at[1, k]) for k in range(count)
        ]
        for copy in loads:
            copy.start()
        for load, store in zip(loads, stores):
            load.wait()
            store.start()
        for copy in stores:
            copy.wait()

    anywhere = pl.BlockSpec(memory_space=pl.ANY)
    return pl.pallas_call(
        kernel,
        out_shape=tuple(jax.ShapeDtypeStruct(item.shape, item.dtype) for item in results),
        in_specs=[anywhere] * count,
        out_specs=[anywhere] * count,
        scratch_shapes=[pltpu.VMEM(item.shape, item.dtype) for item in results]
        + [pltpu.SemaphoreType.DMA((2, count))],
    )(*results)


def in_planes(mesh):
    return mesh.shape["seq"] == 2 and mesh.shape["dp"] == 16


def solution(mesh):
    in_specs = (
        P("dp", "seq", None),
        P("dp", None),
        P("dp", "seq"),
        P("dp", None, "seq"),
        P(("dp", "seq"), None),
        P(("dp", "seq"), None),
        P(("dp", "seq"), None),
        P(("dp", "seq"), None),
        P(("dp", "seq"), None),
        P(("dp", "seq"), None),
        P(),
        P("dp", "seq", None),
    )
    out_specs = (
        P("dp", "seq", None),
        P("dp", "seq", None),
        P("dp", None),
        P(("dp", "seq"), None),
        P(("dp", "seq"), None),
        P(("dp", "seq"), None),
        P(("dp", "seq"), None),
        P(("dp", "seq"), None),
        P(("dp", "seq"), None),
        P(),
    )
    body = plane_shards if in_planes(mesh) else shards
    return jax.shard_map(body, mesh=mesh, in_specs=in_specs, out_specs=out_specs, check_vma=False)
```

```python
import functools
import math
import types

import jax
import jax.numpy as jnp
import ml_dtypes
import numpy as np
from jax import lax
from jax.experimental import pallas as pl
from jax.experimental.pallas import tpu as pltpu
from jax.sharding import PartitionSpec as P

eps_norm = 1e-06
eps_cosine = 1e-06
negative = -1e30
key_rows = 256


def block_split(count, limit):
    size_rows = math.gcd(count, limit)
    return (size_rows, count // size_rows)


def rope_tables(positions, heads):
    unit_pos = (2.0 * positions.astype(jnp.float32) + 1.0) / 16.0 - 1.0
    exponent = (
        jnp.arange(8, dtype=jnp.float32)[None, :] * heads
        + jnp.arange(heads, dtype=jnp.float32)[:, None]
    ) / (8.0 * heads)
    frequency = math.pi * 10.0**exponent
    angles = jnp.moveaxis(unit_pos[..., None, None] * frequency, -4, -2)
    return (jnp.cos(angles), jnp.sin(angles))


def rotate(vector, cosine, sine):
    leading = vector.shape[:-1]
    turned_part = vector[..., :32].reshape(leading + (2, 2, 8))
    first_half = turned_part[..., 0, :]
    second_half = turned_part[..., 1, :]
    turned = jnp.stack(
        [first_half * cosine - second_half * sine, first_half * sine + second_half * cosine],
        axis=-2,
    )
    return jnp.concatenate([turned.reshape(leading + (32,)), vector[..., 32:]], axis=-1)


def norm_forward(value, scale):
    inverse = lax.rsqrt(jnp.mean(value * value, axis=-1, keepdims=True) + eps_norm)
    return (value * inverse * scale[:, None], inverse)


def norm_backward(value, inverse, scale, grad_norm):
    scaled = grad_norm * scale[:, None]
    grad_value = inverse * scaled - value * inverse**3 * jnp.mean(
        scaled * value, axis=-1, keepdims=True
    )
    grad_scale = jnp.sum(grad_norm * value * inverse, axis=1)
    return (grad_value, grad_scale)


def cosine_forward(value, root_scale):
    factor = root_scale[:, None] * lax.rsqrt(
        jnp.sum(value * value, axis=-1, keepdims=True) + eps_cosine
    )
    return (value * factor, factor)


def cosine_backward(value, factor, grad):
    squares = jnp.sum(value * value, axis=-1, keepdims=True) + eps_cosine
    along = jnp.sum(grad * value, axis=-1, keepdims=True)
    grad_value = factor * grad - value * factor * along / squares
    return (grad_value, jnp.sum(along * factor, axis=(0, 1, 3)))


def geglu(value_part, gate_part):
    return value_part * jax.nn.gelu(gate_part, approximate=False)


def pair_grads(queries, grad_att, log_total, deltas, query_crop, key_block, value_block, key_crop):
    scores = jnp.einsum("cqhd,ckhd->cqhk", queries, key_block, preferred_element_type=jnp.float32)
    allowed = (query_crop[:, :, None] == key_crop[:, None, :])[:, :, None, :]
    probs = jnp.exp(jnp.where(allowed, scores - log_total[..., None], negative))
    probs = jnp.where(allowed, probs, 0.0)
    dotted = jnp.einsum(
        "cqhd,ckhd->cqhk", grad_att, value_block, preferred_element_type=jnp.float32
    )
    slope = (probs * (dotted - deltas[..., None])).astype(jnp.bfloat16)
    grad_q = jnp.einsum("cqhk,ckhd->cqhd", slope, key_block, preferred_element_type=jnp.float32)
    grad_k = jnp.einsum("cqhk,cqhd->ckhd", slope, queries, preferred_element_type=jnp.float32)
    grad_v = jnp.einsum(
        "cqhk,cqhd->ckhd", probs.astype(jnp.bfloat16), grad_att, preferred_element_type=jnp.float32
    )
    return (grad_q, grad_k, grad_v)


def pack_terms(terms, lead_shape):
    return jnp.concatenate([term.reshape(lead_shape + (-1,)) for term in terms], axis=-1)


def unpack_terms(packed_row, terms, owners):
    results = []
    offset = 0
    for term in terms:
        own_rows = term.shape[0] // owners
        count = own_rows * term.shape[1]
        results.append(packed_row[offset : offset + count].reshape(own_rows, term.shape[1]))
        offset = offset + count
    return results


def shards(
    block_in,
    conditioning,
    crop_ids,
    positions,
    qkv_weight,
    out_weight,
    up_weight,
    down_weight,
    attn_modulate,
    ffn_modulate,
    head_scale,
    cotangent,
):
    qkv_full, out_full, up_full, down_full, attn_mod, ffn_mod = (
        lax.all_gather(qkv_weight, ("dp", "seq"), axis=0, tiled=True),
        lax.all_gather(out_weight, ("dp", "seq"), axis=0, tiled=True),
        lax.all_gather(up_weight, ("dp", "seq"), axis=0, tiled=True),
        lax.all_gather(down_weight, ("dp", "seq"), axis=0, tiled=True),
        lax.all_gather(attn_modulate, ("dp", "seq"), axis=0, tiled=True),
        lax.all_gather(ffn_modulate, ("dp", "seq"), axis=0, tiled=True),
    )
    canvases, rows, width = block_in.shape
    heads = head_scale.shape[0]
    head_size = width // heads
    hidden_width = down_full.shape[0]
    seq_count = lax.axis_size("seq")
    inputs = block_in.astype(jnp.float32)
    scale_attn = 1.0 + jnp.dot(conditioning, attn_mod, preferred_element_type=jnp.float32)
    scale_ffn = 1.0 + jnp.dot(conditioning, ffn_mod, preferred_element_type=jnp.float32)
    normed_attn, inverse_attn = norm_forward(inputs, scale_attn)
    normed_attn = normed_attn.astype(jnp.bfloat16)
    qkv_all = jnp.einsum(
        "csd,de->cse", normed_attn, qkv_full, preferred_element_type=jnp.float32
    ).reshape(canvases, rows, 3, heads, head_size)
    root_scale = jnp.sqrt(head_scale)
    query_cos, query_factor = cosine_forward(qkv_all[:, :, 0], root_scale)
    key_cos, key_factor = cosine_forward(qkv_all[:, :, 1], root_scale)
    cosine, sine = rope_tables(positions, heads)
    queries = rotate(query_cos, cosine, sine).astype(jnp.bfloat16)
    keys_flat = rotate(key_cos, cosine, sine).astype(jnp.bfloat16).reshape(canvases, rows, width)
    values_flat = qkv_all[:, :, 2].astype(jnp.bfloat16).reshape(canvases, rows, width)
    start_state = (
        jnp.full((canvases, rows, heads), negative, jnp.float32),
        jnp.zeros((canvases, rows, heads), jnp.float32),
        jnp.zeros((canvases, rows, heads, head_size), jnp.float32),
    )
    state_now = start_state
    piece_keys = lax.all_gather(keys_flat, "seq", axis=1, tiled=True)
    piece_values = lax.all_gather(values_flat, "seq", axis=1, tiled=True)
    piece_crop = lax.all_gather(crop_ids, "seq", axis=1, tiled=True)
    size_rows, number = block_split(piece_keys.shape[1], key_rows)

    def step_block(state, block_index):
        running_max, row_total, weighted = state
        offset = block_index * size_rows
        key_block = lax.dynamic_slice_in_dim(piece_keys, offset, size_rows, 1).reshape(
            canvases, size_rows, heads, head_size
        )
        value_block = lax.dynamic_slice_in_dim(piece_values, offset, size_rows, 1).reshape(
            canvases, size_rows, heads, head_size
        )
        crop_block = lax.dynamic_slice_in_dim(piece_crop, offset, size_rows, 1)
        scores = jnp.einsum(
            "cqhd,ckhd->cqhk", queries, key_block, preferred_element_type=jnp.float32
        )
        allowed = (crop_ids[:, :, None] == crop_block[:, None, :])[:, :, None, :]
        scores = jnp.where(allowed, scores, negative)
        new_max = jnp.maximum(running_max, jnp.max(scores, axis=-1))
        weights = jnp.where(allowed, jnp.exp(scores - new_max[..., None]), 0.0)
        shrink = jnp.exp(running_max - new_max)
        row_total = row_total * shrink + jnp.sum(weights, axis=-1)
        weighted = weighted * shrink[..., None] + jnp.einsum(
            "cqhk,ckhd->cqhd",
            weights.astype(jnp.bfloat16),
            value_block,
            preferred_element_type=jnp.float32,
        )
        return ((new_max, row_total, weighted), None)

    state_now, unused = lax.scan(step_block, state_now, jnp.arange(number))
    running_max, row_total, weighted = state_now
    log_total = running_max + jnp.log(row_total)
    attended_raw = weighted / row_total[..., None]
    attended = attended_raw.astype(jnp.bfloat16).reshape(canvases, rows, width)
    middle = inputs + jnp.einsum(
        "csd,de->cse", attended, out_full, preferred_element_type=jnp.float32
    )
    normed_ffn, inverse_ffn = norm_forward(middle, scale_ffn)
    normed_ffn = normed_ffn.astype(jnp.bfloat16)
    up_all = jnp.einsum("csd,de->cse", normed_ffn, up_full, preferred_element_type=jnp.float32)
    value_part = up_all[..., :hidden_width]
    gate_part = up_all[..., hidden_width:]
    hidden = geglu(value_part, gate_part).astype(jnp.bfloat16)
    block_out = (
        middle + jnp.einsum("csf,fd->csd", hidden, down_full, preferred_element_type=jnp.float32)
    ).astype(jnp.bfloat16)
    down_term = jnp.einsum("csf,csd->fd", hidden, cotangent, preferred_element_type=jnp.float32)
    grad_hidden = jnp.einsum(
        "csd,fd->csf", cotangent, down_full, preferred_element_type=jnp.float32
    )
    unused_value, geglu_pull = jax.vjp(geglu, value_part, gate_part)
    grad_value, grad_gate = geglu_pull(grad_hidden)
    grad_up = jnp.concatenate([grad_value, grad_gate], axis=-1).astype(jnp.bfloat16)
    up_term = jnp.einsum("csd,cse->de", normed_ffn, grad_up, preferred_element_type=jnp.float32)
    grad_normed_ffn = jnp.einsum(
        "cse,de->csd", grad_up, up_full, preferred_element_type=jnp.float32
    )
    grad_mid_norm, ffn_scale_sum = norm_backward(middle, inverse_ffn, scale_ffn, grad_normed_ffn)
    grad_middle = cotangent.astype(jnp.float32) + grad_mid_norm
    grad_branch = grad_middle.astype(jnp.bfloat16)
    out_term = jnp.einsum("csd,cse->de", attended, grad_branch, preferred_element_type=jnp.float32)
    grad_attended = (
        jnp.einsum("cse,de->csd", grad_branch, out_full, preferred_element_type=jnp.float32)
        .astype(jnp.bfloat16)
        .reshape(canvases, rows, heads, head_size)
    )
    deltas = jnp.sum(grad_attended.astype(jnp.float32) * attended_raw, axis=-1)
    start_back = (
        jnp.zeros((canvases, rows, heads, head_size), jnp.float32),
        jnp.zeros((canvases, rows * seq_count, 2 * width), jnp.float32),
    )
    state_now = start_back
    fold_piece_keys = lax.all_gather(keys_flat, "seq", axis=1, tiled=True)
    fold_piece_values = lax.all_gather(values_flat, "seq", axis=1, tiled=True)
    fold_piece_crop = lax.all_gather(crop_ids, "seq", axis=1, tiled=True)
    fold_size_rows, number = block_split(fold_piece_keys.shape[1], key_rows)

    def step_block(state, block_index):
        grad_q_sum, grad_kv_all = state
        offset = block_index * fold_size_rows
        key_block = lax.dynamic_slice_in_dim(fold_piece_keys, offset, fold_size_rows, 1).reshape(
            canvases, fold_size_rows, heads, head_size
        )
        value_block = lax.dynamic_slice_in_dim(
            fold_piece_values, offset, fold_size_rows, 1
        ).reshape(canvases, fold_size_rows, heads, head_size)
        crop_block = lax.dynamic_slice_in_dim(fold_piece_crop, offset, fold_size_rows, 1)
        grad_q, grad_k, grad_v = pair_grads(
            queries, grad_attended, log_total, deltas, crop_ids, key_block, value_block, crop_block
        )
        update = jnp.concatenate(
            [
                grad_k.reshape(canvases, fold_size_rows, width),
                grad_v.reshape(canvases, fold_size_rows, width),
            ],
            axis=-1,
        )
        previous = lax.dynamic_slice_in_dim(grad_kv_all, offset, fold_size_rows, 1)
        grad_kv_all = lax.dynamic_update_slice_in_dim(grad_kv_all, previous + update, offset, 1)
        return ((grad_q_sum + grad_q, grad_kv_all), None)

    state_now, unused = lax.scan(step_block, state_now, jnp.arange(number))
    grad_queries, grad_kv_all = state_now
    grad_kv = lax.psum_scatter(
        grad_kv_all.astype(jnp.bfloat16), "seq", scatter_dimension=1, tiled=True
    ).astype(jnp.float32)
    grad_keys = grad_kv[..., :width].reshape(canvases, rows, heads, head_size)
    grad_values = grad_kv[..., width:].reshape(canvases, rows, heads, head_size)
    grad_query_cos = rotate(grad_queries, cosine, -sine)
    grad_key_cos = rotate(grad_keys, cosine, -sine)
    grad_query_raw, query_part = cosine_backward(qkv_all[:, :, 0], query_factor, grad_query_cos)
    grad_key_raw, key_part = cosine_backward(qkv_all[:, :, 1], key_factor, grad_key_cos)
    scale_local = (query_part + key_part) / (2.0 * head_scale)
    grad_qkv = (
        jnp.stack([grad_query_raw, grad_key_raw, grad_values], axis=2)
        .astype(jnp.bfloat16)
        .reshape(canvases, rows, 3 * width)
    )
    qkv_term = jnp.einsum("csd,cse->de", normed_attn, grad_qkv, preferred_element_type=jnp.float32)
    grad_normed_attn = jnp.einsum(
        "cse,de->csd", grad_qkv, qkv_full, preferred_element_type=jnp.float32
    )
    grad_in_norm, attn_scale_sum = norm_backward(inputs, inverse_attn, scale_attn, grad_normed_attn)
    input_grad = grad_middle + grad_in_norm
    attn_sums, ffn_sums = lax.psum((attn_scale_sum, ffn_scale_sum), "seq")
    attn_sums = attn_sums.astype(jnp.bfloat16)
    ffn_sums = ffn_sums.astype(jnp.bfloat16)
    cond_grad = jnp.einsum(
        "cd,nd->cn", attn_sums, attn_mod, preferred_element_type=jnp.float32
    ) + jnp.einsum("cd,nd->cn", ffn_sums, ffn_mod, preferred_element_type=jnp.float32)
    leader = lax.axis_index("seq") == 0
    attn_mod_term = jnp.where(
        leader,
        jnp.einsum("cn,cd->nd", conditioning, attn_sums, preferred_element_type=jnp.float32),
        0.0,
    )
    ffn_mod_term = jnp.where(
        leader,
        jnp.einsum("cn,cd->nd", conditioning, ffn_sums, preferred_element_type=jnp.float32),
        0.0,
    )
    terms = (qkv_term, out_term, up_term, down_term, attn_mod_term, ffn_mod_term)
    groups = lax.axis_size("dp")
    owners = groups * seq_count
    packed = pack_terms(terms, (owners,))
    summed = lax.psum_scatter(packed, ("dp", "seq"), scatter_dimension=0, tiled=True)
    packed_row = summed[0]
    qkv_grad, out_grad, up_grad, down_grad, attnmod_grad, ffnmod_grad = unpack_terms(
        packed_row, terms, owners
    )
    scale_grad = lax.psum(scale_local, ("dp", "seq"))
    return (
        block_out,
        input_grad,
        cond_grad,
        qkv_grad,
        out_grad,
        up_grad,
        down_grad,
        attnmod_grad,
        ffnmod_grad,
        scale_grad,
    )


MESH = pl.DeviceIdType.MESH
BF = jnp.bfloat16
F32 = jnp.float32
PLANE = ((1, 0, 0), (0, 0, 1), (1, 0, 1), (0, 1, 0), (1, 1, 0), (0, 1, 1), (1, 1, 1))
SAME_Y = tuple(
    (step, along)
    for along in (1, 3, 2, 0)
    for step in ((0, 0, 0), (1, 0, 0), (0, 1, 0), (1, 1, 0))
    if along or step != (0, 0, 0)
)
TO_X, TO_Y, TO_FAR = (1, 0, 0), (0, 0, 1), (1, 0, 1)
ERF_P = (
    0.00022905065861350646,
    0.0034082910107109506,
    0.050955695062380861,
    0.18520832239976145,
    1.128379143519084,
)
ERF_Q = (
    -1.1791602954361697e-7,
    0.000023547966471313185,
    0.0010179625278914885,
    0.014070470171167667,
    0.11098505178285362,
    0.49746925110067538,
    1.0,
)


def erf(value):
    value = jnp.clip(value, -3.832506856900711, 3.832506856900711)
    square = value * value
    top = jnp.full_like(value, ERF_P[0])
    for term in ERF_P[1:]:
        top = top * square + term
    bottom = jnp.full_like(value, ERF_Q[0])
    for term in ERF_Q[1:]:
        bottom = bottom * square + term
    return value * top / bottom


def dot(lhs, rhs, on_lhs=1, on_rhs=0):
    return lax.dot_general(
        lhs, rhs, (((on_lhs,), (on_rhs,)), ((), ())), preferred_element_type=F32
    )


def block_kernel(
    lines,
    x_ref,
    cot_ref,
    qkv_ref,
    up_ref,
    out_ref,
    down_ref,
    amod_ref,
    fmod_ref,
    cond_ref,
    crop_ref,
    pos_ref,
    scale_ref,
    table_ref,
    *results_and_scratch,
):
    targets, held = results_and_scratch[:10], results_and_scratch[10:20]
    scratch, give_sems = results_and_scratch[20:-1], results_and_scratch[-1]
    block_out, input_grad, cond_grad, qkv_grad, out_grad = held[:5]
    up_grad, down_grad, amod_grad, fmod_grad, scale_grad = held[5:]
    gives = [pltpu.make_async_copy(held[k], targets[k], give_sems.at[k]) for k in range(10)]
    names = list(scratch_plan(lines, x_ref, qkv_ref, up_ref, out_ref, down_ref))
    s = types.SimpleNamespace(**dict(zip(names, scratch)))
    dp = lax.axis_index("dp")
    y = lax.axis_index("seq")
    z = dp // 4
    x = (dp // 2) % 2
    c = dp % 2
    rows, width = x_ref.shape
    up_rows = up_ref.shape[0]
    own_cols = qkv_ref.shape[1] // 8
    lanes = own_cols // 3
    half_head = out_ref.shape[0]
    hidden = up_ref.shape[1] // 16
    down_rows = down_ref.shape[0]
    mod_rows = amod_ref.shape[0]
    canvas_rows = 2 * rows
    crops = canvas_rows // 16
    me = 4 * x + 2 * c + y
    device_index = 8 * z + me

    def member(step):
        return 4 * ((x + step[0]) % 2) + 2 * ((c + step[1]) % 2) + (y + step[2]) % 2

    def device(step, along=0):
        return (
            ((z + along) % lines) * 4 + ((x + step[0]) % 2) * 2 + (c + step[1]) % 2,
            (y + step[2]) % 2,
        )

    def line_device(along):
        return (jnp.clip(z + along, 0, lines - 1) * 4 + dp % 4, y)

    def inside(along):
        return z + along < lines if along > 0 else z + along >= 0

    here = (0, 0, 0)
    core = (0, 1, 0)
    sends = []

    class Copy:
        def __init__(self, src, dst_there, dst_here, sems, at, target):
            self.out = pltpu.make_async_remote_copy(
                src_ref=src,
                dst_ref=dst_there,
                send_sem=sems.at[0, at],
                recv_sem=sems.at[1, at],
                device_id=target,
                device_id_type=MESH,
            )
            self.into = pltpu.make_async_remote_copy(
                src_ref=src,
                dst_ref=dst_here,
                send_sem=sems.at[0, at],
                recv_sem=sems.at[1, at],
                device_id=target,
                device_id_type=MESH,
            )

        def start(self, when=None):
            if when is None:
                self.out.start()
            else:
                pl.when(when)(self.out.start)
            sends.append((self.out, when))

        def arrive(self):
            self.into.wait_recv()

    class Gather:
        def __init__(self, buffer, sems):
            at = lambda step: buffer.at[member(step)]
            half = buffer.shape[1] // 2
            rows_of = (pl.ds(0, half), pl.ds(half, half))
            part = lambda step, k: buffer.at[member(step), rows_of[k]]
            self.x_own = [
                Copy(part(here, k), part(here, k), part(TO_X, k), sems, k, device(TO_X))
                for k in range(2)
            ]
            self.y_own = [
                Copy(part(here, k), part(here, k), part(TO_Y, k), sems, 2 + k, device(TO_Y))
                for k in range(2)
            ]
            self.y_far = Copy(part(TO_X, 0), part(TO_X, 0), part(TO_FAR, 0), sems, 4, device(TO_Y))
            self.x_far = Copy(part(TO_Y, 1), part(TO_Y, 1), part(TO_FAR, 1), sems, 5, device(TO_X))
            self.pair = Copy(at(here), at(here), at(core), sems, 6, device(core))
            self.cross = [
                Copy(at(step), at(step), at((step[0], 1, step[2])), sems, 7 + k, device(core))
                for k, step in enumerate((TO_X, TO_Y, TO_FAR))
            ]

        def start(self):
            self.x_own[0].start()
            self.y_own[1].start()
            self.x_own[1].start()
            self.y_own[0].start()
            self.pair.start()

        def turn(self):
            self.x_own[0].arrive()
            self.y_far.start()
            self.y_own[1].arrive()
            self.x_far.start()

        def near(self):
            self.y_own[0].arrive()
            self.cross[1].start()
            self.x_own[1].arrive()
            self.cross[0].start()

        def far(self):
            self.y_far.arrive()
            self.x_far.arrive()
            self.cross[2].start()

        def pair_near(self):
            self.pair.arrive()
            self.cross[1].arrive()

        def pair_far(self):
            self.cross[0].arrive()
            self.cross[2].arrive()

        def finish(self):
            self.near()
            self.far()
            self.pair_near()
            self.pair_far()

        def steps(self):
            return {0: self.near, 1: self.pair_near, 2: self.far, 3: self.pair_far}

    class Reduce:
        def __init__(self, part, pair_in, far_in, chip_in, sems):
            self.part, self.pair_in, self.far_in, self.chip_in = part, pair_in, far_in, chip_in
            half = part.shape[1] // 2
            self.rows_of = rows_of = (pl.ds(0, half), pl.ds(half, half))
            self.steps_of = (here, TO_X, TO_Y, TO_FAR)
            self.pair = [
                Copy(
                    part.at[member((step[0], 1, step[2]))],
                    pair_in.at[k],
                    pair_in.at[k],
                    sems,
                    k,
                    device(core),
                )
                for k, step in enumerate(self.steps_of)
            ]
            piece = lambda step, k: part.at[member(step), rows_of[k]]
            self.x_far = Copy(piece(TO_FAR, 0), far_in.at[0], far_in.at[0], sems, 4, device(TO_X))
            self.y_far = Copy(piece(TO_FAR, 1), far_in.at[1], far_in.at[1], sems, 5, device(TO_Y))
            into = lambda way, k: chip_in.at[way, rows_of[k]]
            self.x_own = [
                Copy(piece(TO_X, k), into(0, k), into(0, k), sems, 6 + k, device(TO_X))
                for k in range(2)
            ]
            self.y_own = [
                Copy(piece(TO_Y, k), into(1, k), into(1, k), sems, 8 + k, device(TO_Y))
                for k in range(2)
            ]

        def add_pair(self, k):
            self.pair[k].arrive()
            slot = member(self.steps_of[k])
            total = self.part[slot].astype(F32) + self.pair_in[k].astype(F32)
            self.part[slot] = total.astype(BF)

        def add_far(self, step, k):
            slot = member(step)
            total = self.part[slot, self.rows_of[k], :].astype(F32) + self.far_in[k].astype(F32)
            self.part[slot, self.rows_of[k], :] = total.astype(BF)

        def give_far(self):
            self.pair[3].start()
            self.pair[1].start()

        def send_far(self):
            self.add_pair(3)
            self.x_far.start()
            self.y_far.start()
            self.add_pair(1)
            self.x_own[0].start()

        def give_near(self):
            self.pair[2].start()
            self.pair[0].start()

        def send_near(self):
            self.add_pair(2)
            self.y_own[1].start()

        def steps(self):
            return {0: self.give_far, 1: self.send_far, 2: self.give_near, 3: self.send_near}

        def middle(self):
            self.x_far.arrive()
            self.add_far(TO_Y, 0)
            self.y_own[0].start()
            self.y_far.arrive()
            self.add_far(TO_X, 1)
            self.x_own[1].start()

        def finish(self):
            self.pair[0].arrive()
            total = self.part[me].astype(F32) + self.pair_in[0].astype(F32)
            for copies in (self.x_own, self.y_own):
                for copy in copies:
                    copy.arrive()
            return total + self.chip_in[0].astype(F32) + self.chip_in[1].astype(F32)

    class Spread:
        def __init__(self, source, target, sems):
            self.source, self.target = source, target
            self.copies = [
                Copy(
                    source.at[member(step)],
                    target.at[me],
                    target.at[member(step)],
                    sems,
                    k,
                    device(step),
                )
                for k, step in enumerate(PLANE)
            ]

        def start(self):
            for copy in self.copies:
                copy.start()
            self.target[me] = self.source[me]

        def finish(self):
            for copy in self.copies:
                copy.arrive()

    class Share:
        def __init__(self, buffer, sems, block=None):
            self.copies = [
                Copy(
                    buffer.at[me] if block is None else block,
                    buffer.at[me],
                    buffer.at[member(step)],
                    sems,
                    k,
                    device(step),
                )
                for k, step in enumerate(PLANE)
            ]

        def start(self):
            for copy in self.copies:
                copy.start()

        def finish(self):
            for copy in self.copies:
                copy.arrive()

    class Line:
        def __init__(self, buffer, sems, first=None):
            self.copies = []
            for along in range(1, lines):
                back = (z + lines - along) % lines
                if first is None:
                    mine, theirs = buffer.at[z], buffer.at[back]
                else:
                    mine, theirs = buffer.at[pl.ds(first * z, first)], buffer.at[pl.ds(first * back, first)]
                self.copies.append(Copy(mine, mine, theirs, sems, along - 1, device(here, along)))

        def start(self):
            for copy in self.copies:
                copy.start()

        def finish(self):
            for copy in self.copies:
                copy.arrive()

    class Relay:
        def __init__(self, buffer, sems):
            self.copies = {
                along: Copy(
                    buffer.at[z],
                    buffer.at[z],
                    buffer.at[jnp.clip(z - along, 0, lines - 1)],
                    sems,
                    at,
                    line_device(along),
                )
                for at, along in enumerate((1, -1, 2, -2))
            }
            self.onward = {
                along: Copy(
                    buffer.at[far], buffer.at[far], buffer.at[far], sems, 4, line_device(along)
                )
                for along, far in ((1, 0), (-1, lines - 1))
            }

        def start(self, steps=(2, -2, 1, -1)):
            for along in steps:
                self.copies[along].start(inside(along))

        def middle(self):
            @pl.when(z == 2)
            def up_line():
                self.copies[2].arrive()

            @pl.when(z == 1)
            def down_line():
                self.copies[-2].arrive()

            self.onward[1].start(z == 2)
            self.onward[-1].start(z == 1)

        def finish(self):
            pl.when(z >= 1)(self.copies[1].arrive)
            pl.when(z <= 2)(self.copies[-1].arrive)
            pl.when(z == 3)(self.copies[2].arrive)
            pl.when(z == 0)(self.copies[-2].arrive)
            pl.when(z == 3)(self.onward[1].arrive)
            pl.when(z == 0)(self.onward[-1].arrive)

    class Fold:
        def __init__(self, terms, landed, sems):
            self.terms, self.landed = terms, landed
            self.copies = {
                along: Copy(
                    terms.at[jnp.clip(z + along, 0, lines - 1)],
                    landed.at[min(at, 2)],
                    landed.at[min(at, 2)],
                    sems,
                    at,
                    line_device(along),
                )
                for at, along in enumerate((1, -1, 2, -2))
            }
            self.first = {
                along: Copy(
                    terms.at[far], landed.at[3], landed.at[3], sems, 4, line_device(along)
                )
                for along, far in ((1, lines - 1), (-1, 0))
            }

        def start(self):
            self.first[1].start(z == 0)
            self.first[-1].start(z == lines - 1)
            self.copies[2].start(z == 0)
            self.copies[-2].start(z == lines - 1)
            for along in (1, -1):
                self.copies[along].start(inside(along))

        def middle(self):
            for at, far, along in ((1, lines - 1, 1), (2, 0, -1)):

                @pl.when(z == at)
                def join():
                    self.first[along].arrive()
                    total = self.terms[far].astype(F32) + self.landed[3].astype(F32)
                    self.terms[far] = total.astype(BF)

                self.copies[2 * along].start(z == at)

        def finish(self, total):
            total[...] = self.terms[z].astype(F32)
            for at, (along, when) in enumerate(((1, z >= 1), (-1, z <= 2), (2, z >= 2), (-2, z <= 1))):

                @pl.when(when)
                def add():
                    self.copies[along].arrive()
                    total[...] += self.landed[min(at, 2)].astype(F32)

            return total[...]

    class Canvases:
        def __init__(self, buffer, sems):
            self.copies = []
            for at, (step, along) in enumerate(SAME_Y):
                from_there = device(step, lines - along)[0]
                self.copies.append(
                    Copy(
                        buffer.at[dp],
                        buffer.at[dp],
                        buffer.at[from_there],
                        sems,
                        at,
                        device(step, along),
                    )
                )

        def start(self):
            for copy in self.copies:
                copy.start()

        def finish(self):
            for copy in self.copies:
                copy.arrive()

    def each_canvas(body, near=True, before=None, after=None):
        def step(t, carry):
            for k, action in (before or {}).items():
                pl.when(t == k)(action)
            turn = t if near else 3 - t
            body(2 * ((x + (turn // 2)) % 2) + (c + turn) % 2)
            for k, action in (after or {}).items():
                pl.when(t == k)(action)
            return carry

        lax.fori_loop(0, 4, step, 0)

    def slots(t):
        return pl.ds(2 * t, 2)

    lane = lax.broadcasted_iota(jnp.int32, (1, lanes), 1)
    first_head = lane < lanes // 2
    first_part = (lane % 16) < 8

    def per_head(pair):
        return jnp.where(first_head, pair[0], pair[1])

    def head_sums(value):
        left = jnp.where(first_head, value, 0.0)
        right = jnp.where(first_head, 0.0, value)
        return (
            jnp.sum(left, axis=-1, keepdims=True),
            jnp.sum(right, axis=-1, keepdims=True),
        )

    def partner(value):
        return jnp.where(
            first_part, pltpu.roll(value, lanes - 8, 1), pltpu.roll(value, 8, 1)
        )

    barrier = pltpu.get_barrier_semaphore()
    partners = [device(step) for step in PLANE if step[2]]
    partners += [device(step, along) for step, along in SAME_Y]
    for target in partners:
        pl.semaphore_signal(barrier, inc=1, device_id=target, device_id_type=MESH)
    ids = s.ids
    ids[me] = jnp.zeros(ids.shape[1:], jnp.int32)
    ids[me, 0:1, :] = crop_ref[...]
    ids[me, 1:3, :] = pos_ref[0]
    conds = s.conds
    conds[dp] = jnp.zeros(conds.shape[1:], F32)
    for r in range(cond_ref.shape[1] // 128):
        conds[dp, r : r + 1, :] = cond_ref[:, 128 * r : 128 * (r + 1)].astype(F32)
    s.tokens[me] = x_ref[...]
    s.cots[me] = cot_ref[...]
    s.out_line[z] = out_ref[...]
    s.down_line[z] = down_ref[...]
    mod_full = s.mod_full
    mod_full[...] = jnp.zeros(mod_full.shape, BF)
    mod_full[0:mod_rows, 0:width] = amod_ref[...]
    mod_full[0:mod_rows, width : 2 * width] = fmod_ref[...]

    size = lanes // 2
    qkv_places = [
        (m, (2 * part + k) * size, part * width + (8 * (m % 2) + 4 * k + m // 2) * size)
        for m in range(8)
        for part in range(3)
        for k in range(2)
    ]
    up_places = [
        (m, (lines * part + k) * down_rows, part * 8 * hidden + (8 * k + m) * down_rows)
        for m in range(8)
        for part in range(2)
        for k in range(lines)
    ]
    for m, own, whole in qkv_places:
        s.qkv_cols[m, :, own : own + size] = qkv_ref[:, whole : whole + size]
    for m, own, whole in up_places:
        s.up_cols[m, :, own : own + down_rows] = up_ref[:, whole : whole + down_rows]
    pl.semaphore_wait(barrier, len(partners))

    cond_copy = Canvases(conds, s.sem_cond)
    ids_copy = Share(ids, s.sem_ids)
    qkv_spread = Spread(s.qkv_cols, s.qkv_line.at[z], s.sem_qkv_spread)
    up_spread = Spread(s.up_cols, s.up_line.at[z], s.sem_up_spread)
    qkv_line = [
        Relay(s.qkv_line.at[:, pl.ds(4 * k, 4)], s.sem_qkv_line.at[k]) for k in range(2)
    ]
    out_line = Relay(s.out_line, s.sem_out_line)
    up_line = [Relay(s.up_line.at[:, pl.ds(4 * k, 4)], s.sem_up_line.at[k]) for k in range(2)]
    down_line = Relay(s.down_line, s.sem_down_line)
    token_copy = Gather(s.tokens, s.sem_tokens)
    cot_copy = Gather(s.cots, s.sem_cots)
    cond_copy.start()
    qkv_spread.start()
    token_copy.start()
    out_line.start()
    qkv_spread.finish()
    qkv_line[0].start()
    cond_copy.finish()
    picked = jnp.zeros((conds.shape[0], 128), F32)
    for r in range(cond_ref.shape[1] // 128):
        at_row = lax.broadcasted_iota(jnp.int32, (128, 128), 0) + 128 * r
        at_col = lax.broadcasted_iota(jnp.int32, (128, 128), 1)
        choose = (at_row == at_col + mod_rows * device_index) & (at_col < mod_rows)
        picked = picked + dot(
            conds[:, r, :].astype(BF), jnp.where(choose, 1.0, 0.0).astype(BF)
        )
    cond_mine = picked.astype(BF)
    block_cols = 2 * width // 8
    mod_terms, mod_in = s.mod_terms, s.mod_in
    for m in range(8):
        mod_terms[m] = dot(cond_mine, mod_full[:, block_cols * m : block_cols * (m + 1)])
    mod_spread = Spread(mod_terms, mod_in, s.sem_mod_spread)
    mod_spread.start()
    token_copy.turn()
    mod_spread.finish()
    mod_sum = mod_in[0]
    for m in range(1, 8):
        mod_sum = mod_sum + mod_in[m]
    mod_line = s.mod_line
    mod_line[z] = mod_sum
    mod_copy = Line(mod_line, s.sem_mod_line)
    mod_copy.start()
    qkv_line[1].start()
    up_spread.start()
    ids_copy.start()
    qkv_line[0].middle()
    mod_copy.finish()
    mod_sum = mod_line[0]
    for k in range(1, lines):
        mod_sum = mod_sum + mod_line[k]
    s.mod_total[...] = 1.0 + mod_sum
    mod_share = Share(s.mods, s.sem_mods)
    own_rows = s.mod_total[pl.ds(8 * (z // 2), 8), :]
    s.mods[me] = own_rows
    mod_share.start()
    cot_copy.start()
    out_line.middle()
    mod_share.finish()
    scales = s.scales
    for m in range(8):
        scales[:, block_cols * m : block_cols * (m + 1)] = s.mods[m]

    def scale_row(canvas, ffn):
        row = scales[pl.ds(4 * (z % 2) + canvas, 1), :]
        return row[:, width:] if ffn else row[:, :width]

    own_canvas = 2 * x + c

    def inverse_rms(value):
        return lax.rsqrt(jnp.mean(value * value, axis=-1, keepdims=True) + eps_norm)

    normed = s.normed

    def norm_tokens(canvas):
        value = s.tokens[slots(canvas)].reshape(canvas_rows, width).astype(F32)
        scaled = value * inverse_rms(value) * scale_row(canvas, False)
        normed[slots(canvas)] = scaled.astype(BF).reshape(2, rows, width)

    each_canvas(norm_tokens, before=token_copy.steps())
    qkv_line[1].middle()
    up_spread.finish()
    for line in up_line:
        line.start()
    out_line.finish()
    out_half = s.out_half
    half_copy = Copy(
        s.out_line.at[pl.ds(2 * (1 - y), 2)],
        out_half,
        out_half,
        s.sem_half,
        0,
        device((0, 0, 1)),
    )
    half_copy.start()
    cot_copy.turn()
    ids_copy.finish()
    for line in qkv_line:
        line.finish()
    head_of = lambda k: 8 * y + 4 * k + 2 * x + c
    head_scales = [scale_ref[head_of(k)] for k in range(2)]
    scale_lanes = per_head(head_scales)
    root_lanes = jnp.sqrt(scale_lanes)

    def canvas_ids(canvas, row):
        return jnp.concatenate(
            [ids[2 * canvas, row : row + 1, :], ids[2 * canvas + 1, row : row + 1, :]], axis=1
        )

    def one_hot(row, count):
        return jnp.where(
            lax.broadcasted_iota(jnp.int32, (count, canvas_rows), 0) == row, 1.0, 0.0
        ).astype(BF)

    def attend(canvas):
        qkv = dot(
            normed[slots(canvas)].reshape(canvas_rows, width),
            s.qkv_line[...].reshape(width, own_cols),
        )
        places = [one_hot(canvas_ids(canvas, 1), 16), one_hot(canvas_ids(canvas, 2), 16)]
        turn = dot(jnp.concatenate(places + places, axis=0), table_ref[me], 0, 0)
        s.turns[canvas] = turn
        cosine, sine = turn[:, :lanes], turn[:, lanes:]
        rotated = []
        for part in range(2):
            raw = qkv[:, part * lanes : (part + 1) * lanes]
            s.raw[canvas, part] = raw
            sums = head_sums(raw * raw)
            factor = per_head([lax.rsqrt(value + eps_cosine) for value in sums]) * root_lanes
            turned = raw * factor
            turned = (turned * cosine + partner(turned) * sine).astype(BF)
            s.rotated[canvas, part] = turned
            rotated.append(turned)
        values = qkv[:, 2 * lanes :].astype(BF)
        s.rotated[canvas, 2] = values
        crop_hot = one_hot(canvas_ids(canvas, 0), crops)
        allowed = dot(crop_hot, crop_hot, 0, 0)
        heads = []
        for k in range(2):
            mine = first_head if k == 0 else jnp.logical_not(first_head)
            query = jnp.where(mine, rotated[0], jnp.zeros_like(rotated[0]))
            weights = jnp.exp(dot(query, rotated[1], 1, 1)) * allowed
            probs = weights / jnp.sum(weights, axis=-1, keepdims=True)
            s.probs[canvas, k] = probs
            heads.append(dot(probs.astype(BF), values))
        attended = per_head(heads)
        s.raw_attended[canvas] = attended
        attended = attended.astype(BF)
        s.attended[canvas] = attended
        value = dot(attended, out_full[...].reshape(lanes, width))
        s.mid_part[slots(canvas)] = value.astype(BF).reshape(2, rows, width)

    half_copy.arrive()
    out_full = s.out_full
    for k in range(2):
        out_full[k, y] = s.out_line[2 * y + k]
        out_full[k, 1 - y] = out_half[k]

    mid_reduce = Reduce(
        s.mid_part, s.mid_pair, s.mid_far, s.mid_chip, s.sem_mid
    )
    each_canvas(attend, False, after=mid_reduce.steps())
    mid_reduce.middle()
    cot_copy.finish()
    up_line[0].middle()
    middle = x_ref[...].astype(F32) + mid_reduce.finish()
    s.middle[...] = middle
    ffn_row = scale_row(own_canvas, True)
    s.ffn[me] = (middle * inverse_rms(middle) * ffn_row).astype(BF)
    ffn_copy = Gather(s.ffn, s.sem_ffn)
    ffn_copy.start()
    ffn_copy.turn()
    up_line[1].middle()
    down_line.start()
    for line in up_line:
        line.finish()

    def feed(canvas):
        up = dot(
            s.ffn[slots(canvas)].reshape(canvas_rows, width),
            s.up_line[...].reshape(width, 2 * hidden),
        )
        value, gate = up[:, :hidden], up[:, hidden:]
        cdf = 0.5 + 0.5 * erf(gate * math.sqrt(0.5))
        act = gate * cdf
        s.hidden[canvas] = (value * act).astype(BF)
        s.act[canvas] = act
        density = jnp.exp(-0.5 * gate * gate) * (1.0 / math.sqrt(2.0 * math.pi))
        s.slope[canvas] = value * (cdf + gate * density)

    each_canvas(feed, before=ffn_copy.steps())
    down_line.middle()

    def cots_of(canvas):
        return s.cots[slots(canvas)].reshape(canvas_rows, width)

    all_rows = 8 * rows
    chunk = 256

    def down_term(n, carry):
        cols = pl.ds(pl.multiple_of(n * chunk, chunk), chunk)
        term = dot(
            s.hidden[...].reshape(all_rows, hidden),
            s.cots[:, :, cols].reshape(all_rows, chunk),
            0,
            0,
        )
        s.down_term[:, :, cols] = term.astype(BF).reshape(lines, down_rows, chunk)
        return carry

    lax.fori_loop(0, width // chunk, down_term, 0)
    down_fold = Fold(s.down_term, s.down_in, s.sem_down_fold)
    down_fold.start()
    down_line.finish()

    def feed_back(canvas):
        grad_hidden = dot(cots_of(canvas), s.down_line[...].reshape(hidden, width), 1, 1)
        grad_up = jnp.concatenate(
            [grad_hidden * s.act[canvas], grad_hidden * s.slope[canvas]], axis=1
        ).astype(BF)
        s.grad_up[canvas] = grad_up
        part = dot(grad_up, s.up_line[...].reshape(width, 2 * hidden), 1, 1)
        s.gnf_part[slots(canvas)] = part.astype(BF).reshape(2, rows, width)

    gnf_reduce = Reduce(
        s.gnf_part, s.gnf_pair, s.gnf_far, s.gnf_chip, s.sem_gnf
    )
    each_canvas(feed_back, False, after=gnf_reduce.steps())
    gnf_reduce.middle()

    def up_term(k, carry):
        cols = pl.ds(pl.multiple_of(k * 8 * up_rows, 8 * up_rows), 8 * up_rows)
        term = dot(
            s.ffn[:, :, cols].reshape(all_rows, 8 * up_rows),
            s.grad_up[...].reshape(all_rows, 2 * hidden),
            0,
            0,
        )
        s.up_term[k] = term.astype(BF).reshape(8, up_rows, 2 * hidden)
        return carry

    lax.fori_loop(0, lines, up_term, 0)
    up_fold = Fold(s.up_term, s.up_in, s.sem_up_fold)
    up_fold.start()
    down_fold.middle()

    def norm_back(value, row, grad):
        inverse = inverse_rms(value)
        scaled = grad * row
        along = jnp.mean(scaled * value, axis=-1, keepdims=True)
        grad_value = inverse * scaled - value * (inverse * inverse * inverse) * along
        return grad_value, jnp.sum(grad * value * inverse, axis=0, keepdims=True)

    def put_row(target, offset, row):
        for r in range(width // 128):
            target[offset + r : offset + r + 1, :] = row[:, 128 * r : 128 * (r + 1)]

    grad_mid, ffn_sum = norm_back(s.middle[...], ffn_row, gnf_reduce.finish())
    grad_middle = cot_ref[...].astype(F32) + grad_mid
    s.grad_middle[...] = grad_middle
    s.branch[me] = grad_middle.astype(BF)
    branch_copy = Gather(s.branch, s.sem_branch)
    branch_copy.start()
    sums_own = s.sums_own
    put_row(sums_own, 8, ffn_sum)

    def to_out(canvas):
        part = dot(s.hidden[canvas], s.down_line[...].reshape(hidden, width))
        s.out_part[slots(canvas)] = part.astype(BF).reshape(2, rows, width)

    out_reduce = Reduce(
        s.out_part, s.out_pair, s.out_far, s.out_chip, s.sem_out
    )
    branch_copy.turn()
    each_canvas(to_out)
    branch_copy.finish()
    out_reduce.give_far()
    out_reduce.give_near()

    def attend_back(canvas):
        branch = s.branch[slots(canvas)].reshape(canvas_rows, width)
        grad_att = dot(branch, out_full[...].reshape(lanes, width), 1, 1).astype(BF)
        turn = s.turns[canvas]
        cosine, sine = turn[:, :lanes], turn[:, lanes:]
        query, key, values = (s.rotated[canvas, part] for part in range(3))
        deltas = head_sums(grad_att.astype(F32) * s.raw_attended[canvas])
        grads = [[], [], []]
        for k in range(2):
            mine = first_head if k == 0 else jnp.logical_not(first_head)
            probs = s.probs[canvas, k]
            one_head = jnp.where(mine, grad_att, jnp.zeros_like(grad_att))
            dotted = dot(one_head, values, 1, 1)
            slope = (probs * (dotted - deltas[k])).astype(BF)
            grads[0].append(dot(slope, key))
            grads[1].append(dot(slope, query, 0, 0))
            grads[2].append(dot(probs.astype(BF), grad_att, 0, 0))
        pieces = []
        for part in range(2):
            grad = per_head(grads[part])
            grad = grad * cosine - partner(grad) * sine
            raw = s.raw[canvas, part]
            squares = [value + eps_cosine for value in head_sums(raw * raw)]
            along = head_sums(grad * raw)
            inverse = [lax.rsqrt(value) for value in squares]
            factor = per_head(inverse) * root_lanes
            shrink = per_head([along[k] * inverse[k] * inverse[k] for k in range(2)])
            pieces.append(factor * grad - raw * factor * shrink)
            term = per_head([jnp.sum(along[k] * inverse[k], axis=0, keepdims=True) for k in range(2)])
            s.head_terms[...] += term * root_lanes / (2.0 * scale_lanes)
        pieces.append(per_head(grads[2]))
        grad_qkv = jnp.concatenate(pieces, axis=1).astype(BF)
        s.grad_qkv[canvas] = grad_qkv
        part = dot(grad_qkv, s.qkv_line[...].reshape(width, own_cols), 1, 1)
        s.gna_part[slots(canvas)] = part.astype(BF).reshape(2, rows, width)

    term = dot(
        s.attended[...].reshape(all_rows, lanes),
        s.branch[...].reshape(all_rows, width),
        0,
        0,
    ).astype(BF).reshape(2, 2, half_head, width)
    halves = s.out_halves
    for k in range(2):
        for half in range(2):
            halves[half, k] = term[k, half]
    swap = Copy(
        halves.at[1 - y], s.out_swap, s.out_swap, s.sem_half, 1, device((0, 0, 1))
    )
    swap.start()

    s.head_terms[...] = jnp.zeros((1, lanes), F32)
    gna_reduce = Reduce(
        s.gna_part, s.gna_pair, s.gna_far, s.gna_chip, s.sem_gna
    )
    each_canvas(attend_back, False, after=gna_reduce.steps())
    up_fold.middle()
    out_reduce.send_far()
    out_reduce.send_near()
    gna_reduce.middle()

    swap.arrive()
    out_terms = s.out_terms
    for k in range(2):
        out_terms[2 * y + k] = halves[y, k]
        out_terms[2 * (1 - y) + k] = s.out_swap[k]
    out_fold = Fold(out_terms, s.out_in, s.sem_out_fold)
    out_fold.start()
    def qkv_term(k, carry):
        cols = pl.ds(pl.multiple_of(k * 8 * up_rows, 8 * up_rows), 8 * up_rows)
        term = dot(
            normed[:, :, cols].reshape(all_rows, 8 * up_rows),
            s.grad_qkv[...].reshape(all_rows, own_cols),
            0,
            0,
        )
        s.qkv_term[k] = term.astype(BF).reshape(8, up_rows, own_cols)
        return carry

    lax.fori_loop(0, lines, qkv_term, 0)
    cuts = (pl.ds(0, 6), pl.ds(6, 2))
    qkv_fold = [
        Fold(s.qkv_term.at[:, cut], s.qkv_in.at[:, cut], s.sem_qkv_fold.at[k])
        for k, cut in enumerate(cuts)
    ]
    qkv_fold[0].start()

    grad_in, attn_sum = norm_back(x_ref[...].astype(F32), scale_row(own_canvas, False), gna_reduce.finish())
    input_grad[...] = s.grad_middle[...] + grad_in
    gives[1].start()
    put_row(sums_own, 0, attn_sum)
    head_rows = lax.broadcasted_iota(jnp.int32, (8, lanes), 0)
    head_lane = lax.broadcasted_iota(jnp.int32, (8, lanes), 1)
    head_tile = jnp.zeros((8, lanes), F32)
    for k in range(2):
        value = jnp.sum(
            jnp.where(lane == k * (lanes // 2), s.head_terms[...], 0.0), axis=1, keepdims=True
        )
        head_tile = head_tile + jnp.where(
            (head_rows == 0) & (head_lane == head_of(k)), value, 0.0
        )
    sums_own[16:24, :] = head_tile
    s.sums_plane[me] = sums_own[...]
    sums_share = Share(s.sums_plane, s.sem_sums_share)
    sums_share.start()
    out_reduce.middle()
    out_fold.middle()
    sums_share.finish()
    sums = s.sums
    for k in range(4):
        sums[4 * z + k] = s.sums_plane[2 * k] + s.sums_plane[2 * k + 1]
    all_sums = Line(sums, s.sem_sums, 4)
    all_sums.start()
    qkv_fold[1].start()
    qkv_fold[0].middle()
    down_grad[...] = down_fold.finish(s.down_total).reshape(down_rows, width)
    gives[6].start()
    block_out[...] = (s.middle[...] + out_reduce.finish()).astype(BF)
    gives[0].start()
    s.up_sum[...] = up_fold.finish(s.up_total).astype(BF)
    up_return = Spread(s.up_sum, s.up_back, s.sem_up_back)
    up_return.start()
    up_return.finish()
    for m, own, whole in up_places:
        up_grad[:, whole : whole + down_rows] = s.up_back[m, :, own : own + down_rows].astype(F32)
    gives[5].start()
    qkv_fold[1].middle()
    for fold, cut in zip(qkv_fold, cuts):
        s.qkv_sum[cut] = fold.finish(s.qkv_total.at[cut]).astype(BF)
    qkv_return = Spread(s.qkv_sum, s.qkv_back, s.sem_qkv_back)
    qkv_return.start()

    all_sums.finish()
    rounded = [
        jnp.concatenate([sums[:, offset + r, :] for r in range(width // 128)], axis=1).astype(BF)
        for offset in (0, 8)
    ]
    mine_for = dot(rounded[0], mod_full[:, :width], 1, 1) + dot(
        rounded[1], mod_full[:, width:], 1, 1
    )
    cond_line, cond_in = s.cond_line, s.cond_in
    s.cond_all[...] = mine_for
    for k in range(lines):
        cond_line[k] = s.cond_all[8 * (k // 2) : 8 * (k // 2) + 8, :]
    cond_send = [
        Copy(
            cond_line.at[(z + along) % lines],
            cond_in.at[me, z],
            cond_in.at[me, (z + lines - along) % lines],
            s.sem_cond_line,
            along - 1,
            device(here, along),
        )
        for along in range(1, lines)
    ]
    for copy in cond_send:
        copy.start()
    cond_in[me, z] = cond_line[z]
    amod_grad[...] = dot(cond_mine, rounded[0], 0, 0)[:mod_rows]
    gives[7].start()
    fmod_grad[...] = dot(cond_mine, rounded[1], 0, 0)[:mod_rows]
    gives[8].start()
    head_sum = sums[0, 16:17, :]
    for k in range(1, sums.shape[0]):
        head_sum = head_sum + sums[k, 16:17, :]
    scale_grad[...] = head_sum[:, : scale_grad.shape[1]]
    gives[9].start()
    for copy in cond_send:
        copy.arrive()
    cond_share = Share(cond_in, s.sem_cond_share)
    cond_share.start()
    out_grad[...] = out_fold.finish(s.out_total)
    gives[4].start()
    qkv_return.finish()
    for m, own, whole in qkv_places:
        qkv_grad[:, whole : whole + size] = s.qkv_back[m, :, own : own + size].astype(F32)
    gives[3].start()
    cond_share.finish()
    for k in range(lines):
        for m in range(8):
            at_row = 8 * k + m
            row = cond_in[m, k, pl.ds(4 * (z % 2) + own_canvas, 1), :]
            cond_grad[:, at_row * mod_rows : (at_row + 1) * mod_rows] = row[:, :mod_rows]
    gives[2].start()
    for copy, when in sends:
        if when is None:
            copy.wait_send()
        else:
            pl.when(when)(copy.wait_send)
    for copy in gives:
        copy.wait()


def scratch_plan(lines, x_ref, qkv_ref, up_ref, out_ref, down_ref):
    rows, width = x_ref.shape
    up_rows = up_ref.shape[0]
    own_cols, up_cols = qkv_ref.shape[1] // 8, up_ref.shape[1] // 8
    hidden = up_cols // 2
    half_head = out_ref.shape[0]
    down_rows = down_ref.shape[0]
    lanes = own_cols // 3
    groups = 4 * lines
    plane = (8, rows, width)
    vm = lambda shape, kind=BF: pltpu.VMEM(shape, kind)
    sem = lambda count: pltpu.SemaphoreType.DMA((2, count))
    plan = dict(
        ids=vm((8, 8, rows), jnp.int32),
        conds=vm((groups, 8, 128), F32),
        tokens=vm(plane),
        cots=vm(plane),
        normed=vm(plane),
        ffn=vm(plane),
        branch=vm(plane),
        qkv_cols=vm((8, up_rows, own_cols)),
        up_cols=vm((8, up_rows, up_cols)),
        qkv_line=vm((lines, 8, up_rows, own_cols)),
        up_line=vm((lines, 8, up_rows, up_cols)),
        out_line=vm((lines, half_head, width)),
        down_line=vm((lines, down_rows, width)),
        out_half=vm((2, half_head, width)),
        out_full=vm((2, 2, half_head, width)),
        mod_full=vm((128, 2 * width)),
        mod_terms=vm((8, groups, width // 4), F32),
        mod_in=vm((8, groups, width // 4), F32),
        mod_line=vm((lines, groups, width // 4), F32),
        mod_total=vm((groups, width // 4), F32),
        mods=vm((8, 8, width // 4), F32),
        scales=vm((8, 2 * width), F32),
        turns=vm((4, 2 * rows, 2 * lanes), F32),
        raw=vm((4, 2, 2 * rows, lanes), F32),
        rotated=vm((4, 3, 2 * rows, lanes)),
        probs=vm((4, 2, 2 * rows, 2 * rows), F32),
        raw_attended=vm((4, 2 * rows, lanes), F32),
        attended=vm((4, 2 * rows, lanes)),
        middle=vm((rows, width), F32),
        grad_middle=vm((rows, width), F32),
        hidden=vm((4, 2 * rows, hidden)),
        act=vm((4, 2 * rows, hidden), F32),
        slope=vm((4, 2 * rows, hidden), F32),
        grad_up=vm((4, 2 * rows, up_cols)),
        grad_qkv=vm((4, 2 * rows, own_cols)),
        head_terms=vm((1, lanes), F32),
        sums_own=vm((24, 128), F32),
        sums_plane=vm((8, 24, 128), F32),
        sums=vm((groups, 24, 128), F32),
        cond_all=vm((groups, 128), F32),
        cond_line=vm((lines, 8, 128), F32),
        cond_in=vm((8, lines, 8, 128), F32),
        down_total=vm((down_rows, width), F32),
        up_total=vm((8, up_rows, up_cols), F32),
        qkv_total=vm((8, up_rows, own_cols), F32),
        out_total=vm((half_head, width), F32),
        down_term=vm((lines, down_rows, width)),
        down_in=vm((4, down_rows, width)),
        up_term=vm((lines, 8, up_rows, up_cols)),
        up_in=vm((4, 8, up_rows, up_cols)),
        up_sum=vm((8, up_rows, up_cols)),
        up_back=vm((8, up_rows, up_cols)),
        qkv_term=vm((lines, 8, up_rows, own_cols)),
        qkv_in=vm((4, 8, up_rows, own_cols)),
        qkv_sum=vm((8, up_rows, own_cols)),
        qkv_back=vm((8, up_rows, own_cols)),
        out_halves=vm((2, 2, half_head, width)),
        out_swap=vm((2, half_head, width)),
        out_terms=vm((lines, half_head, width)),
        out_in=vm((4, half_head, width)),
    )
    for name in ("mid", "gnf", "out", "gna"):
        plan[name + "_part"] = vm(plane)
        plan[name + "_pair"] = vm((4, rows, width))
        plan[name + "_far"] = vm((2, rows // 2, width))
        plan[name + "_chip"] = vm((2, rows, width))
        plan["sem_" + name] = sem(10)
    plan.update(
        sem_tokens=sem(10),
        sem_cots=sem(10),
        sem_ffn=sem(10),
        sem_branch=sem(10),
        sem_ids=sem(7),
        sem_qkv_spread=sem(7),
        sem_up_spread=sem(7),
        sem_mod_spread=sem(7),
        sem_mods=sem(7),
        sem_up_back=sem(7),
        sem_qkv_back=sem(7),
        sem_cond_share=sem(7),
        sem_qkv_line=pltpu.SemaphoreType.DMA((2, 2, 5)),
        sem_up_line=pltpu.SemaphoreType.DMA((2, 2, 5)),
        sem_out_line=sem(5),
        sem_down_line=sem(5),
        sem_mod_line=sem(lines - 1),
        sem_cond_line=sem(lines - 1),
        sem_down_fold=sem(5),
        sem_up_fold=sem(5),
        sem_qkv_fold=pltpu.SemaphoreType.DMA((2, 2, 5)),
        sem_out_fold=sem(5),
        sem_cond=sem(15),
        sem_sums=sem(lines - 1),
        sem_sums_share=sem(7),
        sem_half=sem(2),
    )
    return plan


def turn_tables(heads, lines):
    head_size = 64
    table = np.zeros((heads, 2, 16, 2, head_size), np.float64)
    for axis in range(2):
        for j in range(8):
            freq = math.pi * 10.0 ** ((j * heads + np.arange(heads)) / (8.0 * heads))
            unit = (2.0 * np.arange(16) + 1.0) / 16.0 - 1.0
            angle = freq[:, None].astype(np.float32) * unit[None, :].astype(np.float32)
            angle = angle.astype(np.float64)
            for half in range(2):
                at = axis * 16 + half * 8 + j
                table[:, axis, :, 0, at] = np.cos(angle)
                table[:, axis, :, 1, at] = np.sin(angle) * (1.0 if half else -1.0)
    table[:, 0, :, 0, 32:] = 1.0
    high = table.astype(ml_dtypes.bfloat16)
    low = (table - high.astype(np.float64)).astype(ml_dtypes.bfloat16)
    parts = []
    for term in (high, low):
        term = term.reshape(2, 2, 2, 2, 2, 16, 2, head_size)
        term = term.transpose(2, 3, 0, 4, 5, 6, 1, 7)
        parts.append(term.reshape(8, 32, 4 * head_size))
    return np.concatenate(parts, axis=1)


def plane_shards(
    block_in,
    conditioning,
    crop_ids,
    positions,
    qkv_weight,
    out_weight,
    up_weight,
    down_weight,
    attn_modulate,
    ffn_modulate,
    head_scale,
    cotangent,
):
    lines = lax.axis_size("dp") // 4
    rows, width = block_in.shape[1:]
    heads = head_scale.shape[0]
    tables = jnp.asarray(turn_tables(heads, lines))
    kinds = jax.ShapeDtypeStruct
    operands = (
        block_in[0],
        cotangent[0],
        qkv_weight,
        up_weight,
        out_weight,
        down_weight,
        attn_modulate,
        ffn_modulate,
        conditioning,
        crop_ids,
        positions,
        head_scale,
        tables,
    )
    plan = scratch_plan(lines, operands[0], qkv_weight, up_weight, out_weight, down_weight)
    in_vmem = pl.BlockSpec(memory_space=pltpu.VMEM)
    in_specs = [in_vmem] * len(operands)
    in_specs[11] = pl.BlockSpec(memory_space=pltpu.SMEM)
    shapes = (
    kinds((rows, width), BF),
    kinds((rows, width), F32),
    kinds(conditioning.shape, F32),
    kinds(qkv_weight.shape, F32),
    kinds(out_weight.shape, F32),
    kinds(up_weight.shape, F32),
    kinds(down_weight.shape, F32),
    kinds(attn_modulate.shape, F32),
    kinds(ffn_modulate.shape, F32),
    kinds((1, heads), F32),
)
    results = pl.pallas_call(
        functools.partial(block_kernel, lines),
        out_shape=shapes,
        in_specs=in_specs,
        out_specs=[pl.BlockSpec(memory_space=pl.ANY)] * 10,
        scratch_shapes=[pltpu.VMEM(kind.shape, kind.dtype) for kind in shapes]
        + list(plan.values())
        + [pltpu.SemaphoreType.DMA((10,))],
        compiler_params=pltpu.CompilerParams(
            collective_id=0, has_side_effects=True, vmem_limit_bytes=63 * 2**20
        ),
    )(*operands)
    results = settle(results)
    return tuple(item[None] for item in results[:2]) + tuple(results[2:-1]) + (results[-1][0],)


def settle(results):
    count = len(results)

    def kernel(*refs):
        held, sems = refs[2 * count : -1], refs[-1]
        loads = [
            pltpu.make_async_copy(refs[k], held[k], sems.at[0, k]) for k in range(count)
        ]
        stores = [
            pltpu.make_async_copy(held[k], refs[count + k], sems.at[1, k]) for k in range(count)
        ]
        for copy in loads:
            copy.start()
        for load, store in zip(loads, stores):
            load.wait()
            store.start()
        for copy in stores:
            copy.wait()

    anywhere = pl.BlockSpec(memory_space=pl.ANY)
    return pl.pallas_call(
        kernel,
        out_shape=tuple(jax.ShapeDtypeStruct(item.shape, item.dtype) for item in results),
        in_specs=[anywhere] * count,
        out_specs=[anywhere] * count,
        scratch_shapes=[pltpu.VMEM(item.shape, item.dtype) for item in results]
        + [pltpu.SemaphoreType.DMA((2, count))],
    )(*results)


def in_planes(mesh):
    return mesh.shape["seq"] == 2 and mesh.shape["dp"] == 16


def solution(mesh):
    in_specs = (
        P("dp", "seq", None),
        P("dp", None),
        P("dp", "seq"),
        P("dp", None, "seq"),
        P(("dp", "seq"), None),
        P(("dp", "seq"), None),
        P(("dp", "seq"), None),
        P(("dp", "seq"), None),
        P(("dp", "seq"), None),
        P(("dp", "seq"), None),
        P(),
        P("dp", "seq", None),
    )
    out_specs = (
        P("dp", "seq", None),
        P("dp", "seq", None),
        P("dp", None),
        P(("dp", "seq"), None),
        P(("dp", "seq"), None),
        P(("dp", "seq"), None),
        P(("dp", "seq"), None),
        P(("dp", "seq"), None),
        P(("dp", "seq"), None),
        P(),
    )
    body = plane_shards if in_planes(mesh) else shards
    return jax.shard_map(body, mesh=mesh, in_specs=in_specs, out_specs=out_specs, check_vma=False)
```

```python
import functools
import math
import types

import jax
import jax.numpy as jnp
import ml_dtypes
import numpy as np
from jax import lax
from jax.experimental import pallas as pl
from jax.experimental.pallas import tpu as pltpu
from jax.sharding import PartitionSpec as P

eps_norm = 1e-06
eps_cosine = 1e-06
negative = -1e30
key_rows = 256


def block_split(count, limit):
    size_rows = math.gcd(count, limit)
    return (size_rows, count // size_rows)


def rope_tables(positions, heads):
    unit_pos = (2.0 * positions.astype(jnp.float32) + 1.0) / 16.0 - 1.0
    exponent = (
        jnp.arange(8, dtype=jnp.float32)[None, :] * heads
        + jnp.arange(heads, dtype=jnp.float32)[:, None]
    ) / (8.0 * heads)
    frequency = math.pi * 10.0**exponent
    angles = jnp.moveaxis(unit_pos[..., None, None] * frequency, -4, -2)
    return (jnp.cos(angles), jnp.sin(angles))


def rotate(vector, cosine, sine):
    leading = vector.shape[:-1]
    turned_part = vector[..., :32].reshape(leading + (2, 2, 8))
    first_half = turned_part[..., 0, :]
    second_half = turned_part[..., 1, :]
    turned = jnp.stack(
        [first_half * cosine - second_half * sine, first_half * sine + second_half * cosine],
        axis=-2,
    )
    return jnp.concatenate([turned.reshape(leading + (32,)), vector[..., 32:]], axis=-1)


def norm_forward(value, scale):
    inverse = lax.rsqrt(jnp.mean(value * value, axis=-1, keepdims=True) + eps_norm)
    return (value * inverse * scale[:, None], inverse)


def norm_backward(value, inverse, scale, grad_norm):
    scaled = grad_norm * scale[:, None]
    grad_value = inverse * scaled - value * inverse**3 * jnp.mean(
        scaled * value, axis=-1, keepdims=True
    )
    grad_scale = jnp.sum(grad_norm * value * inverse, axis=1)
    return (grad_value, grad_scale)


def cosine_forward(value, root_scale):
    factor = root_scale[:, None] * lax.rsqrt(
        jnp.sum(value * value, axis=-1, keepdims=True) + eps_cosine
    )
    return (value * factor, factor)


def cosine_backward(value, factor, grad):
    squares = jnp.sum(value * value, axis=-1, keepdims=True) + eps_cosine
    along = jnp.sum(grad * value, axis=-1, keepdims=True)
    grad_value = factor * grad - value * factor * along / squares
    return (grad_value, jnp.sum(along * factor, axis=(0, 1, 3)))


def geglu(value_part, gate_part):
    return value_part * jax.nn.gelu(gate_part, approximate=False)


def pair_grads(queries, grad_att, log_total, deltas, query_crop, key_block, value_block, key_crop):
    scores = jnp.einsum("cqhd,ckhd->cqhk", queries, key_block, preferred_element_type=jnp.float32)
    allowed = (query_crop[:, :, None] == key_crop[:, None, :])[:, :, None, :]
    probs = jnp.exp(jnp.where(allowed, scores - log_total[..., None], negative))
    probs = jnp.where(allowed, probs, 0.0)
    dotted = jnp.einsum(
        "cqhd,ckhd->cqhk", grad_att, value_block, preferred_element_type=jnp.float32
    )
    slope = (probs * (dotted - deltas[..., None])).astype(jnp.bfloat16)
    grad_q = jnp.einsum("cqhk,ckhd->cqhd", slope, key_block, preferred_element_type=jnp.float32)
    grad_k = jnp.einsum("cqhk,cqhd->ckhd", slope, queries, preferred_element_type=jnp.float32)
    grad_v = jnp.einsum(
        "cqhk,cqhd->ckhd", probs.astype(jnp.bfloat16), grad_att, preferred_element_type=jnp.float32
    )
    return (grad_q, grad_k, grad_v)


def pack_terms(terms, lead_shape):
    return jnp.concatenate([term.reshape(lead_shape + (-1,)) for term in terms], axis=-1)


def unpack_terms(packed_row, terms, owners):
    results = []
    offset = 0
    for term in terms:
        own_rows = term.shape[0] // owners
        count = own_rows * term.shape[1]
        results.append(packed_row[offset : offset + count].reshape(own_rows, term.shape[1]))
        offset = offset + count
    return results


def shards(
    block_in,
    conditioning,
    crop_ids,
    positions,
    qkv_weight,
    out_weight,
    up_weight,
    down_weight,
    attn_modulate,
    ffn_modulate,
    head_scale,
    cotangent,
):
    qkv_full, out_full, up_full, down_full, attn_mod, ffn_mod = (
        lax.all_gather(qkv_weight, ("dp", "seq"), axis=0, tiled=True),
        lax.all_gather(out_weight, ("dp", "seq"), axis=0, tiled=True),
        lax.all_gather(up_weight, ("dp", "seq"), axis=0, tiled=True),
        lax.all_gather(down_weight, ("dp", "seq"), axis=0, tiled=True),
        lax.all_gather(attn_modulate, ("dp", "seq"), axis=0, tiled=True),
        lax.all_gather(ffn_modulate, ("dp", "seq"), axis=0, tiled=True),
    )
    canvases, rows, width = block_in.shape
    heads = head_scale.shape[0]
    head_size = width // heads
    hidden_width = down_full.shape[0]
    seq_count = lax.axis_size("seq")
    inputs = block_in.astype(jnp.float32)
    scale_attn = 1.0 + jnp.dot(conditioning, attn_mod, preferred_element_type=jnp.float32)
    scale_ffn = 1.0 + jnp.dot(conditioning, ffn_mod, preferred_element_type=jnp.float32)
    normed_attn, inverse_attn = norm_forward(inputs, scale_attn)
    normed_attn = normed_attn.astype(jnp.bfloat16)
    qkv_all = jnp.einsum(
        "csd,de->cse", normed_attn, qkv_full, preferred_element_type=jnp.float32
    ).reshape(canvases, rows, 3, heads, head_size)
    root_scale = jnp.sqrt(head_scale)
    query_cos, query_factor = cosine_forward(qkv_all[:, :, 0], root_scale)
    key_cos, key_factor = cosine_forward(qkv_all[:, :, 1], root_scale)
    cosine, sine = rope_tables(positions, heads)
    queries = rotate(query_cos, cosine, sine).astype(jnp.bfloat16)
    keys_flat = rotate(key_cos, cosine, sine).astype(jnp.bfloat16).reshape(canvases, rows, width)
    values_flat = qkv_all[:, :, 2].astype(jnp.bfloat16).reshape(canvases, rows, width)
    start_state = (
        jnp.full((canvases, rows, heads), negative, jnp.float32),
        jnp.zeros((canvases, rows, heads), jnp.float32),
        jnp.zeros((canvases, rows, heads, head_size), jnp.float32),
    )
    state_now = start_state
    piece_keys = lax.all_gather(keys_flat, "seq", axis=1, tiled=True)
    piece_values = lax.all_gather(values_flat, "seq", axis=1, tiled=True)
    piece_crop = lax.all_gather(crop_ids, "seq", axis=1, tiled=True)
    size_rows, number = block_split(piece_keys.shape[1], key_rows)

    def step_block(state, block_index):
        running_max, row_total, weighted = state
        offset = block_index * size_rows
        key_block = lax.dynamic_slice_in_dim(piece_keys, offset, size_rows, 1).reshape(
            canvases, size_rows, heads, head_size
        )
        value_block = lax.dynamic_slice_in_dim(piece_values, offset, size_rows, 1).reshape(
            canvases, size_rows, heads, head_size
        )
        crop_block = lax.dynamic_slice_in_dim(piece_crop, offset, size_rows, 1)
        scores = jnp.einsum(
            "cqhd,ckhd->cqhk", queries, key_block, preferred_element_type=jnp.float32
        )
        allowed = (crop_ids[:, :, None] == crop_block[:, None, :])[:, :, None, :]
        scores = jnp.where(allowed, scores, negative)
        new_max = jnp.maximum(running_max, jnp.max(scores, axis=-1))
        weights = jnp.where(allowed, jnp.exp(scores - new_max[..., None]), 0.0)
        shrink = jnp.exp(running_max - new_max)
        row_total = row_total * shrink + jnp.sum(weights, axis=-1)
        weighted = weighted * shrink[..., None] + jnp.einsum(
            "cqhk,ckhd->cqhd",
            weights.astype(jnp.bfloat16),
            value_block,
            preferred_element_type=jnp.float32,
        )
        return ((new_max, row_total, weighted), None)

    state_now, unused = lax.scan(step_block, state_now, jnp.arange(number))
    running_max, row_total, weighted = state_now
    log_total = running_max + jnp.log(row_total)
    attended_raw = weighted / row_total[..., None]
    attended = attended_raw.astype(jnp.bfloat16).reshape(canvases, rows, width)
    middle = inputs + jnp.einsum(
        "csd,de->cse", attended, out_full, preferred_element_type=jnp.float32
    )
    normed_ffn, inverse_ffn = norm_forward(middle, scale_ffn)
    normed_ffn = normed_ffn.astype(jnp.bfloat16)
    up_all = jnp.einsum("csd,de->cse", normed_ffn, up_full, preferred_element_type=jnp.float32)
    value_part = up_all[..., :hidden_width]
    gate_part = up_all[..., hidden_width:]
    hidden = geglu(value_part, gate_part).astype(jnp.bfloat16)
    block_out = (
        middle + jnp.einsum("csf,fd->csd", hidden, down_full, preferred_element_type=jnp.float32)
    ).astype(jnp.bfloat16)
    down_term = jnp.einsum("csf,csd->fd", hidden, cotangent, preferred_element_type=jnp.float32)
    grad_hidden = jnp.einsum(
        "csd,fd->csf", cotangent, down_full, preferred_element_type=jnp.float32
    )
    unused_value, geglu_pull = jax.vjp(geglu, value_part, gate_part)
    grad_value, grad_gate = geglu_pull(grad_hidden)
    grad_up = jnp.concatenate([grad_value, grad_gate], axis=-1).astype(jnp.bfloat16)
    up_term = jnp.einsum("csd,cse->de", normed_ffn, grad_up, preferred_element_type=jnp.float32)
    grad_normed_ffn = jnp.einsum(
        "cse,de->csd", grad_up, up_full, preferred_element_type=jnp.float32
    )
    grad_mid_norm, ffn_scale_sum = norm_backward(middle, inverse_ffn, scale_ffn, grad_normed_ffn)
    grad_middle = cotangent.astype(jnp.float32) + grad_mid_norm
    grad_branch = grad_middle.astype(jnp.bfloat16)
    out_term = jnp.einsum("csd,cse->de", attended, grad_branch, preferred_element_type=jnp.float32)
    grad_attended = (
        jnp.einsum("cse,de->csd", grad_branch, out_full, preferred_element_type=jnp.float32)
        .astype(jnp.bfloat16)
        .reshape(canvases, rows, heads, head_size)
    )
    deltas = jnp.sum(grad_attended.astype(jnp.float32) * attended_raw, axis=-1)
    start_back = (
        jnp.zeros((canvases, rows, heads, head_size), jnp.float32),
        jnp.zeros((canvases, rows * seq_count, 2 * width), jnp.float32),
    )
    state_now = start_back
    fold_piece_keys = lax.all_gather(keys_flat, "seq", axis=1, tiled=True)
    fold_piece_values = lax.all_gather(values_flat, "seq", axis=1, tiled=True)
    fold_piece_crop = lax.all_gather(crop_ids, "seq", axis=1, tiled=True)
    fold_size_rows, number = block_split(fold_piece_keys.shape[1], key_rows)

    def step_block(state, block_index):
        grad_q_sum, grad_kv_all = state
        offset = block_index * fold_size_rows
        key_block = lax.dynamic_slice_in_dim(fold_piece_keys, offset, fold_size_rows, 1).reshape(
            canvases, fold_size_rows, heads, head_size
        )
        value_block = lax.dynamic_slice_in_dim(
            fold_piece_values, offset, fold_size_rows, 1
        ).reshape(canvases, fold_size_rows, heads, head_size)
        crop_block = lax.dynamic_slice_in_dim(fold_piece_crop, offset, fold_size_rows, 1)
        grad_q, grad_k, grad_v = pair_grads(
            queries, grad_attended, log_total, deltas, crop_ids, key_block, value_block, crop_block
        )
        update = jnp.concatenate(
            [
                grad_k.reshape(canvases, fold_size_rows, width),
                grad_v.reshape(canvases, fold_size_rows, width),
            ],
            axis=-1,
        )
        previous = lax.dynamic_slice_in_dim(grad_kv_all, offset, fold_size_rows, 1)
        grad_kv_all = lax.dynamic_update_slice_in_dim(grad_kv_all, previous + update, offset, 1)
        return ((grad_q_sum + grad_q, grad_kv_all), None)

    state_now, unused = lax.scan(step_block, state_now, jnp.arange(number))
    grad_queries, grad_kv_all = state_now
    grad_kv = lax.psum_scatter(
        grad_kv_all.astype(jnp.bfloat16), "seq", scatter_dimension=1, tiled=True
    ).astype(jnp.float32)
    grad_keys = grad_kv[..., :width].reshape(canvases, rows, heads, head_size)
    grad_values = grad_kv[..., width:].reshape(canvases, rows, heads, head_size)
    grad_query_cos = rotate(grad_queries, cosine, -sine)
    grad_key_cos = rotate(grad_keys, cosine, -sine)
    grad_query_raw, query_part = cosine_backward(qkv_all[:, :, 0], query_factor, grad_query_cos)
    grad_key_raw, key_part = cosine_backward(qkv_all[:, :, 1], key_factor, grad_key_cos)
    scale_local = (query_part + key_part) / (2.0 * head_scale)
    grad_qkv = (
        jnp.stack([grad_query_raw, grad_key_raw, grad_values], axis=2)
        .astype(jnp.bfloat16)
        .reshape(canvases, rows, 3 * width)
    )
    qkv_term = jnp.einsum("csd,cse->de", normed_attn, grad_qkv, preferred_element_type=jnp.float32)
    grad_normed_attn = jnp.einsum(
        "cse,de->csd", grad_qkv, qkv_full, preferred_element_type=jnp.float32
    )
    grad_in_norm, attn_scale_sum = norm_backward(inputs, inverse_attn, scale_attn, grad_normed_attn)
    input_grad = grad_middle + grad_in_norm
    attn_sums, ffn_sums = lax.psum((attn_scale_sum, ffn_scale_sum), "seq")
    attn_sums = attn_sums.astype(jnp.bfloat16)
    ffn_sums = ffn_sums.astype(jnp.bfloat16)
    cond_grad = jnp.einsum(
        "cd,nd->cn", attn_sums, attn_mod, preferred_element_type=jnp.float32
    ) + jnp.einsum("cd,nd->cn", ffn_sums, ffn_mod, preferred_element_type=jnp.float32)
    leader = lax.axis_index("seq") == 0
    attn_mod_term = jnp.where(
        leader,
        jnp.einsum("cn,cd->nd", conditioning, attn_sums, preferred_element_type=jnp.float32),
        0.0,
    )
    ffn_mod_term = jnp.where(
        leader,
        jnp.einsum("cn,cd->nd", conditioning, ffn_sums, preferred_element_type=jnp.float32),
        0.0,
    )
    terms = (qkv_term, out_term, up_term, down_term, attn_mod_term, ffn_mod_term)
    groups = lax.axis_size("dp")
    owners = groups * seq_count
    packed = pack_terms(terms, (owners,))
    summed = lax.psum_scatter(packed, ("dp", "seq"), scatter_dimension=0, tiled=True)
    packed_row = summed[0]
    qkv_grad, out_grad, up_grad, down_grad, attnmod_grad, ffnmod_grad = unpack_terms(
        packed_row, terms, owners
    )
    scale_grad = lax.psum(scale_local, ("dp", "seq"))
    return (
        block_out,
        input_grad,
        cond_grad,
        qkv_grad,
        out_grad,
        up_grad,
        down_grad,
        attnmod_grad,
        ffnmod_grad,
        scale_grad,
    )


MESH = pl.DeviceIdType.MESH
BF = jnp.bfloat16
F32 = jnp.float32
PLANE = ((1, 0, 0), (0, 0, 1), (1, 0, 1), (0, 1, 0), (1, 1, 0), (0, 1, 1), (1, 1, 1))
SAME_Y = tuple(
    (step, along)
    for along in (1, 3, 2, 0)
    for step in ((0, 0, 0), (1, 0, 0), (0, 1, 0), (1, 1, 0))
    if along or step != (0, 0, 0)
)
OTHERS = tuple((step, along) for along in (1, 3, 2) for step in ((0, 0, 0),) + PLANE)
OTHERS += tuple((step, 0) for step in PLANE)
TO_X, TO_Y, TO_FAR = (1, 0, 0), (0, 0, 1), (1, 0, 1)
ERF_P = (
    0.00022905065861350646,
    0.0034082910107109506,
    0.050955695062380861,
    0.18520832239976145,
    1.128379143519084,
)
ERF_Q = (
    -1.1791602954361697e-7,
    0.000023547966471313185,
    0.0010179625278914885,
    0.014070470171167667,
    0.11098505178285362,
    0.49746925110067538,
    1.0,
)


def erf(value):
    value = jnp.clip(value, -3.832506856900711, 3.832506856900711)
    square = value * value
    top = jnp.full_like(value, ERF_P[0])
    for term in ERF_P[1:]:
        top = top * square + term
    bottom = jnp.full_like(value, ERF_Q[0])
    for term in ERF_Q[1:]:
        bottom = bottom * square + term
    return value * top / bottom


def dot(lhs, rhs, on_lhs=1, on_rhs=0):
    return lax.dot_general(
        lhs, rhs, (((on_lhs,), (on_rhs,)), ((), ())), preferred_element_type=F32
    )


def block_kernel(
    lines,
    x_ref,
    cot_ref,
    qkv_ref,
    up_ref,
    out_ref,
    down_ref,
    amod_ref,
    fmod_ref,
    cond_ref,
    crop_ref,
    pos_ref,
    scale_ref,
    table_ref,
    *results_and_scratch,
):
    targets, held = results_and_scratch[:10], results_and_scratch[10:20]
    scratch, give_sems = results_and_scratch[20:-1], results_and_scratch[-1]
    block_out, input_grad, cond_grad, qkv_grad, out_grad = held[:5]
    up_grad, down_grad, amod_grad, fmod_grad, scale_grad = held[5:]
    gives = [pltpu.make_async_copy(held[k], targets[k], give_sems.at[k]) for k in range(10)]
    names = list(scratch_plan(lines, x_ref, qkv_ref, up_ref, out_ref, down_ref))
    s = types.SimpleNamespace(**dict(zip(names, scratch)))
    dp = lax.axis_index("dp")
    y = lax.axis_index("seq")
    z = dp // 4
    x = (dp // 2) % 2
    c = dp % 2
    rows, width = x_ref.shape
    up_rows = up_ref.shape[0]
    own_cols = qkv_ref.shape[1] // 8
    lanes = own_cols // 3
    half_head = out_ref.shape[0]
    hidden = up_ref.shape[1] // 16
    down_rows = down_ref.shape[0]
    mod_rows = amod_ref.shape[0]
    canvas_rows = 2 * rows
    crops = canvas_rows // 16
    me = 4 * x + 2 * c + y
    device_index = 8 * z + me

    def member(step):
        return 4 * ((x + step[0]) % 2) + 2 * ((c + step[1]) % 2) + (y + step[2]) % 2

    def device(step, along=0):
        return (
            ((z + along) % lines) * 4 + ((x + step[0]) % 2) * 2 + (c + step[1]) % 2,
            (y + step[2]) % 2,
        )

    def line_device(along):
        return (jnp.clip(z + along, 0, lines - 1) * 4 + dp % 4, y)

    def inside(along):
        return z + along < lines if along > 0 else z + along >= 0

    here = (0, 0, 0)
    core = (0, 1, 0)
    sends = []

    class Copy:
        def __init__(self, src, dst_there, dst_here, sems, at, target):
            self.out = pltpu.make_async_remote_copy(
                src_ref=src,
                dst_ref=dst_there,
                send_sem=sems.at[0, at],
                recv_sem=sems.at[1, at],
                device_id=target,
                device_id_type=MESH,
            )
            self.into = pltpu.make_async_remote_copy(
                src_ref=src,
                dst_ref=dst_here,
                send_sem=sems.at[0, at],
                recv_sem=sems.at[1, at],
                device_id=target,
                device_id_type=MESH,
            )

        def start(self, when=None):
            if when is None:
                self.out.start()
            else:
                pl.when(when)(self.out.start)
            sends.append((self.out, when))

        def arrive(self):
            self.into.wait_recv()

    class Gather:
        def __init__(self, buffer, sems):
            at = lambda step: buffer.at[member(step)]
            half = buffer.shape[1] // 2
            rows_of = (pl.ds(0, half), pl.ds(half, half))
            part = lambda step, k: buffer.at[member(step), rows_of[k]]
            self.x_own = [
                Copy(part(here, k), part(here, k), part(TO_X, k), sems, k, device(TO_X))
                for k in range(2)
            ]
            self.y_own = [
                Copy(part(here, k), part(here, k), part(TO_Y, k), sems, 2 + k, device(TO_Y))
                for k in range(2)
            ]
            self.y_far = Copy(part(TO_X, 0), part(TO_X, 0), part(TO_FAR, 0), sems, 4, device(TO_Y))
            self.x_far = Copy(part(TO_Y, 1), part(TO_Y, 1), part(TO_FAR, 1), sems, 5, device(TO_X))
            self.pair = Copy(at(here), at(here), at(core), sems, 6, device(core))
            self.cross = [
                Copy(at(step), at(step), at((step[0], 1, step[2])), sems, 7 + k, device(core))
                for k, step in enumerate((TO_X, TO_Y, TO_FAR))
            ]

        def start(self):
            self.x_own[0].start()
            self.y_own[1].start()
            self.x_own[1].start()
            self.y_own[0].start()
            self.pair.start()

        def turn(self):
            self.x_own[0].arrive()
            self.y_far.start()
            self.y_own[1].arrive()
            self.x_far.start()

        def near(self):
            self.y_own[0].arrive()
            self.cross[1].start()
            self.x_own[1].arrive()
            self.cross[0].start()

        def far(self):
            self.y_far.arrive()
            self.x_far.arrive()
            self.cross[2].start()

        def pair_near(self):
            self.pair.arrive()
            self.cross[1].arrive()

        def pair_far(self):
            self.cross[0].arrive()
            self.cross[2].arrive()

        def finish(self):
            self.near()
            self.far()
            self.pair_near()
            self.pair_far()

        def steps(self):
            return {0: self.near, 1: self.pair_near, 2: self.far, 3: self.pair_far}

    class Reduce:
        def __init__(self, part, pair_in, far_in, chip_in, sems):
            self.part, self.pair_in, self.far_in, self.chip_in = part, pair_in, far_in, chip_in
            half = part.shape[1] // 2
            self.rows_of = rows_of = (pl.ds(0, half), pl.ds(half, half))
            self.steps_of = (here, TO_X, TO_Y, TO_FAR)
            self.pair = [
                Copy(
                    part.at[member((step[0], 1, step[2]))],
                    pair_in.at[k],
                    pair_in.at[k],
                    sems,
                    k,
                    device(core),
                )
                for k, step in enumerate(self.steps_of)
            ]
            piece = lambda step, k: part.at[member(step), rows_of[k]]
            self.x_far = Copy(piece(TO_FAR, 0), far_in.at[0], far_in.at[0], sems, 4, device(TO_X))
            self.y_far = Copy(piece(TO_FAR, 1), far_in.at[1], far_in.at[1], sems, 5, device(TO_Y))
            into = lambda way, k: chip_in.at[way, rows_of[k]]
            self.x_own = [
                Copy(piece(TO_X, k), into(0, k), into(0, k), sems, 6 + k, device(TO_X))
                for k in range(2)
            ]
            self.y_own = [
                Copy(piece(TO_Y, k), into(1, k), into(1, k), sems, 8 + k, device(TO_Y))
                for k in range(2)
            ]

        def add_pair(self, k):
            self.pair[k].arrive()
            slot = member(self.steps_of[k])
            total = self.part[slot].astype(F32) + self.pair_in[k].astype(F32)
            self.part[slot] = total.astype(BF)

        def add_far(self, step, k):
            slot = member(step)
            total = self.part[slot, self.rows_of[k], :].astype(F32) + self.far_in[k].astype(F32)
            self.part[slot, self.rows_of[k], :] = total.astype(BF)

        def give_far(self):
            self.pair[3].start()
            self.pair[1].start()

        def send_far(self):
            self.add_pair(3)
            self.x_far.start()
            self.y_far.start()
            self.add_pair(1)
            self.x_own[0].start()

        def give_near(self):
            self.pair[2].start()
            self.pair[0].start()

        def send_near(self):
            self.add_pair(2)
            self.y_own[1].start()

        def steps(self):
            return {0: self.give_far, 1: self.send_far, 2: self.give_near, 3: self.send_near}

        def middle(self):
            self.x_far.arrive()
            self.add_far(TO_Y, 0)
            self.y_own[0].start()
            self.y_far.arrive()
            self.add_far(TO_X, 1)
            self.x_own[1].start()

        def finish(self):
            self.pair[0].arrive()
            total = self.part[me].astype(F32) + self.pair_in[0].astype(F32)
            for copies in (self.x_own, self.y_own):
                for copy in copies:
                    copy.arrive()
            return total + self.chip_in[0].astype(F32) + self.chip_in[1].astype(F32)

    class Spread:
        def __init__(self, source, target, sems):
            self.source, self.target = source, target
            self.copies = [
                Copy(
                    source.at[member(step)],
                    target.at[me],
                    target.at[member(step)],
                    sems,
                    k,
                    device(step),
                )
                for k, step in enumerate(PLANE)
            ]

        def start(self):
            for copy in self.copies:
                copy.start()
            self.target[me] = self.source[me]

        def finish(self):
            for copy in self.copies:
                copy.arrive()

    class Share:
        def __init__(self, buffer, sems, block=None):
            self.copies = [
                Copy(
                    buffer.at[me] if block is None else block,
                    buffer.at[me],
                    buffer.at[member(step)],
                    sems,
                    k,
                    device(step),
                )
                for k, step in enumerate(PLANE)
            ]

        def start(self):
            for copy in self.copies:
                copy.start()

        def finish(self):
            for copy in self.copies:
                copy.arrive()

    class Line:
        def __init__(self, buffer, sems, first=None):
            self.copies = []
            for along in range(1, lines):
                back = (z + lines - along) % lines
                if first is None:
                    mine, theirs = buffer.at[z], buffer.at[back]
                else:
                    mine, theirs = buffer.at[pl.ds(first * z, first)], buffer.at[pl.ds(first * back, first)]
                self.copies.append(Copy(mine, mine, theirs, sems, along - 1, device(here, along)))

        def start(self):
            for copy in self.copies:
                copy.start()

        def finish(self):
            for copy in self.copies:
                copy.arrive()

    class Relay:
        def __init__(self, buffer, sems):
            self.copies = {
                along: Copy(
                    buffer.at[z],
                    buffer.at[z],
                    buffer.at[jnp.clip(z - along, 0, lines - 1)],
                    sems,
                    at,
                    line_device(along),
                )
                for at, along in enumerate((1, -1, 2, -2))
            }
            self.onward = {
                along: Copy(
                    buffer.at[far], buffer.at[far], buffer.at[far], sems, 4, line_device(along)
                )
                for along, far in ((1, 0), (-1, lines - 1))
            }

        def start(self, steps=(2, -2, 1, -1)):
            for along in steps:
                self.copies[along].start(inside(along))

        def middle(self):
            @pl.when(z == 2)
            def up_line():
                self.copies[2].arrive()

            @pl.when(z == 1)
            def down_line():
                self.copies[-2].arrive()

            self.onward[1].start(z == 2)
            self.onward[-1].start(z == 1)

        def finish(self):
            pl.when(z >= 1)(self.copies[1].arrive)
            pl.when(z <= 2)(self.copies[-1].arrive)
            pl.when(z == 3)(self.copies[2].arrive)
            pl.when(z == 0)(self.copies[-2].arrive)
            pl.when(z == 3)(self.onward[1].arrive)
            pl.when(z == 0)(self.onward[-1].arrive)

    class Fold:
        def __init__(self, terms, landed, sems):
            self.terms, self.landed = terms, landed
            self.copies = {
                along: Copy(
                    terms.at[jnp.clip(z + along, 0, lines - 1)],
                    landed.at[min(at, 2)],
                    landed.at[min(at, 2)],
                    sems,
                    at,
                    line_device(along),
                )
                for at, along in enumerate((1, -1, 2, -2))
            }
            self.first = {
                along: Copy(
                    terms.at[far], landed.at[3], landed.at[3], sems, 4, line_device(along)
                )
                for along, far in ((1, lines - 1), (-1, 0))
            }

        def start(self):
            self.first[1].start(z == 0)
            self.first[-1].start(z == lines - 1)
            self.copies[2].start(z == 0)
            self.copies[-2].start(z == lines - 1)
            for along in (1, -1):
                self.copies[along].start(inside(along))

        def middle(self):
            for at, far, along in ((1, lines - 1, 1), (2, 0, -1)):

                @pl.when(z == at)
                def join():
                    self.first[along].arrive()
                    total = self.terms[far].astype(F32) + self.landed[3].astype(F32)
                    self.terms[far] = total.astype(BF)

                self.copies[2 * along].start(z == at)

        def finish(self, total):
            total[...] = self.terms[z].astype(F32)
            for at, (along, when) in enumerate(((1, z >= 1), (-1, z <= 2), (2, z >= 2), (-2, z <= 1))):

                @pl.when(when)
                def add():
                    self.copies[along].arrive()
                    total[...] += self.landed[min(at, 2)].astype(F32)

            return total[...]

    class Canvases:
        def __init__(self, buffer, sems):
            self.copies = []
            for at, (step, along) in enumerate(SAME_Y):
                from_there = device(step, lines - along)[0]
                self.copies.append(
                    Copy(
                        buffer.at[dp],
                        buffer.at[dp],
                        buffer.at[from_there],
                        sems,
                        at,
                        device(step, along),
                    )
                )

        def start(self):
            for copy in self.copies:
                copy.start()

        def finish(self):
            for copy in self.copies:
                copy.arrive()

    def each_canvas(body, near=True, before=None, after=None):
        def step(t, carry):
            for k, action in (before or {}).items():
                pl.when(t == k)(action)
            turn = t if near else 3 - t
            body(2 * ((x + (turn // 2)) % 2) + (c + turn) % 2)
            for k, action in (after or {}).items():
                pl.when(t == k)(action)
            return carry

        lax.fori_loop(0, 4, step, 0)

    def slots(t):
        return pl.ds(2 * t, 2)

    lane = lax.broadcasted_iota(jnp.int32, (1, lanes), 1)
    first_head = lane < lanes // 2
    first_part = (lane % 16) < 8

    def per_head(pair):
        return jnp.where(first_head, pair[0], pair[1])

    def head_sums(value):
        left = jnp.where(first_head, value, 0.0)
        right = jnp.where(first_head, 0.0, value)
        return (
            jnp.sum(left, axis=-1, keepdims=True),
            jnp.sum(right, axis=-1, keepdims=True),
        )

    def partner(value):
        return jnp.where(
            first_part, pltpu.roll(value, lanes - 8, 1), pltpu.roll(value, 8, 1)
        )

    barrier = pltpu.get_barrier_semaphore()
    partners = [device(step, along) for step, along in OTHERS]
    for target in partners:
        pl.semaphore_signal(barrier, inc=1, device_id=target, device_id_type=MESH)
    ids = s.ids
    ids[me] = jnp.zeros(ids.shape[1:], jnp.int32)
    ids[me, 0:1, :] = crop_ref[...]
    ids[me, 1:3, :] = pos_ref[0]
    conds = s.conds
    conds[dp] = jnp.zeros(conds.shape[1:], F32)
    for r in range(cond_ref.shape[1] // 128):
        conds[dp, r : r + 1, :] = cond_ref[:, 128 * r : 128 * (r + 1)].astype(F32)
    s.tokens[me] = x_ref[...]
    s.cots[me] = cot_ref[...]
    s.out_line[z] = out_ref[...]
    s.down_line[z] = down_ref[...]
    mod_full = s.mod_full
    mod_full[...] = jnp.zeros(mod_full.shape, BF)
    mod_full[0:mod_rows, 0:width] = amod_ref[...]
    mod_full[0:mod_rows, width : 2 * width] = fmod_ref[...]

    size = lanes // 2
    qkv_places = [
        (m, (2 * part + k) * size, part * width + (8 * (m % 2) + 4 * k + m // 2) * size)
        for m in range(8)
        for part in range(3)
        for k in range(2)
    ]
    up_places = [
        (m, (lines * part + k) * down_rows, part * 8 * hidden + (8 * k + m) * down_rows)
        for m in range(8)
        for part in range(2)
        for k in range(lines)
    ]
    for m, own, whole in qkv_places:
        s.qkv_cols[m, :, own : own + size] = qkv_ref[:, whole : whole + size]
    for m, own, whole in up_places:
        s.up_cols[m, :, own : own + down_rows] = up_ref[:, whole : whole + down_rows]
    pl.semaphore_wait(barrier, len(partners))

    cond_copy = Canvases(conds, s.sem_cond)
    ids_copy = Share(ids, s.sem_ids)
    qkv_spread = Spread(s.qkv_cols, s.qkv_line.at[z], s.sem_qkv_spread)
    up_spread = Spread(s.up_cols, s.up_line.at[z], s.sem_up_spread)
    qkv_line = [
        Relay(s.qkv_line.at[:, pl.ds(4 * k, 4)], s.sem_qkv_line.at[k]) for k in range(2)
    ]
    out_line = Relay(s.out_line, s.sem_out_line)
    up_line = [Relay(s.up_line.at[:, pl.ds(4 * k, 4)], s.sem_up_line.at[k]) for k in range(2)]
    down_line = Relay(s.down_line, s.sem_down_line)
    token_copy = Gather(s.tokens, s.sem_tokens)
    cot_copy = Gather(s.cots, s.sem_cots)
    cond_copy.start()
    qkv_spread.start()
    token_copy.start()
    out_line.start()
    qkv_spread.finish()
    qkv_line[0].start()
    cond_copy.finish()
    picked = jnp.zeros((conds.shape[0], 128), F32)
    for r in range(cond_ref.shape[1] // 128):
        at_row = lax.broadcasted_iota(jnp.int32, (128, 128), 0) + 128 * r
        at_col = lax.broadcasted_iota(jnp.int32, (128, 128), 1)
        choose = (at_row == at_col + mod_rows * device_index) & (at_col < mod_rows)
        picked = picked + dot(
            conds[:, r, :].astype(BF), jnp.where(choose, 1.0, 0.0).astype(BF)
        )
    cond_mine = picked.astype(BF)
    block_cols = 2 * width // 8
    mod_terms, mod_in = s.mod_terms, s.mod_in
    for m in range(8):
        mod_terms[m] = dot(cond_mine, mod_full[:, block_cols * m : block_cols * (m + 1)])
    mod_spread = Spread(mod_terms, mod_in, s.sem_mod_spread)
    mod_spread.start()
    token_copy.turn()
    mod_spread.finish()
    mod_sum = mod_in[0]
    for m in range(1, 8):
        mod_sum = mod_sum + mod_in[m]
    mod_line = s.mod_line
    mod_line[z] = mod_sum
    mod_copy = Line(mod_line, s.sem_mod_line)
    mod_copy.start()
    qkv_line[1].start()
    up_spread.start()
    ids_copy.start()
    qkv_line[0].middle()
    mod_copy.finish()
    mod_sum = mod_line[0]
    for k in range(1, lines):
        mod_sum = mod_sum + mod_line[k]
    s.mod_total[...] = 1.0 + mod_sum
    mod_share = Share(s.mods, s.sem_mods)
    own_rows = s.mod_total[pl.ds(8 * (z // 2), 8), :]
    s.mods[me] = own_rows
    mod_share.start()
    cot_copy.start()
    out_line.middle()
    mod_share.finish()
    scales = s.scales
    for m in range(8):
        scales[:, block_cols * m : block_cols * (m + 1)] = s.mods[m]

    def scale_row(canvas, ffn):
        row = scales[pl.ds(4 * (z % 2) + canvas, 1), :]
        return row[:, width:] if ffn else row[:, :width]

    own_canvas = 2 * x + c

    def inverse_rms(value):
        return lax.rsqrt(jnp.mean(value * value, axis=-1, keepdims=True) + eps_norm)

    normed = s.normed

    def norm_tokens(canvas):
        value = s.tokens[slots(canvas)].reshape(canvas_rows, width).astype(F32)
        scaled = value * inverse_rms(value) * scale_row(canvas, False)
        normed[slots(canvas)] = scaled.astype(BF).reshape(2, rows, width)

    each_canvas(norm_tokens, before=token_copy.steps())
    qkv_line[1].middle()
    up_spread.finish()
    for line in up_line:
        line.start()
    out_line.finish()
    out_half = s.out_half
    half_copy = Copy(
        s.out_line.at[pl.ds(2 * (1 - y), 2)],
        out_half,
        out_half,
        s.sem_half,
        0,
        device((0, 0, 1)),
    )
    half_copy.start()
    cot_copy.turn()
    ids_copy.finish()
    for line in qkv_line:
        line.finish()
    head_of = lambda k: 8 * y + 4 * k + 2 * x + c
    head_scales = [scale_ref[head_of(k)] for k in range(2)]
    scale_lanes = per_head(head_scales)
    root_lanes = jnp.sqrt(scale_lanes)

    def canvas_ids(canvas, row):
        return jnp.concatenate(
            [ids[2 * canvas, row : row + 1, :], ids[2 * canvas + 1, row : row + 1, :]], axis=1
        )

    def one_hot(row, count):
        return jnp.where(
            lax.broadcasted_iota(jnp.int32, (count, canvas_rows), 0) == row, 1.0, 0.0
        ).astype(BF)

    def attend(canvas):
        qkv = dot(
            normed[slots(canvas)].reshape(canvas_rows, width),
            s.qkv_line[...].reshape(width, own_cols),
        )
        places = [one_hot(canvas_ids(canvas, 1), 16), one_hot(canvas_ids(canvas, 2), 16)]
        turn = dot(jnp.concatenate(places + places, axis=0), table_ref[me], 0, 0)
        s.turns[canvas] = turn
        cosine, sine = turn[:, :lanes], turn[:, lanes:]
        rotated = []
        for part in range(2):
            raw = qkv[:, part * lanes : (part + 1) * lanes]
            s.raw[canvas, part] = raw
            sums = head_sums(raw * raw)
            factor = per_head([lax.rsqrt(value + eps_cosine) for value in sums]) * root_lanes
            turned = raw * factor
            turned = (turned * cosine + partner(turned) * sine).astype(BF)
            s.rotated[canvas, part] = turned
            rotated.append(turned)
        values = qkv[:, 2 * lanes :].astype(BF)
        s.rotated[canvas, 2] = values
        crop_hot = one_hot(canvas_ids(canvas, 0), crops)
        allowed = dot(crop_hot, crop_hot, 0, 0)
        heads = []
        for k in range(2):
            mine = first_head if k == 0 else jnp.logical_not(first_head)
            query = jnp.where(mine, rotated[0], jnp.zeros_like(rotated[0]))
            weights = jnp.exp(dot(query, rotated[1], 1, 1)) * allowed
            probs = weights / jnp.sum(weights, axis=-1, keepdims=True)
            s.probs[canvas, k] = probs
            heads.append(dot(probs.astype(BF), values))
        attended = per_head(heads)
        s.raw_attended[canvas] = attended
        attended = attended.astype(BF)
        s.attended[canvas] = attended
        value = dot(attended, out_full[...].reshape(lanes, width))
        s.mid_part[slots(canvas)] = value.astype(BF).reshape(2, rows, width)

    half_copy.arrive()
    out_full = s.out_full
    for k in range(2):
        out_full[k, y] = s.out_line[2 * y + k]
        out_full[k, 1 - y] = out_half[k]

    mid_reduce = Reduce(
        s.mid_part, s.mid_pair, s.mid_far, s.mid_chip, s.sem_mid
    )
    each_canvas(attend, False, after=mid_reduce.steps())
    mid_reduce.middle()
    cot_copy.finish()
    up_line[0].middle()
    middle = x_ref[...].astype(F32) + mid_reduce.finish()
    s.middle[...] = middle
    ffn_row = scale_row(own_canvas, True)
    s.ffn[me] = (middle * inverse_rms(middle) * ffn_row).astype(BF)
    ffn_copy = Gather(s.ffn, s.sem_ffn)
    ffn_copy.start()
    ffn_copy.turn()
    up_line[1].middle()
    down_line.start()
    for line in up_line:
        line.finish()

    def feed(canvas):
        up = dot(
            s.ffn[slots(canvas)].reshape(canvas_rows, width),
            s.up_line[...].reshape(width, 2 * hidden),
        )
        value, gate = up[:, :hidden], up[:, hidden:]
        cdf = 0.5 + 0.5 * erf(gate * math.sqrt(0.5))
        act = gate * cdf
        s.hidden[canvas] = (value * act).astype(BF)
        s.act[canvas] = act
        density = jnp.exp(-0.5 * gate * gate) * (1.0 / math.sqrt(2.0 * math.pi))
        s.slope[canvas] = value * (cdf + gate * density)

    each_canvas(feed, before=ffn_copy.steps())
    down_line.middle()

    def cots_of(canvas):
        return s.cots[slots(canvas)].reshape(canvas_rows, width)

    all_rows = 8 * rows
    chunk = 256

    def down_term(n, carry):
        cols = pl.ds(pl.multiple_of(n * chunk, chunk), chunk)
        term = dot(
            s.hidden[...].reshape(all_rows, hidden),
            s.cots[:, :, cols].reshape(all_rows, chunk),
            0,
            0,
        )
        s.down_term[:, :, cols] = term.astype(BF).reshape(lines, down_rows, chunk)
        return carry

    lax.fori_loop(0, width // chunk, down_term, 0)
    down_fold = Fold(s.down_term, s.down_in, s.sem_down_fold)
    down_fold.start()
    down_line.finish()

    def feed_back(canvas):
        grad_hidden = dot(cots_of(canvas), s.down_line[...].reshape(hidden, width), 1, 1)
        grad_up = jnp.concatenate(
            [grad_hidden * s.act[canvas], grad_hidden * s.slope[canvas]], axis=1
        ).astype(BF)
        s.grad_up[canvas] = grad_up
        part = dot(grad_up, s.up_line[...].reshape(width, 2 * hidden), 1, 1)
        s.gnf_part[slots(canvas)] = part.astype(BF).reshape(2, rows, width)

    gnf_reduce = Reduce(
        s.gnf_part, s.gnf_pair, s.gnf_far, s.gnf_chip, s.sem_gnf
    )
    each_canvas(feed_back, False, after=gnf_reduce.steps())
    gnf_reduce.middle()

    def up_term(k, carry):
        cols = pl.ds(pl.multiple_of(k * 8 * up_rows, 8 * up_rows), 8 * up_rows)
        term = dot(
            s.ffn[:, :, cols].reshape(all_rows, 8 * up_rows),
            s.grad_up[...].reshape(all_rows, 2 * hidden),
            0,
            0,
        )
        s.up_term[k] = term.astype(BF).reshape(8, up_rows, 2 * hidden)
        return carry

    lax.fori_loop(0, lines, up_term, 0)
    up_fold = Fold(s.up_term, s.up_in, s.sem_up_fold)
    up_fold.start()
    down_fold.middle()

    def norm_back(value, row, grad):
        inverse = inverse_rms(value)
        scaled = grad * row
        along = jnp.mean(scaled * value, axis=-1, keepdims=True)
        grad_value = inverse * scaled - value * (inverse * inverse * inverse) * along
        return grad_value, jnp.sum(grad * value * inverse, axis=0, keepdims=True)

    def put_row(target, offset, row):
        for r in range(width // 128):
            target[offset + r : offset + r + 1, :] = row[:, 128 * r : 128 * (r + 1)]

    grad_mid, ffn_sum = norm_back(s.middle[...], ffn_row, gnf_reduce.finish())
    grad_middle = cot_ref[...].astype(F32) + grad_mid
    s.grad_middle[...] = grad_middle
    s.branch[me] = grad_middle.astype(BF)
    branch_copy = Gather(s.branch, s.sem_branch)
    branch_copy.start()
    sums_own = s.sums_own
    put_row(sums_own, 8, ffn_sum)

    def to_out(canvas):
        part = dot(s.hidden[canvas], s.down_line[...].reshape(hidden, width))
        s.out_part[slots(canvas)] = part.astype(BF).reshape(2, rows, width)

    out_reduce = Reduce(
        s.out_part, s.out_pair, s.out_far, s.out_chip, s.sem_out
    )
    branch_copy.turn()
    each_canvas(to_out)
    branch_copy.finish()
    out_reduce.give_far()
    out_reduce.give_near()

    def attend_back(canvas):
        branch = s.branch[slots(canvas)].reshape(canvas_rows, width)
        grad_att = dot(branch, out_full[...].reshape(lanes, width), 1, 1).astype(BF)
        turn = s.turns[canvas]
        cosine, sine = turn[:, :lanes], turn[:, lanes:]
        query, key, values = (s.rotated[canvas, part] for part in range(3))
        deltas = head_sums(grad_att.astype(F32) * s.raw_attended[canvas])
        grads = [[], [], []]
        for k in range(2):
            mine = first_head if k == 0 else jnp.logical_not(first_head)
            probs = s.probs[canvas, k]
            one_head = jnp.where(mine, grad_att, jnp.zeros_like(grad_att))
            dotted = dot(one_head, values, 1, 1)
            slope = (probs * (dotted - deltas[k])).astype(BF)
            grads[0].append(dot(slope, key))
            grads[1].append(dot(slope, query, 0, 0))
            grads[2].append(dot(probs.astype(BF), grad_att, 0, 0))
        pieces = []
        for part in range(2):
            grad = per_head(grads[part])
            grad = grad * cosine - partner(grad) * sine
            raw = s.raw[canvas, part]
            squares = [value + eps_cosine for value in head_sums(raw * raw)]
            along = head_sums(grad * raw)
            inverse = [lax.rsqrt(value) for value in squares]
            factor = per_head(inverse) * root_lanes
            shrink = per_head([along[k] * inverse[k] * inverse[k] for k in range(2)])
            pieces.append(factor * grad - raw * factor * shrink)
            term = per_head([jnp.sum(along[k] * inverse[k], axis=0, keepdims=True) for k in range(2)])
            s.head_terms[...] += term * root_lanes / (2.0 * scale_lanes)
        pieces.append(per_head(grads[2]))
        grad_qkv = jnp.concatenate(pieces, axis=1).astype(BF)
        s.grad_qkv[canvas] = grad_qkv
        part = dot(grad_qkv, s.qkv_line[...].reshape(width, own_cols), 1, 1)
        s.gna_part[slots(canvas)] = part.astype(BF).reshape(2, rows, width)

    term = dot(
        s.attended[...].reshape(all_rows, lanes),
        s.branch[...].reshape(all_rows, width),
        0,
        0,
    ).astype(BF).reshape(2, 2, half_head, width)
    halves = s.out_halves
    for k in range(2):
        for half in range(2):
            halves[half, k] = term[k, half]
    swap = Copy(
        halves.at[1 - y], s.out_swap, s.out_swap, s.sem_half, 1, device((0, 0, 1))
    )
    swap.start()

    s.head_terms[...] = jnp.zeros((1, lanes), F32)
    gna_reduce = Reduce(
        s.gna_part, s.gna_pair, s.gna_far, s.gna_chip, s.sem_gna
    )
    each_canvas(attend_back, False, after=gna_reduce.steps())
    up_fold.middle()
    out_reduce.send_far()
    out_reduce.send_near()
    gna_reduce.middle()

    swap.arrive()
    out_terms = s.out_terms
    for k in range(2):
        out_terms[2 * y + k] = halves[y, k]
        out_terms[2 * (1 - y) + k] = s.out_swap[k]
    out_fold = Fold(out_terms, s.out_in, s.sem_out_fold)
    out_fold.start()
    def qkv_term(k, carry):
        cols = pl.ds(pl.multiple_of(k * 8 * up_rows, 8 * up_rows), 8 * up_rows)
        term = dot(
            normed[:, :, cols].reshape(all_rows, 8 * up_rows),
            s.grad_qkv[...].reshape(all_rows, own_cols),
            0,
            0,
        )
        s.qkv_term[k] = term.astype(BF).reshape(8, up_rows, own_cols)
        return carry

    lax.fori_loop(0, lines, qkv_term, 0)
    cuts = (pl.ds(0, 6), pl.ds(6, 2))
    qkv_fold = [
        Fold(s.qkv_term.at[:, cut], s.qkv_in.at[:, cut], s.sem_qkv_fold.at[k])
        for k, cut in enumerate(cuts)
    ]
    qkv_fold[0].start()

    grad_in, attn_sum = norm_back(x_ref[...].astype(F32), scale_row(own_canvas, False), gna_reduce.finish())
    input_grad[...] = s.grad_middle[...] + grad_in
    gives[1].start()
    put_row(sums_own, 0, attn_sum)
    head_rows = lax.broadcasted_iota(jnp.int32, (8, lanes), 0)
    head_lane = lax.broadcasted_iota(jnp.int32, (8, lanes), 1)
    head_tile = jnp.zeros((8, lanes), F32)
    for k in range(2):
        value = jnp.sum(
            jnp.where(lane == k * (lanes // 2), s.head_terms[...], 0.0), axis=1, keepdims=True
        )
        head_tile = head_tile + jnp.where(
            (head_rows == 0) & (head_lane == head_of(k)), value, 0.0
        )
    sums_own[16:24, :] = head_tile
    s.sums_plane[me] = sums_own[...]
    sums_share = Share(s.sums_plane, s.sem_sums_share)
    sums_share.start()
    out_reduce.middle()
    out_fold.middle()
    sums_share.finish()
    sums = s.sums
    for k in range(4):
        sums[4 * z + k] = s.sums_plane[2 * k] + s.sums_plane[2 * k + 1]
    all_sums = Line(sums, s.sem_sums, 4)
    all_sums.start()
    qkv_fold[1].start()
    qkv_fold[0].middle()
    down_grad[...] = down_fold.finish(s.down_total).reshape(down_rows, width)
    gives[6].start()
    block_out[...] = (s.middle[...] + out_reduce.finish()).astype(BF)
    gives[0].start()
    s.up_sum[...] = up_fold.finish(s.up_total).astype(BF)
    up_return = Spread(s.up_sum, s.up_back, s.sem_up_back)
    up_return.start()
    up_return.finish()
    for m, own, whole in up_places:
        up_grad[:, whole : whole + down_rows] = s.up_back[m, :, own : own + down_rows].astype(F32)
    gives[5].start()
    qkv_fold[1].middle()
    for fold, cut in zip(qkv_fold, cuts):
        s.qkv_sum[cut] = fold.finish(s.qkv_total.at[cut]).astype(BF)
    qkv_return = Spread(s.qkv_sum, s.qkv_back, s.sem_qkv_back)
    qkv_return.start()

    all_sums.finish()
    rounded = [
        jnp.concatenate([sums[:, offset + r, :] for r in range(width // 128)], axis=1).astype(BF)
        for offset in (0, 8)
    ]
    mine_for = dot(rounded[0], mod_full[:, :width], 1, 1) + dot(
        rounded[1], mod_full[:, width:], 1, 1
    )
    cond_line, cond_in = s.cond_line, s.cond_in
    s.cond_all[...] = mine_for
    for k in range(lines):
        cond_line[k] = s.cond_all[8 * (k // 2) : 8 * (k // 2) + 8, :]
    cond_send = [
        Copy(
            cond_line.at[(z + along) % lines],
            cond_in.at[me, z],
            cond_in.at[member(step), (z + lines - along) % lines],
            s.sem_cond_line,
            at,
            device(step, along),
        )
        for at, (step, along) in enumerate(OTHERS)
    ]
    for copy in cond_send:
        copy.start()
    cond_in[me, z] = cond_line[z]
    amod_grad[...] = dot(cond_mine, rounded[0], 0, 0)[:mod_rows]
    gives[7].start()
    fmod_grad[...] = dot(cond_mine, rounded[1], 0, 0)[:mod_rows]
    gives[8].start()
    head_sum = sums[0, 16:17, :]
    for k in range(1, sums.shape[0]):
        head_sum = head_sum + sums[k, 16:17, :]
    scale_grad[...] = head_sum[:, : scale_grad.shape[1]]
    gives[9].start()
    out_grad[...] = out_fold.finish(s.out_total)
    gives[4].start()
    qkv_return.finish()
    for m, own, whole in qkv_places:
        qkv_grad[:, whole : whole + size] = s.qkv_back[m, :, own : own + size].astype(F32)
    gives[3].start()
    for copy in cond_send:
        copy.arrive()
    for k in range(lines):
        for m in range(8):
            at_row = 8 * k + m
            row = cond_in[m, k, pl.ds(4 * (z % 2) + own_canvas, 1), :]
            cond_grad[:, at_row * mod_rows : (at_row + 1) * mod_rows] = row[:, :mod_rows]
    gives[2].start()
    for copy, when in sends:
        if when is None:
            copy.wait_send()
        else:
            pl.when(when)(copy.wait_send)
    for copy in gives:
        copy.wait()


def scratch_plan(lines, x_ref, qkv_ref, up_ref, out_ref, down_ref):
    rows, width = x_ref.shape
    up_rows = up_ref.shape[0]
    own_cols, up_cols = qkv_ref.shape[1] // 8, up_ref.shape[1] // 8
    hidden = up_cols // 2
    half_head = out_ref.shape[0]
    down_rows = down_ref.shape[0]
    lanes = own_cols // 3
    groups = 4 * lines
    plane = (8, rows, width)
    vm = lambda shape, kind=BF: pltpu.VMEM(shape, kind)
    sem = lambda count: pltpu.SemaphoreType.DMA((2, count))
    plan = dict(
        ids=vm((8, 8, rows), jnp.int32),
        conds=vm((groups, 8, 128), F32),
        tokens=vm(plane),
        cots=vm(plane),
        normed=vm(plane),
        ffn=vm(plane),
        branch=vm(plane),
        qkv_cols=vm((8, up_rows, own_cols)),
        up_cols=vm((8, up_rows, up_cols)),
        qkv_line=vm((lines, 8, up_rows, own_cols)),
        up_line=vm((lines, 8, up_rows, up_cols)),
        out_line=vm((lines, half_head, width)),
        down_line=vm((lines, down_rows, width)),
        out_half=vm((2, half_head, width)),
        out_full=vm((2, 2, half_head, width)),
        mod_full=vm((128, 2 * width)),
        mod_terms=vm((8, groups, width // 4), F32),
        mod_in=vm((8, groups, width // 4), F32),
        mod_line=vm((lines, groups, width // 4), F32),
        mod_total=vm((groups, width // 4), F32),
        mods=vm((8, 8, width // 4), F32),
        scales=vm((8, 2 * width), F32),
        turns=vm((4, 2 * rows, 2 * lanes), F32),
        raw=vm((4, 2, 2 * rows, lanes), F32),
        rotated=vm((4, 3, 2 * rows, lanes)),
        probs=vm((4, 2, 2 * rows, 2 * rows), F32),
        raw_attended=vm((4, 2 * rows, lanes), F32),
        attended=vm((4, 2 * rows, lanes)),
        middle=vm((rows, width), F32),
        grad_middle=vm((rows, width), F32),
        hidden=vm((4, 2 * rows, hidden)),
        act=vm((4, 2 * rows, hidden), F32),
        slope=vm((4, 2 * rows, hidden), F32),
        grad_up=vm((4, 2 * rows, up_cols)),
        grad_qkv=vm((4, 2 * rows, own_cols)),
        head_terms=vm((1, lanes), F32),
        sums_own=vm((24, 128), F32),
        sums_plane=vm((8, 24, 128), F32),
        sums=vm((groups, 24, 128), F32),
        cond_all=vm((groups, 128), F32),
        cond_line=vm((lines, 8, 128), F32),
        cond_in=vm((8, lines, 8, 128), F32),
        down_total=vm((down_rows, width), F32),
        up_total=vm((8, up_rows, up_cols), F32),
        qkv_total=vm((8, up_rows, own_cols), F32),
        out_total=vm((half_head, width), F32),
        down_term=vm((lines, down_rows, width)),
        down_in=vm((4, down_rows, width)),
        up_term=vm((lines, 8, up_rows, up_cols)),
        up_in=vm((4, 8, up_rows, up_cols)),
        up_sum=vm((8, up_rows, up_cols)),
        up_back=vm((8, up_rows, up_cols)),
        qkv_term=vm((lines, 8, up_rows, own_cols)),
        qkv_in=vm((4, 8, up_rows, own_cols)),
        qkv_sum=vm((8, up_rows, own_cols)),
        qkv_back=vm((8, up_rows, own_cols)),
        out_halves=vm((2, 2, half_head, width)),
        out_swap=vm((2, half_head, width)),
        out_terms=vm((lines, half_head, width)),
        out_in=vm((4, half_head, width)),
    )
    for name in ("mid", "gnf", "out", "gna"):
        plan[name + "_part"] = vm(plane)
        plan[name + "_pair"] = vm((4, rows, width))
        plan[name + "_far"] = vm((2, rows // 2, width))
        plan[name + "_chip"] = vm((2, rows, width))
        plan["sem_" + name] = sem(10)
    plan.update(
        sem_tokens=sem(10),
        sem_cots=sem(10),
        sem_ffn=sem(10),
        sem_branch=sem(10),
        sem_ids=sem(7),
        sem_qkv_spread=sem(7),
        sem_up_spread=sem(7),
        sem_mod_spread=sem(7),
        sem_mods=sem(7),
        sem_up_back=sem(7),
        sem_qkv_back=sem(7),
        sem_qkv_line=pltpu.SemaphoreType.DMA((2, 2, 5)),
        sem_up_line=pltpu.SemaphoreType.DMA((2, 2, 5)),
        sem_out_line=sem(5),
        sem_down_line=sem(5),
        sem_mod_line=sem(lines - 1),
        sem_cond_line=sem(31),
        sem_down_fold=sem(5),
        sem_up_fold=sem(5),
        sem_qkv_fold=pltpu.SemaphoreType.DMA((2, 2, 5)),
        sem_out_fold=sem(5),
        sem_cond=sem(15),
        sem_sums=sem(lines - 1),
        sem_sums_share=sem(7),
        sem_half=sem(2),
    )
    return plan


def turn_tables(heads, lines):
    head_size = 64
    table = np.zeros((heads, 2, 16, 2, head_size), np.float64)
    for axis in range(2):
        for j in range(8):
            freq = math.pi * 10.0 ** ((j * heads + np.arange(heads)) / (8.0 * heads))
            unit = (2.0 * np.arange(16) + 1.0) / 16.0 - 1.0
            angle = freq[:, None].astype(np.float32) * unit[None, :].astype(np.float32)
            angle = angle.astype(np.float64)
            for half in range(2):
                at = axis * 16 + half * 8 + j
                table[:, axis, :, 0, at] = np.cos(angle)
                table[:, axis, :, 1, at] = np.sin(angle) * (1.0 if half else -1.0)
    table[:, 0, :, 0, 32:] = 1.0
    high = table.astype(ml_dtypes.bfloat16)
    low = (table - high.astype(np.float64)).astype(ml_dtypes.bfloat16)
    parts = []
    for term in (high, low):
        term = term.reshape(2, 2, 2, 2, 2, 16, 2, head_size)
        term = term.transpose(2, 3, 0, 4, 5, 6, 1, 7)
        parts.append(term.reshape(8, 32, 4 * head_size))
    return np.concatenate(parts, axis=1)


def plane_shards(
    block_in,
    conditioning,
    crop_ids,
    positions,
    qkv_weight,
    out_weight,
    up_weight,
    down_weight,
    attn_modulate,
    ffn_modulate,
    head_scale,
    cotangent,
):
    lines = lax.axis_size("dp") // 4
    rows, width = block_in.shape[1:]
    heads = head_scale.shape[0]
    tables = jnp.asarray(turn_tables(heads, lines))
    kinds = jax.ShapeDtypeStruct
    operands = (
        block_in[0],
        cotangent[0],
        qkv_weight,
        up_weight,
        out_weight,
        down_weight,
        attn_modulate,
        ffn_modulate,
        conditioning,
        crop_ids,
        positions,
        head_scale,
        tables,
    )
    plan = scratch_plan(lines, operands[0], qkv_weight, up_weight, out_weight, down_weight)
    in_vmem = pl.BlockSpec(memory_space=pltpu.VMEM)
    in_specs = [in_vmem] * len(operands)
    in_specs[11] = pl.BlockSpec(memory_space=pltpu.SMEM)
    shapes = (
    kinds((rows, width), BF),
    kinds((rows, width), F32),
    kinds(conditioning.shape, F32),
    kinds(qkv_weight.shape, F32),
    kinds(out_weight.shape, F32),
    kinds(up_weight.shape, F32),
    kinds(down_weight.shape, F32),
    kinds(attn_modulate.shape, F32),
    kinds(ffn_modulate.shape, F32),
    kinds((1, heads), F32),
)
    results = pl.pallas_call(
        functools.partial(block_kernel, lines),
        out_shape=shapes,
        in_specs=in_specs,
        out_specs=[pl.BlockSpec(memory_space=pl.ANY)] * 10,
        scratch_shapes=[pltpu.VMEM(kind.shape, kind.dtype) for kind in shapes]
        + list(plan.values())
        + [pltpu.SemaphoreType.DMA((10,))],
        compiler_params=pltpu.CompilerParams(
            collective_id=0, has_side_effects=True, vmem_limit_bytes=63 * 2**20
        ),
    )(*operands)
    results = settle(results)
    return tuple(item[None] for item in results[:2]) + tuple(results[2:-1]) + (results[-1][0],)


def settle(results):
    count = len(results)

    def kernel(*refs):
        held, sems = refs[2 * count : -1], refs[-1]
        loads = [
            pltpu.make_async_copy(refs[k], held[k], sems.at[0, k]) for k in range(count)
        ]
        stores = [
            pltpu.make_async_copy(held[k], refs[count + k], sems.at[1, k]) for k in range(count)
        ]
        for copy in loads:
            copy.start()
        for load, store in zip(loads, stores):
            load.wait()
            store.start()
        for copy in stores:
            copy.wait()

    anywhere = pl.BlockSpec(memory_space=pl.ANY)
    return pl.pallas_call(
        kernel,
        out_shape=tuple(jax.ShapeDtypeStruct(item.shape, item.dtype) for item in results),
        in_specs=[anywhere] * count,
        out_specs=[anywhere] * count,
        scratch_shapes=[pltpu.VMEM(item.shape, item.dtype) for item in results]
        + [pltpu.SemaphoreType.DMA((2, count))],
    )(*results)


def in_planes(mesh):
    return mesh.shape["seq"] == 2 and mesh.shape["dp"] == 16


def solution(mesh):
    in_specs = (
        P("dp", "seq", None),
        P("dp", None),
        P("dp", "seq"),
        P("dp", None, "seq"),
        P(("dp", "seq"), None),
        P(("dp", "seq"), None),
        P(("dp", "seq"), None),
        P(("dp", "seq"), None),
        P(("dp", "seq"), None),
        P(("dp", "seq"), None),
        P(),
        P("dp", "seq", None),
    )
    out_specs = (
        P("dp", "seq", None),
        P("dp", "seq", None),
        P("dp", None),
        P(("dp", "seq"), None),
        P(("dp", "seq"), None),
        P(("dp", "seq"), None),
        P(("dp", "seq"), None),
        P(("dp", "seq"), None),
        P(("dp", "seq"), None),
        P(),
    )
    body = plane_shards if in_planes(mesh) else shards
    return jax.shard_map(body, mesh=mesh, in_specs=in_specs, out_specs=out_specs, check_vma=False)
```
